256 devices in a mesh: dp: 4 (over z_lo), mrow: 16 (over z_hi, y, core), mcol: 4 (over x).
Axes of the slice: x: 4, y: 4, z: 8 (z_hi: 2, z_lo: 4; z = z_hi * 4 + z_lo), core: 2. Of those that a mesh axis runs over, the one named last changes fastest.
Arguments:
- patches: bfloat16 [32, 256, 6144], P('dp', None, ('mcol', 'mrow')), may hold values from -6 to 6
- keep_index: int32 [32, 128], P('dp'), may hold values from 0 to 255, as said below
- counts: int32 [4], replicated, may hold values from 1 to 8, 16 in all
- gain: float32 [6144], P(('mcol', 'mrow')), may hold values from 0.5 to 1.5
- w_qkv: bfloat16 [6144, 3, 4096], P('mcol', None, 'mrow'), may hold values from -0.05103104 to 0.05103104
- w_out: bfloat16 [4096, 6144], P('mrow', 'mcol'), may hold values from -0.375 to 0.375
- cotangent: bfloat16 [4096, 6144], P('dp', ('mcol', 'mrow')), may hold values from -6 to 6
Outputs:
- outputs: bfloat16 [4096, 6144], P('dp', ('mcol', 'mrow'))
- d_patches: bfloat16 [32, 256, 6144], P('dp', None, ('mcol', 'mrow'))
- grad_qkv: float32 [6144, 3, 4096], P(('mcol', 'dp'), None, 'mrow')
- grad_out: float32 [4096, 6144], P('mrow', ('mcol', 'dp'))
- grad_gain: float32 [6144], P(('mcol', 'mrow', 'dp'))
The draws below stay inside these ranges and needn't reach their ends.
Inputs may be any that keep to these rules, and one draw needn't show every extreme that they name: `keep_index`: each row holds 128 distinct patch numbers in increasing order. The counts sum to 16; the largest is exactly 8.
All inputs are finite; a program needn't handle non-finite values.
Results may differ from the reference program's by a relative error of at most 0.02.
Values may be sent and summed in bfloat16 or wider, within the bound.
A program may use at most 128 MiB of HBM per device.

```python
import math
from functools import partial
import jax
import jax.numpy as jnp
import numpy as np
from jax import lax

D = 6144
HEADS = 32
HD = 128
P_SIZE = 256
KEEP = 128
CAP = 8
IMAGES = 32
LIVE = 16
TOKENS = 4096
N_DP = 4


def draw_keep_index(key, part):
    key = jax.random.fold_in(key, 7)
    row_keys = jax.random.split(key, IMAGES)
    chosen = jax.vmap(lambda row_key: jnp.sort(jax.random.permutation(row_key, P_SIZE)[:KEEP]))(row_keys)
    return chosen.astype(jnp.int32)


def draw_w_qkv(key, part):
    key = jax.random.fold_in(key, 11)
    noise_key = jax.random.fold_in(key, 1)
    offset_key = jax.random.fold_in(key, 2)
    scale = D ** (-0.5)
    noise = jax.random.normal(noise_key, (D, 3, HEADS * HD), jnp.float32)
    offset = jax.random.uniform(offset_key, (1, 3, HEADS * HD), jnp.float32, -1.35, 1.35)
    return (jnp.clip(noise + offset, -3.98, 3.98) * scale).astype(jnp.bfloat16)


def level_of(stream_key, extent, cuts, smallest, top_value):
    level = 1.0
    for position, shards_of in cuts:
        steps = jax.random.uniform(jax.random.fold_in(jax.random.fold_in(stream_key, 6), position), (shards_of,), jnp.float32, smallest / len(cuts), top_value / len(cuts))
        level = level * jnp.repeat(jnp.exp(steps), extent[position] // shards_of).reshape((-1,) + (1,) * (len(extent) - 1 - position))
    return level


def profile(amount, total, most, slope):
    portions = [(1 << 20) // math.isqrt(rank ** slope) + 1 for rank in range(2, amount + 1)]
    rest, given = total - most - (amount - 1), [1] * (amount - 1)
    while rest > 0:
        movable = [i for i in range(amount - 1) if given[i] < most]
        whole, left = sum([portions[i] for i in movable]), rest
        for i in movable:
            more = min(most - given[i], max(1, left * portions[i] // whole), rest)
            given[i] = given[i] + more
            rest = rest - more
    return np.array([most] + given)


def uneven_parts(own_key, count, total, limit, lean):
    if count == 2:
        one = jax.random.randint(own_key, (), max(1, total - limit), min(limit, total - 1) + 1)
        return jnp.stack([one, total - one])
    sizes = jnp.asarray(profile(count, total, limit, lean), jnp.int32)
    couples = (count - 1) // 2
    source_of, sink = sizes[1:1 + 2 * couples:2], sizes[2:2 + 2 * couples:2]
    margin = jnp.minimum(source_of - 1, limit - sink)
    moved = jax.random.randint(jax.random.fold_in(own_key, 1), (couples,), 0, 1 << 20) % (margin + 1)
    sizes = sizes.at[1:1 + 2 * couples:2].set(source_of - moved).at[2:2 + 2 * couples:2].set(sink + moved)
    return sizes[jax.random.permutation(jax.random.fold_in(own_key, 2), count)]


def scatter_about(rng, shape, width, limit, shards=(), kind=jnp.bfloat16):
    level = level_of(rng, shape, shards, -0.22, 0.18) if shards else 1.0
    result = jax.random.normal(rng, shape, jnp.float32) * width * level
    return jnp.minimum(jnp.maximum(result, -limit), limit).astype(kind)


def setup_inputs(seed: int = 0) -> dict:
    key_list = jax.random.split(jax.random.key(seed), 8)
    patches = scatter_about(key_list[0], (IMAGES, P_SIZE, D), 1.0, 6.0, ((0, 4), (2, 64)))
    keep_index = draw_keep_index(jax.random.fold_in(key_list[7], 71), 0)
    counts = uneven_parts(key_list[2], N_DP, LIVE, CAP, 2).astype(jnp.int32)
    gain = jnp.clip(1.0 + 0.1 * jax.random.normal(key_list[3], (D,), jnp.float32), 0.5, 1.5)
    w_qkv = draw_w_qkv(jax.random.fold_in(key_list[7], 71), 0)
    w_out = scatter_about(key_list[5], (HEADS * HD, D), (HEADS * HD // 16) ** -0.5, 0.375, ((0, 16), (1, 4)))
    cotangent = scatter_about(key_list[6], (TOKENS, D), 1.0, 6.0, ((0, 4), (1, 64)))
    return dict(patches=patches, keep_index=keep_index, counts=counts, gain=gain, w_qkv=w_qkv, w_out=w_out, cotangent=cotangent)


EPSILON = 1e-06

def normalize(values):
    centred = values - lax.optimization_barrier(jnp.mean(values, axis=-1, keepdims=True))
    return centred * lax.rsqrt(lax.optimization_barrier(jnp.mean(centred * centred, axis=-1, keepdims=True)) + EPSILON)

def attend(qkv_rows, length):
    total_rows = qkv_rows.shape[0]
    head_count = qkv_rows.shape[2]
    head_size = qkv_rows.shape[3]
    blocks = qkv_rows.reshape(total_rows // length, length, 3, head_count, head_size)
    query_rows = normalize(blocks[:, :, 0])
    key_rows = normalize(blocks[:, :, 1])
    value_rows = blocks[:, :, 2]
    scores = jnp.einsum('bqhd,bkhd->bhqk', query_rows, key_rows, precision=lax.Precision.HIGHEST) * head_size ** (-0.5)
    weights = jnp.exp(scores)
    weights = weights / lax.optimization_barrier(jnp.sum(weights, axis=-1, keepdims=True))
    head_mixed = jnp.einsum('bhqk,bkhd->bqhd', weights, value_rows, precision=lax.Precision.HIGHEST)
    return head_mixed.reshape(total_rows, head_count * head_size)

def reference(patches, keep_index, counts, gain, w_qkv, w_out, cotangent):
    image_ids = jnp.arange(IMAGES, dtype=jnp.int32)
    kept_rows = jnp.take_along_axis(patches, keep_index[:, :, None].astype(jnp.int32), axis=1).reshape(TOKENS, D)
    live_image = (image_ids % CAP < counts[image_ids // CAP]).astype(jnp.float32)
    live_rows = jnp.repeat(live_image, KEEP)[:, None]
    inputs_f = kept_rows.astype(jnp.float32)
    mean_row = lax.optimization_barrier(jnp.sum(inputs_f, axis=1, keepdims=True)) / D
    square_row = lax.optimization_barrier(jnp.sum(inputs_f * inputs_f, axis=1, keepdims=True)) / D
    inv_scale = lax.rsqrt(square_row - mean_row * mean_row + EPSILON)
    centred_rows = (inputs_f - mean_row) * inv_scale
    normed = (centred_rows * gain).astype(jnp.bfloat16)
    stacked = w_qkv.reshape(D, 3 * HEADS * HD)
    qkv_rows = jnp.dot(normed, stacked, preferred_element_type=jnp.float32).reshape(TOKENS, 3, HEADS, HD)
    head_mixed, pullback = jax.vjp(partial(attend, length=KEEP), qkv_rows)
    heads_out = head_mixed.astype(jnp.bfloat16)
    attn_out = jnp.dot(heads_out, w_out, preferred_element_type=jnp.float32)
    outputs = ((inputs_f + attn_out) * live_rows).astype(jnp.bfloat16)
    upstream = (cotangent.astype(jnp.float32) * live_rows).astype(jnp.bfloat16)
    d_mixed = jnp.dot(upstream, w_out.T, preferred_element_type=jnp.float32)
    d_qkv = pullback(d_mixed)[0].astype(jnp.bfloat16).reshape(TOKENS, 3 * HEADS * HD)
    grad_out = jnp.dot(heads_out.T, upstream, preferred_element_type=jnp.float32)
    grad_qkv = jnp.dot(normed.T, d_qkv, preferred_element_type=jnp.float32).reshape(D, 3, HEADS * HD)
    d_normed = jnp.dot(d_qkv, stacked.T, preferred_element_type=jnp.float32)
    grad_gain = lax.optimization_barrier(jnp.sum(d_normed * centred_rows, axis=0))
    d_hat = d_normed * gain
    mean_hat = lax.optimization_barrier(jnp.sum(d_hat, axis=1, keepdims=True)) / D
    mean_cross = lax.optimization_barrier(jnp.sum(d_hat * centred_rows, axis=1, keepdims=True)) / D
    d_inputs = upstream.astype(jnp.float32) + inv_scale * (d_hat - mean_hat - centred_rows * mean_cross)
    d_patches = jnp.zeros((IMAGES, P_SIZE, D), jnp.bfloat16).at[image_ids[:, None], keep_index.astype(jnp.int32)].set(d_inputs.astype(jnp.bfloat16).reshape(IMAGES, KEEP, D))
    return (outputs, d_patches, grad_qkv, grad_out, grad_gain)
```

```python
from functools import partial

import jax
import jax.numpy as jnp
from jax import lax
from jax.experimental import pallas as pl
from jax.experimental.pallas import tpu as pltpu
from jax.sharding import PartitionSpec as P

D = 6144
HD = 128
KEEP = 128
EPSILON = 1e-06

F32 = jnp.float32
BF16 = jnp.bfloat16
MESH = pl.DeviceIdType.MESH
VM = pl.BlockSpec(memory_space=pltpu.VMEM)
SM = pl.BlockSpec(memory_space=pltpu.SMEM)
DMA = pltpu.SemaphoreType.DMA


def dot(a, b, ca, cb):
    return lax.dot_general(a, b, (((ca,), (cb,)), ((), ())), preferred_element_type=F32)


def remote(src, dst, send, recv, where):
    return pltpu.make_async_remote_copy(
        src_ref=src, dst_ref=dst, send_sem=send, recv_sem=recv, device_id=where, device_id_type=MESH
    )


def greet(peers):
    barrier = pltpu.get_barrier_semaphore()
    for peer in peers:
        pl.semaphore_signal(barrier, inc=1, device_id=peer, device_id_type=MESH)
    pl.semaphore_wait(barrier, len(peers))


class Place:
    def __init__(self):
        self.me = lax.axis_index("mrow")
        self.core = lax.rem(self.me, 2)
        self.y = lax.rem(self.me // 2, 4)
        self.zh = self.me // 8
        self.x = lax.axis_index("mcol")
        self.sib = self.at(self.zh, 0, 1 - self.core)
        self.anti = self.at(1 - self.zh, 0, self.core)
        self.ys = [self.at(self.zh, d, self.core) for d in range(4)]
        self.xs = [lax.rem(self.x + d, 4) for d in range(4)]

    def at(self, zh, dy, core):
        return zh * 8 + lax.rem(self.y + dy, 4) * 2 + core

    def peers(self):
        rows = [self.sib, self.anti] + self.ys[1:]
        return [{"mrow": r} for r in rows] + [{"mcol": c} for c in self.xs[1:]]


class SmallSum:
    def __init__(self, place, val, box, send, recv, x_rows):
        self.place, self.val, self.box = place, val, box
        self.send, self.recv, self.x_rows = send, recv, x_rows
        self.live = []
        self.n = 0

    def push(self, peers, rows=None):
        self.live = []
        for where in peers:
            k = self.n
            self.n += 1
            stage = self.val.at[self.stage]
            box = self.box.at[k]
            if rows is not None:
                stage, box = stage.at[:rows], box.at[:rows]
            c = remote(stage, box, self.send.at[k], self.recv.at[k], where)
            c.start()
            self.live.append((k, c))

    def start(self, value):
        self.stage = 0
        self.val[0] = value
        self.push([{"mrow": self.place.sib}])

    def step(self):
        total = self.val[self.stage]
        rows = self.x_rows if self.stage == 3 else total.shape[0]
        total = total[:rows]
        for k, c in self.live:
            c.wait()
            total = total + self.box[k, :rows]
        self.stage += 1
        if self.stage < 4:
            self.val[self.stage] = total
        if self.stage == 1:
            self.push([{"mrow": r} for r in self.place.ys[1:]])
        elif self.stage == 2:
            self.push([{"mrow": self.place.anti}])
        elif self.stage == 3:
            self.push([{"mcol": c} for c in self.place.xs[1:]], self.x_rows)
        return total


def prep_kernel(n, p_ref, k_ref, c_ref, live_ref, x_ref, u_ref, s_ref):
    patch = lax.broadcasted_iota(jnp.int32, (p_ref.shape[1], KEEP), 0)
    eye = (
        lax.broadcasted_iota(jnp.int32, (KEEP, KEEP), 0)
        == lax.broadcasted_iota(jnp.int32, (KEEP, KEEP), 1)
    ).astype(F32).astype(BF16)
    for i in range(n):
        lanes = slice(i * KEEP, (i + 1) * KEEP)
        pick = (patch == k_ref[i : i + 1, :]).astype(F32).astype(BF16)
        rows = dot(p_ref[i], pick, 0, 0)
        x_ref[:, lanes] = rows.astype(BF16)
        s_ref[i : i + 1, :] = jnp.sum(rows, axis=0, keepdims=True)
        s_ref[n + i : n + i + 1, :] = jnp.sum(rows * rows, axis=0, keepdims=True)
        u_ref[:, lanes] = (dot(c_ref[lanes, :], eye, 0, 0) * live_ref[i]).astype(BF16)


def gather_kernel(
    x_ref, u_ref, s_ref, xg, ug, st, box, val, ss, sr, zsend, ysend, fsend, csend, xr, ur
):
    place = Place()
    greet(place.peers())
    me, sib = place.me, {"mrow": place.sib}
    right, left = {"mrow": place.ys[1]}, {"mrow": place.ys[3]}
    arrays = ((x_ref, xg, xr), (u_ref, ug, ur))
    small = SmallSum(place, val, box, ss, sr, st.shape[0] - 16)
    sends = []
    ncore = [0]

    def push(a, src, slot, sem, where):
        _, out, recv = arrays[a]
        c = remote(src, out.at[slot], sem, recv.at[slot], where)
        c.start()
        sends.append(c)

    def got(a, slot):
        src, out, recv = arrays[a]
        remote(src, out.at[slot], zsend.at[0], recv.at[slot], sib).wait_recv()

    def to_sib(slot):
        for a in range(2):
            push(a, arrays[a][1].at[slot], slot, csend.at[a, ncore[0]], sib)
        ncore[0] += 1

    small.start(s_ref[...])
    for a in range(2):
        push(a, arrays[a][0], me, zsend.at[a], {"mrow": place.anti})
    for a in range(2):
        push(a, arrays[a][0], me, ysend.at[a, 0], right)
        push(a, arrays[a][0], me, ysend.at[a, 1], left)
    for a in range(2):
        push(a, arrays[a][0], me, csend.at[a, 0], sib)
    ncore[0] = 1
    xg[me] = x_ref[...]
    ug[me] = u_ref[...]
    small.step()
    anti = place.anti
    for a in range(2):
        got(a, anti)
        push(a, arrays[a][1].at[anti], anti, ysend.at[a, 2], right)
        push(a, arrays[a][1].at[anti], anti, ysend.at[a, 3], left)
    to_sib(anti)
    small.step()
    for half, zh in enumerate((place.zh, 1 - place.zh)):
        before, after = place.at(zh, 3, place.core), place.at(zh, 1, place.core)
        got(0, before)
        push(0, xg.at[before], before, fsend.at[0, half], right)
        got(1, after)
        push(1, ug.at[after], after, fsend.at[1, half], left)
        got(1, before)
        to_sib(before)
        got(0, after)
        to_sib(after)
        if half == 0:
            small.step()
    for zh in (place.zh, 1 - place.zh):
        far = place.at(zh, 2, place.core)
        got(0, far)
        got(1, far)
        to_sib(far)
    st[...] = jnp.concatenate([small.step(), val[3, st.shape[0] - 16 :]], axis=0)
    for zh in range(2):
        for dy in range(4):
            for a in range(2):
                got(a, place.at(zh, dy, 1 - place.core))
    for c in sends:
        c.wait_send()


def attend(q, k, v, do):
    def norm(t):
        c = t - jnp.mean(t, axis=0, keepdims=True)
        i = lax.rsqrt(jnp.mean(c * c, axis=0, keepdims=True) + EPSILON)
        return c * i, i

    def norm_back(d, y, i):
        return i * (
            d - jnp.mean(d, axis=0, keepdims=True) - y * jnp.mean(d * y, axis=0, keepdims=True)
        )

    def mm(a, b, ca, cb):
        return lax.dot_general(
            a, b, (((ca,), (cb,)), ((), ())), preferred_element_type=F32, precision=lax.Precision.HIGHEST
        )

    scale = HD ** (-0.5)
    qn, iq = norm(q)
    kn, ik = norm(k)
    w = jnp.exp(mm(kn, qn, 0, 0) * scale)
    w = w / jnp.sum(w, axis=0, keepdims=True)
    out = mm(v, w, 1, 0)
    dw = mm(v, do, 0, 0)
    ds = w * (dw - jnp.sum(w * dw, axis=0, keepdims=True)) * scale
    dv = mm(do, w, 1, 1)
    dq = norm_back(mm(kn, ds, 1, 0), qn, iq)
    dk = norm_back(mm(qn, ds, 1, 1), kn, ik)
    return out, dq, dk, dv


def middle_kernel(
    q_ref, m_ref, dall, hall, work, own, bq, bm, sq, sm, rq, rm, gs, gr
):
    x = lax.axis_index("mcol")
    xs = [lax.rem(x + d, 4) for d in range(4)]
    greet([{"mcol": c} for c in (xs[1], xs[3])])
    right, left = {"mcol": xs[1]}, {"mcol": xs[3]}
    width = own.shape[1]
    qrows = q_ref.shape[0]
    half = own.shape[0] // 2
    mrows = m_ref.shape[0]
    qminus = qrows - half

    def lanes(block):
        return pl.ds(pl.multiple_of(block * width, width), width)

    sends = []
    def push_plus(src, slot, where):
        c = remote(src, bq.at[slot], sq.at[slot], rq.at[slot], where)
        c.start()
        sends.append(c)

    def push_minus(srcq, srcm, slot, where):
        c = remote(srcq, bq.at[slot, :qminus], sq.at[slot], rq.at[slot], where)
        d = remote(srcm, bm.at[slot], sm.at[slot], rm.at[slot], where)
        c.start()
        d.start()
        sends.extend((c, d))

    def got_plus(slot):
        remote(bq.at[slot], bq.at[slot], sq.at[slot], rq.at[slot], right).wait_recv()

    def got_minus(slot):
        remote(bq.at[slot, :qminus], bq.at[slot, :qminus], sq.at[slot], rq.at[slot], right).wait_recv()
        remote(bm.at[slot], bm.at[slot], sm.at[slot], rm.at[slot], right).wait_recv()

    plus, minus = pl.ds(0, half), pl.ds(half, qminus)
    push_plus(q_ref.at[plus, lanes(xs[2])], 0, right)
    push_minus(q_ref.at[minus, lanes(xs[2])], m_ref.at[:, lanes(xs[2])], 1, left)
    push_plus(q_ref.at[plus, lanes(xs[3])], 2, left)
    push_minus(q_ref.at[minus, lanes(xs[1])], m_ref.at[:, lanes(xs[1])], 3, right)
    got_plus(0)
    work[:half] = (bq[0].astype(F32) + q_ref[plus, lanes(xs[1])].astype(F32)).astype(BF16)
    push_plus(work.at[:half], 4, right)
    got_minus(1)
    work[half:qrows] = (
        bq[1, :qminus].astype(F32) + q_ref[minus, lanes(xs[3])].astype(F32)
    ).astype(BF16)
    work[qrows:] = (bm[1].astype(F32) + m_ref[:, lanes(xs[3])].astype(F32)).astype(BF16)
    push_minus(work.at[half:qrows], work.at[qrows:], 5, left)
    got_plus(2)
    got_minus(3)
    got_plus(4)
    got_minus(5)
    heads = mrows // HD

    def total(r0, c0):
        cols = pl.ds(pl.multiple_of(x * width + c0, HD), HD)
        here = slice(c0, c0 + HD)
        if r0 < half:
            parts = q_ref[r0 : r0 + HD, cols], bq[2, r0 : r0 + HD, here], bq[4, r0 : r0 + HD, here]
        elif r0 < qrows:
            b = slice(r0 - half, r0 - half + HD)
            parts = q_ref[r0 : r0 + HD, cols], bq[3, b, here], bq[5, b, here]
        else:
            b = slice(r0 - qrows, r0 - qrows + HD)
            parts = m_ref[b, cols], bm[3, b, here], bm[5, b, here]
        return parts[0].astype(F32) + parts[1].astype(F32) + parts[2].astype(F32)

    for c0 in range(0, width, HD):
        here = slice(c0, c0 + HD)
        for h in range(heads):
            q, k, v, do = (total((part * heads + h) * HD, c0) for part in range(4))
            out, dq, dk, dv = attend(q, k, v, do)
            for part, value in enumerate((dq, dk, dv, out)):
                r0 = (part * heads + h) * HD
                own[r0 : r0 + HD, here] = value.astype(BF16)

    dst = ((dall, pl.ds(0, half), pl.ds(0, half)),
           (dall, pl.ds(half, qminus), pl.ds(half, qminus)),
           (hall, pl.ds(qrows, mrows), pl.ds(0, mrows)))

    def push_part(p, block, src, k, where):
        out, _, rows = dst[p]
        c = remote(src, out.at[rows, lanes(block)], gs.at[p, k], gr.at[p, block], where)
        c.start()
        sends.append(c)

    def got_part(p, block):
        out, rows_own, rows = dst[p]
        remote(own.at[rows_own], out.at[rows, lanes(block)], gs.at[p, 0], gr.at[p, block], right).wait_recv()

    for p in range(3):
        for k, where in enumerate((right, left)):
            push_part(p, x, own.at[dst[p][1]], k, where)
    dall[:, lanes(x)] = own[:qrows]
    hall[:, lanes(x)] = own[qrows:]
    got_part(0, xs[3])
    push_part(0, xs[3], dall.at[dst[0][2], lanes(xs[3])], 2, right)
    for p in (1, 2):
        got_part(p, xs[1])
        out = dst[p][0]
        push_part(p, xs[1], out.at[dst[p][2], lanes(xs[1])], 2, left)
    got_part(1, xs[3])
    got_part(2, xs[3])
    got_part(0, xs[1])
    for p in range(3):
        got_part(p, xs[2])
    for c in sends:
        c.wait_send()


def reduce_kernel(
    a_ref, n_ref, s_ref, g_ref, o_ref, ra, rn, st, rg, ro,
    box, val, cbox, ybuf, ysum, ztot, zbox, gr_buf, gl_buf, or_buf, ol_buf,
    ss, sr, csend, crecv, ysend, yrecv, zsend, zrecv, dsend, drecv,
):
    place = Place()
    dp = lax.axis_index("dp")
    ndp = lax.axis_size("dp")
    near = [{"dp": lax.rem(dp + 1, ndp)}, {"dp": lax.rem(dp + ndp - 1, ndp)}]
    greet(place.peers() + near)
    right, left = {"mrow": place.ys[1]}, {"mrow": place.ys[3]}
    sib, anti = {"mrow": place.sib}, {"mrow": place.anti}
    core, zh = place.core, place.zh
    ydev = [lax.rem(place.y + d, 4) for d in range(4)]
    arrays = (a_ref, n_ref)
    outs = (ra, rn)
    rows = ra.shape[0]
    sends = []

    small = SmallSum(place, val, box, ss, sr, st.shape[0])
    small.start(s_ref[...])

    gcols = ro.shape[1]
    bufs = ((gr_buf, or_buf), (gl_buf, ol_buf))

    def own_block(t):
        return g_ref.at[t], o_ref.at[:, pl.ds(pl.multiple_of(t * gcols, gcols), gcols)]

    def line_copies(direction, t, own):
        slot = t - 1 if direction == 0 else t
        srcs = own_block(t) if own else tuple(b.at[slot] for b in bufs[direction])
        return [
            remote(
                srcs[i], bufs[direction][i].at[slot],
                dsend.at[direction, slot, i], drecv.at[direction, slot, i], near[direction],
            )
            for i in range(2)
        ]

    def forward(direction, t):
        slot = t - 1 if direction == 0 else t
        for c in line_copies(direction, t, False):
            c.wait_recv()
        gb, ob = bufs[direction][0].at[slot], bufs[direction][1].at[slot]
        add_rows(gb, g_ref.at[t])
        add_rows(ob, o_ref.at[:, pl.ds(pl.multiple_of(t * gcols, gcols), gcols)])
        for c in line_copies(direction, t, False):
            c.start()

    def add_rows(dst, src):
        @pl.loop(0, dst.shape[0] // 16)
        def _(i):
            r = pl.ds(pl.multiple_of(i * 16, 16), 16)
            dst[r] = (dst[r].astype(F32) + src[r].astype(F32)).astype(BF16)

    @pl.when(dp == 0)
    def _():
        for t in (3, 2, 1):
            for c in line_copies(0, t, True):
                c.start()

    @pl.when(dp == 3)
    def _():
        for t in (0, 1, 2):
            for c in line_copies(1, t, True):
                c.start()

    order = (2, 1, 3, 0)
    cores = []
    for d in order:
        for a in range(2):
            c = remote(
                arrays[a].at[:, ydev[d], 1 - core], cbox.at[a, d], csend.at[a, d], crecv.at[a, d], sib
            )
            c.start()
            cores.append(c)

    def core_sum(a, d, extra=None):
        remote(
            arrays[a].at[:, ydev[d], 1 - core], cbox.at[a, d], csend.at[a, d], crecv.at[a, d], sib
        ).wait_recv()
        add_in(cbox.at[a, d], [arrays[a].at[:, ydev[d], core]] + ([extra] if extra is not None else []))

    def add_in(dst, srcs):
        for z in range(2):
            @pl.loop(0, rows // 16)
            def _(i):
                r = pl.ds(pl.multiple_of(i * 16, 16), 16)
                total = dst[z, r].astype(F32)
                for s in srcs:
                    total = total + s[z, r].astype(F32)
                dst[z, r] = total.astype(BF16)

    def ypush(a, src, slot, where):
        c = remote(src, ybuf.at[a, slot], ysend.at[a, slot], yrecv.at[a, slot], where)
        c.start()
        sends.append(c)

    def ygot(a, slot):
        remote(ybuf.at[a, slot], ybuf.at[a, slot], ysend.at[a, slot], yrecv.at[a, slot], right).wait_recv()

    ahead, behind = (right, left), (left, right)
    nxt, prv = (1, 3), (3, 1)
    for a in range(2):
        core_sum(a, 2)
        ypush(a, cbox.at[a, 2], 0, ahead[a])
    small.step()
    for a in range(2):
        core_sum(a, prv[a])
        ypush(a, cbox.at[a, prv[a]], 1, behind[a])
    for a in range(2):
        core_sum(a, nxt[a])
    small.step()
    for a in range(2):
        ygot(a, 0)
        add_in(cbox.at[a, nxt[a]], [ybuf.at[a, 0]])
        ypush(a, cbox.at[a, nxt[a]], 2, ahead[a])
    for a in range(2):
        core_sum(a, 0)
    small.step()

    @pl.when(dp == 1)
    def _():
        forward(0, 3)

    @pl.when(dp == 2)
    def _():
        forward(1, 0)

    zcopies = []
    for a in range(2):
        ygot(a, 1)
        ygot(a, 2)

        @pl.loop(0, rows // 16)
        def _(i):
            r = pl.ds(pl.multiple_of(i * 16, 16), 16)
            for z in range(2):
                ysum[a, z, r] = (
                    cbox[a, 0, z, r].astype(F32)
                    + ybuf[a, 1, z, r].astype(F32)
                    + ybuf[a, 2, z, r].astype(F32)
                )
            ztot[a, r] = ysum[a, 1 - zh, r].astype(BF16)

        c = remote(ztot.at[a], zbox.at[a], zsend.at[a], zrecv.at[a], anti)
        c.start()
        zcopies.append(c)
    st[...] = small.step()

    @pl.when(dp == 1)
    def _():
        forward(0, 2)
        forward(1, 0)

    @pl.when(dp == 2)
    def _():
        forward(1, 1)
        forward(0, 3)

    for a in range(2):
        zcopies[a].wait()

        @pl.loop(0, rows // 16)
        def _(i):
            r = pl.ds(pl.multiple_of(i * 16, 16), 16)
            outs[a][r] = ysum[a, zh, r] + zbox[a, r].astype(F32)

    def finish(direction, into, first):
        slot = dp - 1 if direction == 0 else dp
        for c in line_copies(direction, dp, False):
            c.wait_recv()
        for b, own, out in (
            (bufs[direction][0].at[slot], g_ref.at[dp], rg),
            (bufs[direction][1].at[slot], own_block(dp)[1], ro),
        ):
            @pl.loop(0, out.shape[0] // 16)
            def _(i):
                r = pl.ds(pl.multiple_of(i * 16, 16), 16)
                base = own[r].astype(F32) if first else out[r]
                out[r] = base + b[r].astype(F32)

    @pl.when(dp == 0)
    def _():
        finish(1, None, True)

    @pl.when(dp > 0)
    def _():
        finish(0, None, True)

    @pl.when((dp > 0) & (dp < 3))
    def _():
        finish(1, None, False)

    for c in cores + sends:
        c.wait_send()
    for t in range(1, 4):
        @pl.when(dp < t)
        def _():
            for c in line_copies(0, t, False):
                c.wait_send()
    for t in range(3):
        @pl.when(dp > t)
        def _():
            for c in line_copies(1, t, False):
                c.wait_send()


def gain_kernel(g_ref, out, box, send, recv):
    dp = lax.axis_index("dp")
    others = [lax.rem(dp + d, 4) for d in range(1, 4)]
    greet([{"dp": o} for o in others])
    copies = []
    for k, o in enumerate(others):
        c = remote(g_ref, box.at[k], send.at[k], recv.at[k], {"dp": o})
        c.start()
        copies.append(c)
    total = g_ref[...]
    for k, c in enumerate(copies):
        c.wait()
        total = total + box[k]
    out[...] = total


def post_kernel(n, x_ref, a_ref, d_ref, u_ref, k_ref, live_ref, g_ref, st_ref, bt_ref, out, dp_out, gg):
    patch = lax.broadcasted_iota(jnp.int32, (dp_out.shape[1], KEEP), 0)
    eye = (
        lax.broadcasted_iota(jnp.int32, (KEEP, KEEP), 0)
        == lax.broadcasted_iota(jnp.int32, (KEEP, KEEP), 1)
    ).astype(F32).astype(BF16)
    gain = g_ref[...]
    acc = jnp.zeros(gg.shape, F32)
    for i in range(n):
        lanes = slice(i * KEEP, (i + 1) * KEEP)
        mean = st_ref[i : i + 1, :] * (1.0 / D)
        inv = lax.rsqrt(st_ref[n + i : n + i + 1, :] * (1.0 / D) - mean * mean + EPSILON)
        mean_hat = bt_ref[i : i + 1, :] * (1.0 / D)
        mean_cross = bt_ref[n + i : n + i + 1, :] * (1.0 / D)
        rows = x_ref[:, lanes].astype(F32)
        centred = (rows - mean) * inv
        normed_grad = d_ref[:, lanes]
        acc = acc + normed_grad * centred
        d_in = u_ref[:, lanes].astype(F32) + inv * (
            normed_grad * gain - mean_hat - centred * mean_cross
        )
        pick = (patch == k_ref[i : i + 1, :]).astype(F32).astype(BF16)
        dp_out[i] = dot(pick, d_in.astype(BF16), 1, 1).astype(BF16)
        res = ((rows + a_ref[:, lanes]) * live_ref[i]).astype(BF16)
        out[lanes, :] = dot(eye, res, 1, 1).astype(BF16)
    gg[...] = acc


def call(kernel, outs, scratch=(), cid=None, vmem=48, smem=(), n_in=0):
    params = dict(vmem_limit_bytes=vmem * 1024 * 1024)
    if cid is not None:
        params.update(collective_id=cid, has_side_effects=True)
    return pl.pallas_call(
        kernel,
        out_shape=[jax.ShapeDtypeStruct(*o) for o in outs],
        in_specs=[SM if i in smem else VM for i in range(n_in)],
        out_specs=[VM] * len(outs),
        scratch_shapes=list(scratch),
        compiler_params=pltpu.CompilerParams(**params),
    )


def sharded(patches, keep_index, counts, gain, w_qkv, w_out, cotangent):
    n, patch_count, width = patches.shape
    rows = n * KEEP
    me = lax.axis_index("mrow")
    own_count = counts[lax.axis_index("dp")]
    live = (jnp.arange(n, dtype=jnp.int32) < own_count).astype(F32)
    stacked = w_qkv.reshape(w_qkv.shape[0], -1)
    feats, heads3 = stacked.shape
    heads = w_out.shape[0]
    share = rows // 4

    xt, ut, sums = call(
        partial(prep_kernel, n),
        [((width, rows), BF16), ((width, rows), BF16), ((2 * n, KEEP), F32)],
        smem=(3,), n_in=4,
    )(patches, keep_index, cotangent, live)
    gain_row = jnp.pad(gain, (0, KEEP - width))[None]
    own_gain = jnp.where(jnp.arange(16)[:, None] == me, gain_row, 0.0)
    small = 2 * n + 16
    xg, ug, stats = call(
        gather_kernel,
        [((16, width, rows), BF16), ((16, width, rows), BF16), ((small, KEEP), F32)],
        [
            pltpu.VMEM((8, small, KEEP), F32), pltpu.VMEM((4, small, KEEP), F32),
            DMA((8,)), DMA((8,)), DMA((2,)), DMA((2, 4)), DMA((2, 2)), DMA((2, 8)),
            DMA((16,)), DMA((16,)),
        ],
        cid=1, n_in=3,
    )(xt, ut, jnp.concatenate([sums, own_gain], axis=0))
    x_all = xg.reshape(feats, rows)
    u_all = ug.reshape(feats, rows)
    gain_all = stats[2 * n :, :width].reshape(feats, 1)
    stats = stats[: 2 * n]
    mean = stats[:n].reshape(1, rows) / D
    inv = lax.rsqrt(stats[n:].reshape(1, rows) / D - mean * mean + EPSILON)
    normed_f = (x_all.astype(F32) - mean) * inv * gain_all
    normed = normed_f.astype(BF16)
    qkv_part = dot(stacked, normed, 0, 0).astype(BF16)
    mix_part = dot(w_out, u_all, 1, 0).astype(BF16)
    half = (heads3 + heads) // 2
    d_all, h_all = call(
        middle_kernel,
        [((heads3, rows), BF16), ((heads, rows), BF16)],
        [
            pltpu.VMEM((heads3 + heads, share), BF16), pltpu.VMEM((heads3 + heads, share), BF16),
            pltpu.VMEM((6, half, share), BF16), pltpu.VMEM((6, heads, share), BF16),
            DMA((6,)), DMA((6,)), DMA((6,)), DMA((6,)), DMA((3, 3)), DMA((3, 4)),
        ],
        cid=2, n_in=2,
    )(qkv_part, mix_part)
    attn_part = dot(w_out, h_all, 0, 0).astype(BF16)
    dn_f = dot(stacked, d_all, 1, 0)
    hat = dn_f * gain_all
    cross = dn_f * normed_f
    back = jnp.concatenate(
        [jnp.sum(hat, axis=0).reshape(n, KEEP), jnp.sum(cross, axis=0).reshape(n, KEEP)], axis=0
    )
    dn_part = dn_f.astype(BF16)
    g_qkv = dot(normed, d_all, 1, 1).astype(BF16)
    g_out = dot(h_all, u_all, 1, 1).astype(BF16)
    ndp = 4
    gr, gc = feats // ndp, feats // ndp
    blk = (2, width, rows)
    attn, dn, back, grad_qkv, grad_out = call(
        reduce_kernel,
        [
            ((width, rows), F32), ((width, rows), F32), ((2 * n, KEEP), F32),
            ((gr, heads3), F32), ((heads, gc), F32),
        ],
        [
            pltpu.VMEM((8, 2 * n, KEEP), F32), pltpu.VMEM((4, 2 * n, KEEP), F32),
            pltpu.VMEM((2, 4) + blk, BF16), pltpu.VMEM((2, 3) + blk, BF16),
            pltpu.VMEM((2,) + blk, F32), pltpu.VMEM((2, width, rows), BF16),
            pltpu.VMEM((2, width, rows), BF16),
            pltpu.VMEM((3, gr, heads3), BF16), pltpu.VMEM((3, gr, heads3), BF16),
            pltpu.VMEM((3, heads, gc), BF16), pltpu.VMEM((3, heads, gc), BF16),
            DMA((8,)), DMA((8,)), DMA((2, 4)), DMA((2, 4)), DMA((2, 3)), DMA((2, 3)),
            DMA((2,)), DMA((2,)), DMA((2, 3, 2)), DMA((2, 3, 2)),
        ],
        cid=3, n_in=5, vmem=56,
    )(
        attn_part.reshape(2, 4, 2, width, rows), dn_part.reshape(2, 4, 2, width, rows), back,
        g_qkv.reshape(ndp, gr, heads3), g_out,
    )
    outputs, d_patches, gg = call(
        partial(post_kernel, n),
        [((rows, width), BF16), ((n, patch_count, width), BF16), ((width, KEEP), F32)],
        smem=(5,), n_in=9,
    )(xt, attn, dn, ut, keep_index, live, gain[:, None], stats, back)
    gg = jnp.pad(jnp.sum(gg, axis=1)[None], ((0, 7), (0, KEEP - width)))
    total = call(
        gain_kernel, [((8, KEEP), F32)],
        [pltpu.VMEM((3, 8, KEEP), F32), DMA((3,)), DMA((3,))], cid=4, n_in=1,
    )(gg)[0]
    part = width // ndp
    grad_gain = lax.dynamic_slice(total[0], (lax.axis_index("dp") * part,), (part,))
    return (
        outputs, d_patches, grad_qkv.reshape(gr, 3, heads3 // 3), grad_out, grad_gain
    )


def solution(mesh):
    placed = (
        P("dp", None, ("mcol", "mrow")),
        P("dp", None),
        P(),
        P(("mcol", "mrow")),
        P("mcol", None, "mrow"),
        P("mrow", "mcol"),
        P("dp", ("mcol", "mrow")),
    )
    return jax.shard_map(
        sharded,
        mesh=mesh,
        in_specs=placed,
        out_specs=(
            P("dp", ("mcol", "mrow")),
            P("dp", None, ("mcol", "mrow")),
            P(("mcol", "dp"), None, "mrow"),
            P("mrow", ("mcol", "dp")),
            P(("mcol", "mrow", "dp")),
        ),
        check_vma=False,
    )
```

```python
from functools import partial

import jax
import jax.numpy as jnp
from jax import lax
from jax.experimental import pallas as pl
from jax.experimental.pallas import tpu as pltpu
from jax.sharding import PartitionSpec as P

D = 6144
HD = 128
KEEP = 128
SLOTS = 4
SPARE = 6
CHUNKS = 3
EPSILON = 1e-06

F32 = jnp.float32
BF16 = jnp.bfloat16
MESH = pl.DeviceIdType.MESH
VM = pl.BlockSpec(memory_space=pltpu.VMEM)
SM = pl.BlockSpec(memory_space=pltpu.SMEM)
DMA = pltpu.SemaphoreType.DMA


def dot(a, b, ca, cb):
    return lax.dot_general(a, b, (((ca,), (cb,)), ((), ())), preferred_element_type=F32)


def remote(src, dst, send, recv, where):
    return pltpu.make_async_remote_copy(
        src_ref=src, dst_ref=dst, send_sem=send, recv_sem=recv, device_id=where, device_id_type=MESH
    )


def clamp(value, top):
    return jnp.minimum(jnp.maximum(value, 0), top)


def greet(peers):
    barrier = pltpu.get_barrier_semaphore()
    for peer in peers:
        pl.semaphore_signal(barrier, inc=1, device_id=peer, device_id_type=MESH)
    pl.semaphore_wait(barrier, len(peers))


def span(start, size, step=None):
    return pl.ds(pl.multiple_of(start, step or size), size)


class Place:
    def __init__(self):
        self.me = lax.axis_index("mrow")
        self.core = lax.rem(self.me, 2)
        self.y = lax.rem(lax.div(self.me, 2), 4)
        self.zh = lax.div(self.me, 8)
        self.x = lax.axis_index("mcol")
        self.dp = lax.axis_index("dp")
        self.sib = self.at(self.zh, 0, 1 - self.core)
        self.anti = self.at(1 - self.zh, 0, self.core)
        self.ys = [self.at(self.zh, d, self.core) for d in range(4)]
        self.xs = [lax.rem(self.x + d, 4) for d in range(4)]
        self.dps = [lax.rem(self.dp + d, 4) for d in range(4)]

    def at(self, zh, dy, core):
        return zh * 8 + lax.rem(self.y + dy, 4) * 2 + core

    def peers(self):
        rows = [self.sib, self.anti] + self.ys[1:]
        return (
            [{"mrow": r} for r in rows]
            + [{"mcol": c} for c in self.xs[1:]]
            + [{"dp": c} for c in self.dps[1:]]
        )


class Share:
    def __init__(self, counts, dp):
        c = [counts[g] for g in range(4)]
        keep = [jnp.minimum(v, SLOTS) for v in c]
        zero = jnp.int32(0)
        self.own = self.extra = self.spare_at = self.free = self.free_at = zero
        spare_at = free_at = zero
        for g in range(4):
            here = dp == g
            spare, free = c[g] - keep[g], SLOTS - keep[g]
            self.own = jnp.where(here, keep[g], self.own)
            self.extra = jnp.where(here, spare, self.extra)
            self.free = jnp.where(here, free, self.free)
            self.spare_at = jnp.where(here, spare_at, self.spare_at)
            self.free_at = jnp.where(here, free_at, self.free_at)
            spare_at, free_at = spare_at + spare, free_at + free

    def sent(self, slot):
        k = slot - self.spare_at
        return (k >= 0) & (k < self.extra), clamp(SLOTS + k, 2 * SLOTS - 1)

    def taken(self, position):
        return position < self.own, clamp(self.free_at + position - self.own, SPARE - 1)


class SmallSum:
    def __init__(self, place, val, box, send, recv, x_rows):
        self.place, self.val, self.box = place, val, box
        self.send, self.recv, self.x_rows = send, recv, x_rows
        self.live = []
        self.n = 0

    def push(self, peers, rows=None):
        self.live = []
        for where in peers:
            k = self.n
            self.n += 1
            stage = self.val.at[self.stage]
            box = self.box.at[k]
            if rows is not None:
                stage, box = stage.at[:rows], box.at[:rows]
            c = remote(stage, box, self.send.at[k], self.recv.at[k], where)
            c.start()
            self.live.append((k, c))

    def start(self, value):
        self.stage = 0
        self.val[0] = value
        self.push([{"mrow": self.place.sib}])

    def step(self):
        total = self.val[self.stage]
        rows = self.x_rows if self.stage == 3 else total.shape[0]
        total = total[:rows]
        for k, c in self.live:
            c.wait()
            total = total + self.box[k, :rows]
        self.stage += 1
        if self.stage < 4:
            self.val[self.stage] = total
        if self.stage == 1:
            self.push([{"mrow": r} for r in self.place.ys[1:]])
        elif self.stage == 2:
            self.push([{"mrow": self.place.anti}])
        elif self.stage == 3:
            self.push([{"mcol": c} for c in self.place.xs[1:]], self.x_rows)
        return total


class Chain:
    def __init__(self, place, own, got, fwd, send, recv):
        self.dp, self.own, self.got, self.fwd, self.send, self.recv = place.dp, own, got, fwd, send, recv
        self.near = [{"dp": place.dps[1]}, {"dp": place.dps[3]}]
        self.width = own.shape[2] // CHUNKS

    def lanes(self, ch):
        return pl.ds(ch * self.width, self.width)

    def copy(self, way, ch, first):
        src = self.own if first else self.fwd.at[way]
        return remote(
            src.at[:, :, self.lanes(ch)], self.got.at[way, :, :, self.lanes(ch)],
            self.send.at[way, ch], self.recv.at[way, ch], self.near[way],
        )

    def forward(self, way, ch):
        self.copy(way, ch, False).wait_recv()
        here = self.lanes(ch)
        self.fwd[way, :, :, here] = (
            self.got[way, :, :, here].astype(F32) + self.own[:, :, here].astype(F32)
        ).astype(BF16)
        self.copy(way, ch, False).start()

    def start(self):
        for dp, way in ((0, 0), (3, 1)):
            @pl.when(self.dp == dp)
            def _():
                for ch in range(CHUNKS):
                    self.copy(way, ch, True).start()
                self.got[way] = jnp.zeros(self.got.shape[1:], BF16)

    def run(self):
        for dp, way in ((1, 0), (2, 1)):
            @pl.when(self.dp == dp)
            def _():
                for w, ch in ((way, 0), (way, 1), (1 - way, 0), (way, 2), (1 - way, 1), (1 - way, 2)):
                    self.forward(w, ch)
        for dp, way in ((0, 1), (3, 0)):
            @pl.when(self.dp == dp)
            def _():
                for ch in range(CHUNKS):
                    self.copy(way, ch, False).wait_recv()
        for way, last in ((0, 3), (1, 0)):
            @pl.when(self.dp != last)
            def _():
                for ch in range(CHUNKS):
                    self.copy(way, ch, False).wait_send()

    def slot(self, a, s):
        here = slice(s * KEEP, (s + 1) * KEEP)
        return (
            self.own[a, :, here].astype(F32)
            + self.got[0, a, :, here].astype(F32)
            + self.got[1, a, :, here].astype(F32)
        )


def attend(q, k, v, do):
    def norm(t):
        c = t - jnp.mean(t, axis=0, keepdims=True)
        i = lax.rsqrt(jnp.mean(c * c, axis=0, keepdims=True) + EPSILON)
        return c * i, i

    def norm_back(d, y, i):
        return i * (
            d - jnp.mean(d, axis=0, keepdims=True) - y * jnp.mean(d * y, axis=0, keepdims=True)
        )

    def mm(a, b, ca, cb):
        return lax.dot_general(
            a, b, (((ca,), (cb,)), ((), ())), preferred_element_type=F32, precision=lax.Precision.HIGHEST
        )

    scale = HD ** (-0.5)
    qn, iq = norm(q)
    kn, ik = norm(k)
    w = jnp.exp(mm(kn, qn, 0, 0) * scale)
    w = w / jnp.sum(w, axis=0, keepdims=True)
    out = mm(v, w, 1, 0)
    dw = mm(v, do, 0, 0)
    ds = w * (dw - jnp.sum(w * dw, axis=0, keepdims=True)) * scale
    dv = mm(do, w, 1, 1)
    dq = norm_back(mm(kn, ds, 1, 0), qn, iq)
    dk = norm_back(mm(qn, ds, 1, 1), kn, ik)
    return out, dq, dk, dv


def gather_rows(place, locs, alls, small, zsend, ysend, fsend, csend, recv, meanwhile):
    width = locs[0].shape[0]
    me, sib, core = place.me, {"mrow": place.sib}, place.core
    right, left = {"mrow": place.ys[1]}, {"mrow": place.ys[3]}
    sends = []
    ncore = [0]

    def there(a, slot):
        return alls[a].at[span(slot * width, width)]

    def push(a, src, slot, sem, where):
        c = remote(src, there(a, slot), sem, recv.at[a, slot], where)
        c.start()
        sends.append(c)

    def got(a, slot):
        remote(locs[a], there(a, slot), zsend.at[0], recv.at[a, slot], sib).wait_recv()

    def to_sib(slot):
        for a in range(2):
            push(a, there(a, slot), slot, csend.at[a, ncore[0]], sib)
        ncore[0] += 1

    for a in range(2):
        push(a, locs[a], me, zsend.at[a], {"mrow": place.anti})
    for a in range(2):
        push(a, locs[a], me, ysend.at[a, 0], right)
        push(a, locs[a], me, ysend.at[a, 1], left)
    for a in range(2):
        push(a, locs[a], me, csend.at[a, 0], sib)
    ncore[0] = 1
    for a in range(2):
        alls[a][span(me * width, width)] = locs[a][...]
    small.step()
    meanwhile()
    anti = place.anti
    for a in range(2):
        got(a, anti)
        push(a, there(a, anti), anti, ysend.at[a, 2], right)
        push(a, there(a, anti), anti, ysend.at[a, 3], left)
    to_sib(anti)
    small.step()
    for half, zh in enumerate((place.zh, 1 - place.zh)):
        before, after = place.at(zh, 3, core), place.at(zh, 1, core)
        got(0, before)
        push(0, there(0, before), before, fsend.at[0, half], right)
        got(1, after)
        push(1, there(1, after), after, fsend.at[1, half], left)
        got(1, before)
        to_sib(before)
        got(0, after)
        to_sib(after)
        if half == 0:
            small.step()
    for zh in (place.zh, 1 - place.zh):
        far = place.at(zh, 2, core)
        got(0, far)
        got(1, far)
        to_sib(far)
    total = small.step()
    for zh in range(2):
        for dy in range(4):
            for a in range(2):
                got(a, place.at(zh, dy, 1 - core))
    for c in sends:
        c.wait_send()
    return total


def middle(place, q_ref, m_ref, dall, hall, work, own, bq, bm, sq, sm, rq, rm, gs, gr):
    x, xs = place.x, place.xs
    right, left = {"mcol": xs[1]}, {"mcol": xs[3]}
    width = own.shape[1]
    qrows = q_ref.shape[0]
    half = own.shape[0] // 2
    mrows = m_ref.shape[0]
    qminus = qrows - half

    def lanes(block):
        return span(block * width, width)

    sends = []

    def push_plus(src, slot, where):
        c = remote(src, bq.at[slot], sq.at[slot], rq.at[slot], where)
        c.start()
        sends.append(c)

    def push_minus(srcq, srcm, slot, where):
        c = remote(srcq, bq.at[slot, :qminus], sq.at[slot], rq.at[slot], where)
        d = remote(srcm, bm.at[slot], sm.at[slot], rm.at[slot], where)
        c.start()
        d.start()
        sends.extend((c, d))

    def got_plus(slot):
        remote(bq.at[slot], bq.at[slot], sq.at[slot], rq.at[slot], right).wait_recv()

    def got_minus(slot):
        remote(bq.at[slot, :qminus], bq.at[slot, :qminus], sq.at[slot], rq.at[slot], right).wait_recv()
        remote(bm.at[slot], bm.at[slot], sm.at[slot], rm.at[slot], right).wait_recv()

    plus, minus = pl.ds(0, half), pl.ds(half, qminus)
    push_plus(q_ref.at[plus, lanes(xs[2])], 0, right)
    push_minus(q_ref.at[minus, lanes(xs[2])], m_ref.at[:, lanes(xs[2])], 1, left)
    push_plus(q_ref.at[plus, lanes(xs[3])], 2, left)
    push_minus(q_ref.at[minus, lanes(xs[1])], m_ref.at[:, lanes(xs[1])], 3, right)
    got_plus(0)
    work[:half] = (bq[0].astype(F32) + q_ref[plus, lanes(xs[1])].astype(F32)).astype(BF16)
    push_plus(work.at[:half], 4, right)
    got_minus(1)
    work[half:qrows] = (
        bq[1, :qminus].astype(F32) + q_ref[minus, lanes(xs[3])].astype(F32)
    ).astype(BF16)
    work[qrows:] = (bm[1].astype(F32) + m_ref[:, lanes(xs[3])].astype(F32)).astype(BF16)
    push_minus(work.at[half:qrows], work.at[qrows:], 5, left)
    got_plus(2)
    got_minus(3)
    got_plus(4)
    got_minus(5)
    heads = mrows // HD

    def total(r0):
        cols = lanes(x)
        if r0 < half:
            parts = q_ref[r0 : r0 + HD, cols], bq[2, r0 : r0 + HD], bq[4, r0 : r0 + HD]
        elif r0 < qrows:
            b = slice(r0 - half, r0 - half + HD)
            parts = q_ref[r0 : r0 + HD, cols], bq[3, b], bq[5, b]
        else:
            b = slice(r0 - qrows, r0 - qrows + HD)
            parts = m_ref[b, cols], bm[3, b], bm[5, b]
        return parts[0].astype(F32) + parts[1].astype(F32) + parts[2].astype(F32)

    for h in range(heads):
        q, k, v, do = (total((part * heads + h) * HD) for part in range(4))
        out, dq, dk, dv = attend(q, k, v, do)
        for part, value in enumerate((dq, dk, dv, out)):
            r0 = (part * heads + h) * HD
            own[r0 : r0 + HD] = value.astype(BF16)

    dst = (
        (dall, pl.ds(0, half), pl.ds(0, half)),
        (dall, pl.ds(half, qminus), pl.ds(half, qminus)),
        (hall, pl.ds(qrows, mrows), pl.ds(0, mrows)),
    )

    def push_part(p, block, src, k, where):
        out, _, rows = dst[p]
        c = remote(src, out.at[rows, lanes(block)], gs.at[p, k], gr.at[p, block], where)
        c.start()
        sends.append(c)

    def got_part(p, block):
        out, rows_own, rows = dst[p]
        remote(
            own.at[rows_own], out.at[rows, lanes(block)], gs.at[p, 0], gr.at[p, block], right
        ).wait_recv()

    for p in range(3):
        for k, where in enumerate((right, left)):
            push_part(p, x, own.at[dst[p][1]], k, where)
    dall[:, lanes(x)] = own[:qrows]
    hall[:, lanes(x)] = own[qrows:]
    got_part(0, xs[3])
    push_part(0, xs[3], dall.at[dst[0][2], lanes(xs[3])], 2, right)
    for p in (1, 2):
        got_part(p, xs[1])
        out = dst[p][0]
        push_part(p, xs[1], out.at[dst[p][2], lanes(xs[1])], 2, left)
    got_part(1, xs[3])
    got_part(2, xs[3])
    got_part(0, xs[1])
    for p in range(3):
        got_part(p, xs[2])
    for c in sends:
        c.wait_send()


class Line:
    def __init__(self, place, owns, bufs, send, recv):
        self.dp, self.owns, self.bufs, self.send, self.recv = place.dp, owns, bufs, send, recv
        self.near = [{"dp": place.dps[1]}, {"dp": place.dps[3]}]

    def copies(self, way, t, own):
        slot = t - 1 if way == 0 else t
        return [
            remote(
                o.at[t] if own else b.at[way, slot], b.at[way, slot],
                self.send.at[way, slot, i], self.recv.at[way, slot, i], self.near[way],
            )
            for i, (o, b) in enumerate(zip(self.owns, self.bufs))
        ]

    def start(self):
        for dp, way, blocks in ((0, 0, (3, 2, 1)), (3, 1, (0, 1, 2))):
            @pl.when(self.dp == dp)
            def _():
                for t in blocks:
                    for c in self.copies(way, t, True):
                        c.start()

    def forward(self, way, t):
        slot = t - 1 if way == 0 else t
        for c in self.copies(way, t, False):
            c.wait_recv()
        for o, b in zip(self.owns, self.bufs):
            add_blocks(b.at[way, slot], o.at[t])
        for c in self.copies(way, t, False):
            c.start()

    def turn(self, n):
        for dp, todo in (
            (1, ([(0, 3)], [(0, 2), (1, 0)])[n]),
            (2, ([(1, 0)], [(1, 1), (0, 3)])[n]),
        ):
            @pl.when(self.dp == dp)
            def _():
                for way, t in todo:
                    self.forward(way, t)

    def finish(self, outs):
        dp = self.dp

        def add(way, first):
            for c in self.copies(way, dp, False):
                c.wait_recv()
            slot = dp - 1 if way == 0 else dp
            for o, b, out in zip(self.owns, self.bufs, outs):
                add_blocks(out, b.at[way, slot], o.at[dp] if first else out)

        @pl.when(dp == 0)
        def _():
            add(1, True)

        @pl.when(dp > 0)
        def _():
            add(0, True)

        @pl.when((dp > 0) & (dp < 3))
        def _():
            add(1, False)

        for t in range(1, 4):
            @pl.when(dp < t)
            def _():
                for c in self.copies(0, t, False):
                    c.wait_send()
        for t in range(3):
            @pl.when(dp > t)
            def _():
                for c in self.copies(1, t, False):
                    c.wait_send()


def add_blocks(out, *srcs):
    if len(srcs) == 1:
        srcs = (out,) + srcs
    for p in range(out.shape[0]):
        @pl.loop(0, out.shape[1] // 16)
        def _(i):
            r = span(i * 16, 16)
            total = srcs[0][p, r].astype(F32)
            for s in srcs[1:]:
                total = total + s[p, r].astype(F32)
            out[p, r] = total.astype(out.dtype)


def prep_kernel(counts, p_ref, k_ref, c_ref, own, spare, sel):
    share = Share(counts, lax.axis_index("dp"))
    patch = lax.broadcasted_iota(jnp.int32, (p_ref.shape[2], KEEP), 0)

    def put(out, place, img, mine):
        flag = jnp.where(mine, 1.0, 0.0)
        here = slice(place * KEEP, (place + 1) * KEEP)
        pick = (patch == k_ref[pl.ds(img, 1), :]).astype(F32).astype(BF16)
        out[0, :, here] = (dot(p_ref[img], pick, 1, 0) * flag).astype(BF16)
        out[1, :, here] = (c_ref[:, span(img * KEEP, KEEP)].astype(F32) * flag).astype(BF16)

    for j in range(SLOTS):
        put(own, j, j, j < share.own)
    for s in range(SPARE):
        mine, img = share.sent(s)
        put(spare, s, img, mine)
    for j in range(SLOTS):
        keep, slot = share.taken(j)
        for s in range(SPARE):
            flag = jnp.where((slot == s) & jnp.logical_not(keep), 1.0, 0.0)
            sel[j * SPARE + s : j * SPARE + s + 1, :] = jnp.zeros((1, KEEP), F32) + flag


def main_kernel(
    first, sp_own, sel, g_ref, w_ref, wo_ref,
    out_own, out_buf, out_got, gq_out, go_out, gain_out,
    x_loc, u_loc, x_all, u_all, normed, wt, wot,
    sp_got, sp_fwd, rt_fwd,
    box1, val1, box2, val2,
    q_part, m_part, d_all, h_all, work, own, bq, bm,
    a_part, n_part, cbox, ybuf, ysum, ztot, zbox,
    gq, go, gq_buf, go_buf, gbox, gval,
    s1s, s1r, s2s, s2r, zs1, ys1, fs1, cs1, r1,
    sps, spr, rts, rtr,
    sq, sm, rq, rm, gs, gr,
    cs2, cr2, ys2, yr2, zs2, zr2, lns, lnr, ggs, ggr,
):
    place = Place()
    greet(place.peers())
    width = x_loc.shape[0]
    core, zh = place.core, place.zh
    chain = Chain(place, sp_own, sp_got, sp_fwd, sps, spr)
    chain.start()
    chain.run()
    spare = [[chain.slot(a, s) for s in range(SPARE)] for a in range(2)]
    sums, squares = [], []
    for j in range(SLOTS):
        here = slice(j * KEEP, (j + 1) * KEEP)
        values = []
        for a, loc in enumerate((x_loc, u_loc)):
            v = first[a, :, here].astype(F32)
            for s in range(SPARE):
                v = v + spare[a][s] * sel[j * SPARE + s : j * SPARE + s + 1, :]
            loc[:, here] = v.astype(BF16)
            values.append(v)
        sums.append(jnp.sum(values[0], axis=0, keepdims=True))
        squares.append(jnp.sum(values[0] * values[0], axis=0, keepdims=True))
    me_row = lax.broadcasted_iota(jnp.int32, (16, KEEP), 0) == place.me
    own_gain = jnp.where(me_row, g_ref[...], 0.0)

    small = SmallSum(place, val1, box1, s1s, s1r, 2 * SLOTS)
    small.start(jnp.concatenate(sums + squares + [own_gain], axis=0))

    def turn_weights():
        for p in range(3):
            wt[p] = jnp.transpose(w_ref[p])
        wot[...] = jnp.transpose(wo_ref[...])

    stats = gather_rows(
        place, (x_loc, u_loc), (x_all, u_all), small, zs1, ys1, fs1, cs1, r1, turn_weights
    )
    gain_cols = jnp.transpose(
        jnp.concatenate([val1[3, 2 * SLOTS :], jnp.zeros((KEEP - 16, KEEP), F32)], axis=0)
    )
    mean = stats[:SLOTS] * (1.0 / D)
    inv = lax.rsqrt(stats[SLOTS:] * (1.0 / D) - mean * mean + EPSILON)
    for b in range(16):
        rb = slice(b * width, (b + 1) * width)
        col = gain_cols[:width, b : b + 1]
        for j in range(SLOTS):
            here = slice(j * KEEP, (j + 1) * KEEP)
            centred = (x_all[rb, here].astype(F32) - mean[j : j + 1]) * inv[j : j + 1]
            normed[rb, here] = (centred * col).astype(BF16)

    part = w_ref.shape[2]
    for p in range(3):
        q_part[p * part : (p + 1) * part] = dot(wt[p], normed[...], 1, 0).astype(BF16)
    m_part[...] = dot(wo_ref[...], u_all[...], 1, 0).astype(BF16)

    middle(place, q_part, m_part, d_all, h_all, work, own, bq, bm, sq, sm, rq, rm, gs, gr)

    hat = [jnp.zeros((8, KEEP), F32) for _ in range(SLOTS)]
    cross = [jnp.zeros((8, KEEP), F32) for _ in range(SLOTS)]
    feats = normed.shape[0]
    block = 2 * width
    for b in range(feats // block):
        rb = slice(b * block, (b + 1) * block)
        a_part[rb] = dot(wot[rb], h_all[...], 1, 0).astype(BF16)
        dn = dot(w_ref[0, rb], d_all[:part], 1, 0)
        for p in (1, 2):
            dn = dn + dot(w_ref[p, rb], d_all[p * part : (p + 1) * part], 1, 0)
        n_part[rb] = dn.astype(BF16)
        for i in range(2):
            col = gain_cols[:width, 2 * b + i : 2 * b + i + 1]
            ri = slice(i * width, (i + 1) * width)
            ra = slice((2 * b + i) * width, (2 * b + i + 1) * width)
            for j in range(SLOTS):
                here = slice(j * KEEP, (j + 1) * KEEP)
                d_hat = dn[ri, here] * col
                centred = (x_all[ra, here].astype(F32) - mean[j : j + 1]) * inv[j : j + 1]
                hat[j] = hat[j] + jnp.sum(d_hat.reshape(-1, 8, KEEP), axis=0)
                cross[j] = cross[j] + jnp.sum((d_hat * centred).reshape(-1, 8, KEEP), axis=0)
    back_part = jnp.concatenate(
        [jnp.sum(t, axis=0, keepdims=True) for t in hat + cross], axis=0
    )
    small = SmallSum(place, val2, box2, s2s, s2r, 2 * SLOTS)
    small.start(back_part)

    arrays = (a_part, n_part)
    sib, anti = {"mrow": place.sib}, {"mrow": place.anti}
    right, left = {"mrow": place.ys[1]}, {"mrow": place.ys[3]}
    sends = []

    def target(a, z, d, c):
        return arrays[a].at[span(place.at(z, d, c) * width, width)]

    def core_copy(a, d, z):
        return remote(
            target(a, z, d, 1 - core), cbox.at[a, d, z], cs2.at[a, d, z], cr2.at[a, d, z], sib
        )

    for d in (2, 1, 3, 0):
        for a in range(2):
            for z in range(2):
                c = core_copy(a, d, z)
                c.start()
                sends.append(c)

    def add_in(dst, srcs):
        for z in range(2):
            @pl.loop(0, width // 16)
            def _(i):
                r = span(i * 16, 16)
                total = dst[z, r].astype(F32)
                for s in srcs:
                    total = total + s[z][r].astype(F32)
                dst[z, r] = total.astype(BF16)

    def core_sum(a, d):
        for z in range(2):
            core_copy(a, d, z).wait_recv()
        add_in(cbox.at[a, d], [[target(a, z, d, core) for z in range(2)]])

    def ypush(a, src, slot, where):
        c = remote(src, ybuf.at[a, slot], ys2.at[a, slot], yr2.at[a, slot], where)
        c.start()
        sends.append(c)

    def ygot(a, slot):
        remote(ybuf.at[a, slot], ybuf.at[a, slot], ys2.at[a, slot], yr2.at[a, slot], right).wait_recv()

    ahead, behind = (right, left), (left, right)
    nxt, prv = (1, 3), (3, 1)
    for a in range(2):
        core_sum(a, 2)
        ypush(a, cbox.at[a, 2], 0, ahead[a])
    small.step()
    for a in range(2):
        core_sum(a, prv[a])
        ypush(a, cbox.at[a, prv[a]], 1, behind[a])
    for a in range(2):
        core_sum(a, nxt[a])
    small.step()

    quarter = feats // 4
    line = Line(place, (gq, go), (gq_buf, go_buf), lns, lnr)
    for t in range(4):
        rt = slice(t * quarter, (t + 1) * quarter)
        for p in range(3):
            gq[t, p] = dot(normed[rt], d_all[p * part : (p + 1) * part], 1, 1).astype(BF16)
        go[t, 0] = dot(h_all[...], u_all[rt], 1, 1).astype(BF16)
    line.start()

    for a in range(2):
        ygot(a, 0)
        add_in(cbox.at[a, nxt[a]], [[ybuf.at[a, 0, z] for z in range(2)]])
        ypush(a, cbox.at[a, nxt[a]], 2, ahead[a])
    for a in range(2):
        core_sum(a, 0)
    small.step()
    zcopies = []
    for a in range(2):
        ygot(a, 1)
        ygot(a, 2)

        @pl.loop(0, width // 16)
        def _(i):
            r = span(i * 16, 16)
            for z in range(2):
                ysum[a, z, r] = (
                    cbox[a, 0, z, r].astype(F32)
                    + ybuf[a, 1, z, r].astype(F32)
                    + ybuf[a, 2, z, r].astype(F32)
                )
            ztot[a, r] = ysum[a, 1 - zh, r].astype(BF16)

        c = remote(ztot.at[a], zbox.at[a], zs2.at[a], zr2.at[a], anti)
        c.start()
        zcopies.append(c)
    back = small.step()
    line.turn(0)
    for c in zcopies:
        c.wait()

    mean_hat = back[:SLOTS] * (1.0 / D)
    mean_cross = back[SLOTS:] * (1.0 / D)
    gain_col = jnp.transpose(jnp.broadcast_to(g_ref[...], (KEEP, KEEP)))[:width, :1]
    acc = jnp.zeros((width, KEEP), F32)
    for j in range(SLOTS):
        here = slice(j * KEEP, (j + 1) * KEEP)
        attn = ysum[0, zh, :, here] + zbox[0, :, here].astype(F32)
        dn = ysum[1, zh, :, here] + zbox[1, :, here].astype(F32)
        xv = x_loc[:, here].astype(F32)
        centred = (xv - mean[j : j + 1]) * inv[j : j + 1]
        acc = acc + dn * centred
        d_in = u_loc[:, here].astype(F32) + inv[j : j + 1] * (
            dn * gain_col - mean_hat[j : j + 1] - centred * mean_cross[j : j + 1]
        )
        out_own[0, :, here] = (xv + attn).astype(BF16)
        out_own[1, :, here] = d_in.astype(BF16)
    for s in range(SPARE):
        for a in range(2):
            value = jnp.zeros((width, KEEP), F32)
            for j in range(SLOTS):
                value = value + out_own[a, :, j * KEEP : (j + 1) * KEEP].astype(F32) * (
                    sel[j * SPARE + s : j * SPARE + s + 1, :]
                )
            out_buf[a, :, s * KEEP : (s + 1) * KEEP] = value.astype(BF16)
    gain_row = jnp.sum(
        jnp.transpose(jnp.concatenate([acc, jnp.zeros((KEEP - width, KEEP), F32)], axis=0)),
        axis=0, keepdims=True,
    )
    gval[...] = jnp.broadcast_to(gain_row, gval.shape)
    back_chain = Chain(place, out_buf, out_got, rt_fwd, rts, rtr)
    back_chain.start()
    gains = []
    for k in range(3):
        c = remote(gval, gbox.at[k], ggs.at[k], ggr.at[k], {"dp": place.dps[k + 1]})
        c.start()
        gains.append(c)
    back_chain.run()
    total = gval[...]
    for k, c in enumerate(gains):
        c.wait()
        total = total + gbox[k]
    gain_out[...] = total
    line.turn(1)
    line.finish((gq_out, go_out))
    for c in sends:
        c.wait_send()


def post_kernel(n, counts, k_ref, own_ref, buf_ref, got_ref, out, dp_out):
    share = Share(counts, lax.axis_index("dp"))
    patch = lax.broadcasted_iota(jnp.int32, (dp_out.shape[2], KEEP), 0)
    for i in range(n):
        lanes = slice(i * KEEP, (i + 1) * KEEP)
        if i < SLOTS:
            flag = jnp.where(i < share.own, 1.0, 0.0)
            res, d_in = (own_ref[a, :, lanes].astype(F32) * flag for a in range(2))
        else:
            slot = clamp(share.spare_at + i - SLOTS, SPARE - 1)
            flag = jnp.where(i - SLOTS < share.extra, 1.0, 0.0)
            here = span(slot * KEEP, KEEP)
            res, d_in = (
                (
                    buf_ref[a, :, here].astype(F32)
                    + got_ref[0, a, :, here].astype(F32)
                    + got_ref[1, a, :, here].astype(F32)
                )
                * flag
                for a in range(2)
            )
        pick = (patch == k_ref[i : i + 1, :]).astype(F32).astype(BF16)
        out[:, lanes] = res.astype(BF16)
        dp_out[i] = dot(d_in.astype(BF16), pick, 1, 1).astype(BF16)


def sharded(patches, keep_index, counts, gain, w_qkv, w_out, cotangent):
    n, patch_count, width = patches.shape
    total_rows = n * KEEP
    rows = SLOTS * KEEP
    feats = w_qkv.shape[0]
    heads = w_out.shape[0]
    heads3 = 3 * heads
    quarter = feats // 4
    half = (heads3 + heads) // 2
    gain_row = jnp.pad(gain, (0, KEEP - width))[None]
    spare = SPARE * KEEP
    small = 2 * SLOTS + 16
    blk = (2, width, rows)

    def v(shape, dtype=BF16):
        return pltpu.VMEM(shape, dtype)

    scratch = [
        v((width, rows)), v((width, rows)), v((feats, rows)), v((feats, rows)), v((feats, rows)),
        v((3, heads, feats)), v((feats, heads)),
        v((2, 2, width, spare)), v((2, 2, width, spare)), v((2, 2, width, spare)),
        v((8, small, KEEP), F32), v((4, small, KEEP), F32),
        v((8, 2 * SLOTS, KEEP), F32), v((4, 2 * SLOTS, KEEP), F32),
        v((heads3, rows)), v((heads, rows)), v((heads3, rows)), v((heads, rows)),
        v((heads3 + heads, KEEP)), v((heads3 + heads, KEEP)),
        v((6, half, KEEP)), v((6, heads, KEEP)),
        v((feats, rows)), v((feats, rows)), v((2, 4) + blk), v((2, 3) + blk),
        v((2,) + blk, F32), v((2, width, rows)), v((2, width, rows)),
        v((4, 3, quarter, heads)), v((4, 1, heads, quarter)),
        v((2, 3, 3, quarter, heads)), v((2, 3, 1, heads, quarter)),
        v((3, 8, KEEP), F32), v((8, KEEP), F32),
        DMA((8,)), DMA((8,)), DMA((8,)), DMA((8,)),
        DMA((2,)), DMA((2, 4)), DMA((2, 2)), DMA((2, 8)), DMA((2, 16)),
        DMA((2, CHUNKS)), DMA((2, CHUNKS)), DMA((2, CHUNKS)), DMA((2, CHUNKS)),
        DMA((6,)), DMA((6,)), DMA((6,)), DMA((6,)), DMA((3, 3)), DMA((3, 4)),
        DMA((2, 4, 2)), DMA((2, 4, 2)), DMA((2, 3)), DMA((2, 3)), DMA((2,)), DMA((2,)),
        DMA((2, 3, 2)), DMA((2, 3, 2)), DMA((3,)), DMA((3,)),
    ]
    shape = jax.ShapeDtypeStruct
    first, spare_own, sel = pl.pallas_call(
        prep_kernel,
        out_shape=[
            shape((2, width, rows), BF16), shape((2, width, spare), BF16),
            shape((SLOTS * SPARE, KEEP), F32),
        ],
        in_specs=[SM] + [VM] * 3,
        out_specs=[VM] * 3,
        compiler_params=pltpu.CompilerParams(vmem_limit_bytes=32 * 1024 * 1024),
    )(counts, jnp.transpose(patches, (0, 2, 1)), keep_index, cotangent.T)
    out_own, out_buf, out_got, gq, go, gg = pl.pallas_call(
        main_kernel,
        out_shape=[
            shape((2, width, rows), BF16), shape((2, width, spare), BF16),
            shape((2, 2, width, spare), BF16),
            shape((3, quarter, heads), F32), shape((1, heads, quarter), F32),
            shape((8, KEEP), F32),
        ],
        in_specs=[VM] * 6,
        out_specs=[VM] * 6,
        scratch_shapes=scratch,
        compiler_params=pltpu.CompilerParams(
            vmem_limit_bytes=58 * 1024 * 1024, collective_id=1, has_side_effects=True
        ),
    )(
        first, spare_own, sel, gain_row, jnp.transpose(w_qkv, (1, 0, 2)), w_out,
    )
    outputs, d_patches = pl.pallas_call(
        partial(post_kernel, n),
        out_shape=[shape((width, total_rows), BF16), shape((n, width, patch_count), BF16)],
        in_specs=[SM] + [VM] * 4,
        out_specs=[VM] * 2,
        compiler_params=pltpu.CompilerParams(vmem_limit_bytes=32 * 1024 * 1024),
    )(counts, keep_index, out_own, out_buf, out_got)
    part = width // 4
    grad_gain = lax.dynamic_slice(gg[0], (lax.axis_index("dp") * part,), (part,))
    return (
        outputs.T, jnp.transpose(d_patches, (0, 2, 1)), jnp.transpose(gq, (1, 0, 2)), go[0], grad_gain
    )


def solution(mesh):
    placed = (
        P("dp", None, ("mcol", "mrow")),
        P("dp", None),
        P(),
        P(("mcol", "mrow")),
        P("mcol", None, "mrow"),
        P("mrow", "mcol"),
        P("dp", ("mcol", "mrow")),
    )
    return jax.shard_map(
        sharded,
        mesh=mesh,
        in_specs=placed,
        out_specs=(
            P("dp", ("mcol", "mrow")),
            P("dp", None, ("mcol", "mrow")),
            P(("mcol", "dp"), None, "mrow"),
            P("mrow", ("mcol", "dp")),
            P(("mcol", "mrow", "dp")),
        ),
        check_vma=False,
    )
```

```python
from functools import partial

import jax
import jax.numpy as jnp
from jax import lax
from jax.experimental import pallas as pl
from jax.experimental.pallas import tpu as pltpu
from jax.sharding import PartitionSpec as P

D = 6144
HD = 128
KEEP = 128
SLOTS = 4
SPARE = 6
CHUNKS = 3
EPSILON = 1e-06

F32 = jnp.float32
BF16 = jnp.bfloat16
MESH = pl.DeviceIdType.MESH
VM = pl.BlockSpec(memory_space=pltpu.VMEM)
SM = pl.BlockSpec(memory_space=pltpu.SMEM)
ANY = pl.BlockSpec(memory_space=pl.ANY)
DMA = pltpu.SemaphoreType.DMA


def dot(a, b, ca, cb):
    return lax.dot_general(a, b, (((ca,), (cb,)), ((), ())), preferred_element_type=F32)


def remote(src, dst, send, recv, where):
    return pltpu.make_async_remote_copy(
        src_ref=src, dst_ref=dst, send_sem=send, recv_sem=recv, device_id=where, device_id_type=MESH
    )


def clamp(value, top):
    return jnp.minimum(jnp.maximum(value, 0), top)


def greet(peers):
    barrier = pltpu.get_barrier_semaphore()
    for peer in peers:
        pl.semaphore_signal(barrier, inc=1, device_id=peer, device_id_type=MESH)
    pl.semaphore_wait(barrier, len(peers))


def span(start, size, step=None):
    return pl.ds(pl.multiple_of(start, step or size), size)


def load(pairs, sem):
    copies = [pltpu.make_async_copy(src, dst, sem.at[i]) for i, (src, dst) in enumerate(pairs)]
    for c in copies:
        c.start()
    for c in copies:
        c.wait()


class Place:
    def __init__(self):
        self.me = lax.axis_index("mrow")
        self.core = lax.rem(self.me, 2)
        self.y = lax.rem(lax.div(self.me, 2), 4)
        self.zh = lax.div(self.me, 8)
        self.x = lax.axis_index("mcol")
        self.dp = lax.axis_index("dp")
        self.sib = self.at(self.zh, 0, 1 - self.core)
        self.anti = self.at(1 - self.zh, 0, self.core)
        self.ys = [self.at(self.zh, d, self.core) for d in range(4)]
        self.xs = [lax.rem(self.x + d, 4) for d in range(4)]
        self.dps = [lax.rem(self.dp + d, 4) for d in range(4)]

    def at(self, zh, dy, core):
        return zh * 8 + lax.rem(self.y + dy, 4) * 2 + core

    def peers(self):
        rows = [self.sib, self.anti] + self.ys[1:]
        return (
            [{"mrow": r} for r in rows]
            + [{"mcol": c} for c in self.xs[1:]]
            + [{"dp": c} for c in self.dps[1:]]
        )


class Share:
    def __init__(self, counts, dp):
        c = [counts[g] for g in range(4)]
        keep = [jnp.minimum(v, SLOTS) for v in c]
        zero = jnp.int32(0)
        self.own = self.extra = self.spare_at = self.free = self.free_at = zero
        spare_at = free_at = zero
        for g in range(4):
            here = dp == g
            spare, free = c[g] - keep[g], SLOTS - keep[g]
            self.own = jnp.where(here, keep[g], self.own)
            self.extra = jnp.where(here, spare, self.extra)
            self.free = jnp.where(here, free, self.free)
            self.spare_at = jnp.where(here, spare_at, self.spare_at)
            self.free_at = jnp.where(here, free_at, self.free_at)
            spare_at, free_at = spare_at + spare, free_at + free

    def sent(self, slot):
        k = slot - self.spare_at
        return (k >= 0) & (k < self.extra), clamp(SLOTS + k, 2 * SLOTS - 1)

    def taken(self, position):
        return position < self.own, clamp(self.free_at + position - self.own, SPARE - 1)


class SmallSum:
    def __init__(self, place, val, box, send, recv, x_rows):
        self.place, self.val, self.box = place, val, box
        self.send, self.recv, self.x_rows = send, recv, x_rows
        self.live = []
        self.n = 0

    def push(self, peers, rows=None):
        self.live = []
        for where in peers:
            k = self.n
            self.n += 1
            stage = self.val.at[self.stage]
            box = self.box.at[k]
            if rows is not None:
                stage, box = stage.at[:rows], box.at[:rows]
            c = remote(stage, box, self.send.at[k], self.recv.at[k], where)
            c.start()
            self.live.append((k, c))

    def start(self, value):
        self.stage = 0
        self.val[0] = value
        self.push([{"mrow": self.place.sib}])

    def step(self):
        total = self.val[self.stage]
        rows = self.x_rows if self.stage == 3 else total.shape[0]
        total = total[:rows]
        for k, c in self.live:
            c.wait()
            total = total + self.box[k, :rows]
        self.stage += 1
        if self.stage < 4:
            self.val[self.stage] = total
        if self.stage == 1:
            self.push([{"mrow": r} for r in self.place.ys[1:]])
        elif self.stage == 2:
            self.push([{"mrow": self.place.anti}])
        elif self.stage == 3:
            self.push([{"mcol": c} for c in self.place.xs[1:]], self.x_rows)
        return total


class Chain:
    def __init__(self, place, own, got, fwd, send, recv):
        self.dp, self.own, self.got, self.fwd, self.send, self.recv = place.dp, own, got, fwd, send, recv
        self.near = [{"dp": place.dps[1]}, {"dp": place.dps[3]}]
        self.width = own.shape[2] // CHUNKS

    def lanes(self, ch):
        return pl.ds(ch * self.width, self.width)

    def copy(self, way, ch, first):
        src = self.own if first else self.fwd.at[way]
        return remote(
            src.at[:, :, self.lanes(ch)], self.got.at[way, :, :, self.lanes(ch)],
            self.send.at[way, ch], self.recv.at[way, ch], self.near[way],
        )

    def forward(self, way, ch):
        self.copy(way, ch, False).wait_recv()
        here = self.lanes(ch)
        self.fwd[way, :, :, here] = (
            self.got[way, :, :, here].astype(F32) + self.own[:, :, here].astype(F32)
        ).astype(BF16)
        self.copy(way, ch, False).start()

    def start(self):
        for dp, way in ((0, 0), (3, 1)):
            @pl.when(self.dp == dp)
            def _():
                for ch in range(CHUNKS):
                    self.copy(way, ch, True).start()
                self.got[way] = jnp.zeros(self.got.shape[1:], BF16)

    def run(self):
        for dp, way in ((1, 0), (2, 1)):
            @pl.when(self.dp == dp)
            def _():
                for w, ch in ((way, 0), (way, 1), (1 - way, 0), (way, 2), (1 - way, 1), (1 - way, 2)):
                    self.forward(w, ch)
        for dp, way in ((0, 1), (3, 0)):
            @pl.when(self.dp == dp)
            def _():
                for ch in range(CHUNKS):
                    self.copy(way, ch, False).wait_recv()
        for way, last in ((0, 3), (1, 0)):
            @pl.when(self.dp != last)
            def _():
                for ch in range(CHUNKS):
                    self.copy(way, ch, False).wait_send()

    def slot(self, a, s):
        here = slice(s * KEEP, (s + 1) * KEEP)
        return (
            self.own[a, :, here].astype(F32)
            + self.got[0, a, :, here].astype(F32)
            + self.got[1, a, :, here].astype(F32)
        )


def attend(q, k, v, do):
    def norm(t):
        c = t - jnp.mean(t, axis=0, keepdims=True)
        i = lax.rsqrt(jnp.mean(c * c, axis=0, keepdims=True) + EPSILON)
        return c * i, i

    def norm_back(d, y, i):
        return i * (
            d - jnp.mean(d, axis=0, keepdims=True) - y * jnp.mean(d * y, axis=0, keepdims=True)
        )

    def mm(a, b, ca, cb):
        return lax.dot_general(
            a, b, (((ca,), (cb,)), ((), ())), preferred_element_type=F32, precision=lax.Precision.HIGHEST
        )

    scale = HD ** (-0.5)
    qn, iq = norm(q)
    kn, ik = norm(k)
    w = jnp.exp(mm(kn, qn, 0, 0) * scale)
    w = w / jnp.sum(w, axis=0, keepdims=True)
    out = mm(v, w, 1, 0)
    dw = mm(v, do, 0, 0)
    ds = w * (dw - jnp.sum(w * dw, axis=0, keepdims=True)) * scale
    dv = mm(do, w, 1, 1)
    dq = norm_back(mm(kn, ds, 1, 0), qn, iq)
    dk = norm_back(mm(qn, ds, 1, 1), kn, ik)
    return out, dq, dk, dv


def gather_rows(place, locs, alls, small, zsend, ysend, fsend, csend, recv, meanwhile):
    width = locs[0].shape[0]
    me, sib, core = place.me, {"mrow": place.sib}, place.core
    right, left = {"mrow": place.ys[1]}, {"mrow": place.ys[3]}
    sends = []
    ncore = [0]

    def there(a, slot):
        return alls[a].at[span(slot * width, width)]

    def push(a, src, slot, sem, where):
        c = remote(src, there(a, slot), sem, recv.at[a, slot], where)
        c.start()
        sends.append(c)

    def got(a, slot):
        remote(locs[a], there(a, slot), zsend.at[0], recv.at[a, slot], sib).wait_recv()

    def to_sib(slot):
        for a in range(2):
            push(a, there(a, slot), slot, csend.at[a, ncore[0]], sib)
        ncore[0] += 1

    for a in range(2):
        push(a, locs[a], me, zsend.at[a], {"mrow": place.anti})
    for a in range(2):
        push(a, locs[a], me, ysend.at[a, 0], right)
        push(a, locs[a], me, ysend.at[a, 1], left)
    for a in range(2):
        push(a, locs[a], me, csend.at[a, 0], sib)
    ncore[0] = 1
    for a in range(2):
        alls[a][span(me * width, width)] = locs[a][...]
    small.step()
    meanwhile()
    anti = place.anti
    for a in range(2):
        got(a, anti)
        push(a, there(a, anti), anti, ysend.at[a, 2], right)
        push(a, there(a, anti), anti, ysend.at[a, 3], left)
    to_sib(anti)
    small.step()
    for half, zh in enumerate((place.zh, 1 - place.zh)):
        before, after = place.at(zh, 3, core), place.at(zh, 1, core)
        got(0, before)
        push(0, there(0, before), before, fsend.at[0, half], right)
        got(1, after)
        push(1, there(1, after), after, fsend.at[1, half], left)
        got(1, before)
        to_sib(before)
        got(0, after)
        to_sib(after)
        if half == 0:
            small.step()
    for zh in (place.zh, 1 - place.zh):
        far = place.at(zh, 2, core)
        got(0, far)
        got(1, far)
        to_sib(far)
    total = small.step()
    for zh in range(2):
        for dy in range(4):
            for a in range(2):
                got(a, place.at(zh, dy, 1 - core))
    for c in sends:
        c.wait_send()
    return total


class RingX:
    def __init__(self, place, dh, send, recv):
        self.x, self.xs, self.dh, self.send, self.recv = place.x, place.xs, dh, send, recv
        self.right, self.left = {"mcol": place.xs[1]}, {"mcol": place.xs[3]}
        self.half = dh.shape[1] // 2
        self.width = dh.shape[2] // 4
        self.sends = []

    def copy(self, slot, p, block, k, where):
        view = self.dh.at[slot, pl.ds(p * self.half, self.half), span(block * self.width, self.width)]
        return remote(view, view, self.send.at[slot, p, k], self.recv.at[slot, p, block], where)

    def push(self, slot, p, block, k, where):
        c = self.copy(slot, p, block, k, where)
        c.start()
        self.sends.append(c)

    def got(self, slot, p, block):
        self.copy(slot, p, block, 0, self.right).wait_recv()

    def start(self, slot):
        for p in range(2):
            self.push(slot, p, self.x, 0, self.right)
            self.push(slot, p, self.x, 1, self.left)

    def forward(self, slot):
        self.got(slot, 0, self.xs[3])
        self.push(slot, 0, self.xs[3], 2, self.right)
        self.got(slot, 1, self.xs[1])
        self.push(slot, 1, self.xs[1], 2, self.left)

    def finish(self, slot):
        self.got(slot, 1, self.xs[3])
        self.got(slot, 0, self.xs[1])
        self.got(slot, 0, self.xs[2])
        self.got(slot, 1, self.xs[2])


class Quarters:
    def __init__(self, place, arrays, out, zsend, zrecv, send, recv):
        self.place, self.arrays, self.out = place, arrays, out
        self.zsend, self.zrecv, self.send, self.recv = zsend, zrecv, send, recv
        self.share = out.shape[2] // 8
        self.sends = []
        self.n = [0, 0]
        self.right, self.left = {"mrow": place.ys[1]}, {"mrow": place.ys[3]}
        self.sib = {"mrow": place.sib}

    def index(self, dy, core):
        return lax.rem(self.place.y + dy, 4) * 2 + core

    def view(self, a, index):
        return self.out.at[a, 1:4, span(index * self.share, self.share)]

    def zcopy(self, a, r):
        dp, mine = self.place.dps[r], self.index(0, self.place.core)
        src = self.arrays[a].at[span(dp * self.out.shape[2] + mine * self.share, self.share)]
        dst = self.out.at[a, r, span(mine * self.share, self.share)]
        return remote(src, dst, self.zsend.at[a, r], self.zrecv.at[a, r], {"dp": dp})

    def push(self, a, index, where):
        k = self.n[a]
        self.n[a] += 1
        c = remote(self.view(a, index), self.view(a, index), self.send.at[a, k], self.recv.at[a, index], where)
        c.start()
        self.sends.append(c)

    def got(self, a, index):
        remote(
            self.view(a, index), self.view(a, index), self.send.at[a, 0], self.recv.at[a, index], self.sib
        ).wait_recv()

    def start(self):
        for a in range(2):
            for r in (1, 3, 2):
                self.zcopy(a, r).start()

    def spread(self):
        mine = self.index(0, self.place.core)
        for a in range(2):
            for r in (1, 3, 2):
                self.zcopy(a, r).wait()
            for where in (self.right, self.left, self.sib):
                self.push(a, mine, where)

    def forward(self):
        before, after = self.index(3, self.place.core), self.index(1, self.place.core)
        self.got(0, before)
        self.push(0, before, self.right)
        self.got(1, after)
        self.push(1, after, self.left)
        self.got(1, before)
        self.got(0, after)
        for a in range(2):
            self.push(a, before, self.sib)
            self.push(a, after, self.sib)

    def far(self):
        far = self.index(2, self.place.core)
        for a in range(2):
            self.got(a, far)
            self.push(a, far, self.sib)

    def finish(self):
        for a in range(2):
            for dy in range(4):
                self.got(a, self.index(dy, 1 - self.place.core))


def middle(place, q_ref, m_ref, own, work, bq, bm, sq, sm, rq, rm, between):
    x, xs = place.x, place.xs
    right, left = {"mcol": xs[1]}, {"mcol": xs[3]}
    width = work.shape[1]
    qrows = q_ref.shape[0]
    half = work.shape[0] // 2
    mrows = m_ref.shape[0]
    qminus = qrows - half
    def lanes(block):
        return span(block * width, width)

    sends = []

    def push_plus(src, slot, where):
        c = remote(src, bq.at[slot], sq.at[slot], rq.at[slot], where)
        c.start()
        sends.append(c)

    def push_minus(srcq, srcm, slot, where):
        c = remote(srcq, bq.at[slot, :qminus], sq.at[slot], rq.at[slot], where)
        d = remote(srcm, bm.at[slot], sm.at[slot], rm.at[slot], where)
        c.start()
        d.start()
        sends.extend((c, d))

    def got_plus(slot):
        remote(bq.at[slot], bq.at[slot], sq.at[slot], rq.at[slot], right).wait_recv()

    def got_minus(slot):
        remote(bq.at[slot, :qminus], bq.at[slot, :qminus], sq.at[slot], rq.at[slot], right).wait_recv()
        remote(bm.at[slot], bm.at[slot], sm.at[slot], rm.at[slot], right).wait_recv()

    plus, minus = pl.ds(0, half), pl.ds(half, qminus)
    push_plus(q_ref.at[plus, lanes(xs[2])], 0, right)
    push_minus(q_ref.at[minus, lanes(xs[2])], m_ref.at[:, lanes(xs[2])], 1, left)
    push_plus(q_ref.at[plus, lanes(xs[3])], 2, left)
    push_minus(q_ref.at[minus, lanes(xs[1])], m_ref.at[:, lanes(xs[1])], 3, right)
    got_plus(0)
    work[:half] = (bq[0].astype(F32) + q_ref[plus, lanes(xs[1])].astype(F32)).astype(BF16)
    push_plus(work.at[:half], 4, right)
    got_minus(1)
    work[half:qrows] = (
        bq[1, :qminus].astype(F32) + q_ref[minus, lanes(xs[3])].astype(F32)
    ).astype(BF16)
    work[qrows:] = (bm[1].astype(F32) + m_ref[:, lanes(xs[3])].astype(F32)).astype(BF16)
    push_minus(work.at[half:qrows], work.at[qrows:], 5, left)
    got_plus(2)
    got_minus(3)
    got_plus(4)
    got_minus(5)
    between()
    heads = mrows // HD

    def total(r0):
        cols = lanes(x)
        if r0 < half:
            parts = q_ref[r0 : r0 + HD, cols], bq[2, r0 : r0 + HD], bq[4, r0 : r0 + HD]
        elif r0 < qrows:
            b = slice(r0 - half, r0 - half + HD)
            parts = q_ref[r0 : r0 + HD, cols], bq[3, b], bq[5, b]
        else:
            b = slice(r0 - qrows, r0 - qrows + HD)
            parts = m_ref[b, cols], bm[3, b], bm[5, b]
        return parts[0].astype(F32) + parts[1].astype(F32) + parts[2].astype(F32)

    for h in range(heads):
        q, k, v, do = (total((part * heads + h) * HD) for part in range(4))
        out, dq, dk, dv = attend(q, k, v, do)
        for part, value in enumerate((dq, dk, dv, out)):
            r0 = (part * heads + h) * HD
            own[r0 : r0 + HD, lanes(x)] = value.astype(BF16)
    for c in sends:
        c.wait_send()


def prep_kernel(counts, p_hbm, k_hbm, c_hbm, own, spare, sel, p_ref, k_ref, c_ref, sem):
    load(((p_hbm, p_ref), (k_hbm, k_ref), (c_hbm, c_ref)), sem)
    share = Share(counts, lax.axis_index("dp"))
    patch = lax.broadcasted_iota(jnp.int32, (p_ref.shape[2], KEEP), 0)

    def put(out, place, img, mine):
        flag = jnp.where(mine, 1.0, 0.0)
        here = slice(place * KEEP, (place + 1) * KEEP)
        pick = (patch == k_ref[pl.ds(img, 1), :]).astype(F32).astype(BF16)
        out[0, :, here] = (dot(p_ref[img], pick, 1, 0) * flag).astype(BF16)
        out[1, :, here] = (c_ref[:, span(img * KEEP, KEEP)].astype(F32) * flag).astype(BF16)

    for j in range(SLOTS):
        put(own, j, j, j < share.own)
    for s in range(SPARE):
        mine, img = share.sent(s)
        put(spare, s, img, mine)
    for j in range(SLOTS):
        keep, slot = share.taken(j)
        for s in range(SPARE):
            flag = jnp.where((slot == s) & jnp.logical_not(keep), 1.0, 0.0)
            sel[j * SPARE + s : j * SPARE + s + 1, :] = jnp.zeros((1, KEEP), F32) + flag


def main_kernel(
    first, sp_own, sel, g_ref, w_hbm, wo_hbm,
    out_own, out_buf, out_got, gq_out, go_out, gain_out,
    x_loc, u_loc, x_all, u_all, normed, wt, wot,
    sp_got, sp_fwd, rt_fwd,
    box1, val1, box2, val2,
    q_part, m_part, work, bq, bm,
    a_part, n_part, cbox, ybuf, ysum, ztot, zbox,
    dh, quarters, w_ref, wo_ref, gbox, gval,
    s1s, s1r, s2s, s2r, zs1, ys1, fs1, cs1, r1,
    sps, spr, rts, rtr,
    sq, sm, rq, rm,
    cs2, cr2, ys2, yr2, zs2, zr2, dxs, dxr, dzs, dzr, qzs, qzr, qys, qyr, wsem, ggs, ggr,
):
    loads = [pltpu.make_async_copy(w_hbm, w_ref, wsem.at[0]), pltpu.make_async_copy(wo_hbm, wo_ref, wsem.at[1])]
    for c in loads:
        c.start()
    place = Place()
    greet(place.peers())
    width = x_loc.shape[0]
    core, zh = place.core, place.zh
    chain = Chain(place, sp_own, sp_got, sp_fwd, sps, spr)
    chain.start()
    chain.run()
    spare = [[chain.slot(a, s) for s in range(SPARE)] for a in range(2)]
    sums, squares = [], []
    for j in range(SLOTS):
        here = slice(j * KEEP, (j + 1) * KEEP)
        values = []
        for a, loc in enumerate((x_loc, u_loc)):
            v = first[a, :, here].astype(F32)
            for s in range(SPARE):
                v = v + spare[a][s] * sel[j * SPARE + s : j * SPARE + s + 1, :]
            loc[:, here] = v.astype(BF16)
            values.append(v)
        sums.append(jnp.sum(values[0], axis=0, keepdims=True))
        squares.append(jnp.sum(values[0] * values[0], axis=0, keepdims=True))
    me_row = lax.broadcasted_iota(jnp.int32, (16, KEEP), 0) == place.me
    gval[...] = jnp.zeros(gval.shape, F32)
    gval[:1, :width] = g_ref[...]
    gain_row = gval[:1]
    own_gain = jnp.where(me_row, gain_row, 0.0)

    small = SmallSum(place, val1, box1, s1s, s1r, 2 * SLOTS)
    small.start(jnp.concatenate(sums + squares + [own_gain], axis=0))

    def turn_weights():
        for c in loads:
            c.wait()
        for p in range(3):
            wt[p] = jnp.transpose(w_ref[p])
        wot[...] = jnp.transpose(wo_ref[...])

    stats = gather_rows(
        place, (x_loc, u_loc), (x_all, u_all), small, zs1, ys1, fs1, cs1, r1, turn_weights
    )
    gain_cols = jnp.transpose(
        jnp.concatenate([val1[3, 2 * SLOTS :], jnp.zeros((KEEP - 16, KEEP), F32)], axis=0)
    )
    mean = stats[:SLOTS] * (1.0 / D)
    inv = lax.rsqrt(stats[SLOTS:] * (1.0 / D) - mean * mean + EPSILON)
    for b in range(16):
        rb = slice(b * width, (b + 1) * width)
        col = gain_cols[:width, b : b + 1]
        for j in range(SLOTS):
            here = slice(j * KEEP, (j + 1) * KEEP)
            centred = (x_all[rb, here].astype(F32) - mean[j : j + 1]) * inv[j : j + 1]
            normed[rb, here] = (centred * col).astype(BF16)

    fetch = Quarters(place, (normed, u_all), quarters, qzs, qzr, qys, qyr)
    fetch.start()
    part = w_ref.shape[2]
    for p in range(3):
        q_part[p * part : (p + 1) * part] = dot(wt[p], normed[...], 1, 0).astype(BF16)
    m_part[...] = dot(wo_ref[...], u_all[...], 1, 0).astype(BF16)

    mine = dh.at[0]
    middle(place, q_part, m_part, mine, work, bq, bm, sq, sm, rq, rm, fetch.spread)

    ring = RingX(place, dh, dxs, dxr)
    ring.start(0)
    here = span(place.x * KEEP, KEEP)
    zsends = [
        remote(dh.at[0, :, here], dh.at[r, :, here], dzs.at[r], dzr.at[r], {"dp": place.dps[r]})
        for r in range(1, 4)
    ]
    for r in (1, 3, 2):
        zsends[r - 1].start()
    fetch.forward()
    ring.forward(0)
    ring.finish(0)
    d_all, h_all = dh.at[0, : 3 * part], dh.at[0, 3 * part :]

    hat = [jnp.zeros((8, KEEP), F32) for _ in range(SLOTS)]
    cross = [jnp.zeros((8, KEEP), F32) for _ in range(SLOTS)]
    feats = normed.shape[0]
    block = 2 * width
    for b in range(feats // block):
        rb = slice(b * block, (b + 1) * block)
        a_part[rb] = dot(wot[rb], h_all[...], 1, 0).astype(BF16)
        dn = dot(w_ref[0, rb], d_all[:part], 1, 0)
        for p in (1, 2):
            dn = dn + dot(w_ref[p, rb], d_all[p * part : (p + 1) * part], 1, 0)
        n_part[rb] = dn.astype(BF16)
        for i in range(2):
            col = gain_cols[:width, 2 * b + i : 2 * b + i + 1]
            ri = slice(i * width, (i + 1) * width)
            ra = slice((2 * b + i) * width, (2 * b + i + 1) * width)
            for j in range(SLOTS):
                here = slice(j * KEEP, (j + 1) * KEEP)
                d_hat = dn[ri, here] * col
                centred = (x_all[ra, here].astype(F32) - mean[j : j + 1]) * inv[j : j + 1]
                hat[j] = hat[j] + jnp.sum(d_hat.reshape(-1, 8, KEEP), axis=0)
                cross[j] = cross[j] + jnp.sum((d_hat * centred).reshape(-1, 8, KEEP), axis=0)
    back_part = jnp.concatenate(
        [jnp.sum(t, axis=0, keepdims=True) for t in hat + cross], axis=0
    )
    small = SmallSum(place, val2, box2, s2s, s2r, 2 * SLOTS)
    small.start(back_part)

    arrays = (a_part, n_part)
    sib, anti = {"mrow": place.sib}, {"mrow": place.anti}
    right, left = {"mrow": place.ys[1]}, {"mrow": place.ys[3]}
    sends = []

    def target(a, z, d, c):
        return arrays[a].at[span(place.at(z, d, c) * width, width)]

    def core_copy(a, d, z):
        return remote(
            target(a, z, d, 1 - core), cbox.at[a, d, z], cs2.at[a, d, z], cr2.at[a, d, z], sib
        )

    for d in (2, 1, 3, 0):
        for a in range(2):
            for z in range(2):
                c = core_copy(a, d, z)
                c.start()
                sends.append(c)

    def add_in(dst, srcs):
        for z in range(2):
            @pl.loop(0, width // 16)
            def _(i):
                r = span(i * 16, 16)
                total = dst[z, r].astype(F32)
                for s in srcs:
                    total = total + s[z][r].astype(F32)
                dst[z, r] = total.astype(BF16)

    def core_sum(a, d):
        for z in range(2):
            core_copy(a, d, z).wait_recv()
        add_in(cbox.at[a, d], [[target(a, z, d, core) for z in range(2)]])

    def ypush(a, src, slot, where):
        c = remote(src, ybuf.at[a, slot], ys2.at[a, slot], yr2.at[a, slot], where)
        c.start()
        sends.append(c)

    def ygot(a, slot):
        remote(ybuf.at[a, slot], ybuf.at[a, slot], ys2.at[a, slot], yr2.at[a, slot], right).wait_recv()

    ahead, behind = (right, left), (left, right)
    nxt, prv = (1, 3), (3, 1)
    for a in range(2):
        core_sum(a, 2)
        ypush(a, cbox.at[a, 2], 0, ahead[a])
    small.step()
    for a in range(2):
        core_sum(a, prv[a])
        ypush(a, cbox.at[a, prv[a]], 1, behind[a])
    for a in range(2):
        core_sum(a, nxt[a])
    small.step()

    fetch.far()
    for a in range(2):
        ygot(a, 0)
        add_in(cbox.at[a, nxt[a]], [[ybuf.at[a, 0, z] for z in range(2)]])
        ypush(a, cbox.at[a, nxt[a]], 2, ahead[a])
    for a in range(2):
        core_sum(a, 0)
    small.step()
    for r in (1, 3, 2):
        zsends[r - 1].wait_recv()
        ring.start(r)
    zcopies = []
    for a in range(2):
        ygot(a, 1)
        ygot(a, 2)

        @pl.loop(0, width // 16)
        def _(i):
            r = span(i * 16, 16)
            for z in range(2):
                ysum[a, z, r] = (
                    cbox[a, 0, z, r].astype(F32)
                    + ybuf[a, 1, z, r].astype(F32)
                    + ybuf[a, 2, z, r].astype(F32)
                )
            ztot[a, r] = ysum[a, 1 - zh, r].astype(BF16)

        c = remote(ztot.at[a], zbox.at[a], zs2.at[a], zr2.at[a], anti)
        c.start()
        zcopies.append(c)
    back = small.step()
    for r in (1, 3, 2):
        ring.forward(r)
    for c in zcopies:
        c.wait()

    mean_hat = back[:SLOTS] * (1.0 / D)
    mean_cross = back[SLOTS:] * (1.0 / D)
    gain_col = jnp.transpose(jnp.broadcast_to(gain_row, (KEEP, KEEP)))[:width, :1]
    acc = jnp.zeros((width, KEEP), F32)
    for j in range(SLOTS):
        here = slice(j * KEEP, (j + 1) * KEEP)
        attn = ysum[0, zh, :, here] + zbox[0, :, here].astype(F32)
        dn = ysum[1, zh, :, here] + zbox[1, :, here].astype(F32)
        xv = x_loc[:, here].astype(F32)
        centred = (xv - mean[j : j + 1]) * inv[j : j + 1]
        acc = acc + dn * centred
        d_in = u_loc[:, here].astype(F32) + inv[j : j + 1] * (
            dn * gain_col - mean_hat[j : j + 1] - centred * mean_cross[j : j + 1]
        )
        out_own[0, :, here] = (xv + attn).astype(BF16)
        out_own[1, :, here] = d_in.astype(BF16)
    for s in range(SPARE):
        for a in range(2):
            value = jnp.zeros((width, KEEP), F32)
            for j in range(SLOTS):
                value = value + out_own[a, :, j * KEEP : (j + 1) * KEEP].astype(F32) * (
                    sel[j * SPARE + s : j * SPARE + s + 1, :]
                )
            out_buf[a, :, s * KEEP : (s + 1) * KEEP] = value.astype(BF16)
    gain_row = jnp.sum(
        jnp.transpose(jnp.concatenate([acc, jnp.zeros((KEEP - width, KEEP), F32)], axis=0)),
        axis=0, keepdims=True,
    )
    gval[...] = jnp.broadcast_to(gain_row, gval.shape)
    back_chain = Chain(place, out_buf, out_got, rt_fwd, rts, rtr)
    back_chain.start()
    gains = []
    for k in range(3):
        c = remote(gval, gbox.at[k], ggs.at[k], ggr.at[k], {"dp": place.dps[k + 1]})
        c.start()
        gains.append(c)
    fetch.finish()
    quarter = quarters.shape[2]
    for a, arr in enumerate((normed, u_all)):
        quarters[a, 0] = arr[span(place.dp * quarter, quarter)]
    for r in (1, 3, 2):
        ring.finish(r)
    for p in range(3):
        total = dot(quarters[0, 0], dh[0, p * part : (p + 1) * part], 1, 1)
        for r in range(1, 4):
            total = total + dot(quarters[0, r], dh[r, p * part : (p + 1) * part], 1, 1)
        gq_out[p] = total
    total = dot(dh[0, 3 * part :], quarters[1, 0], 1, 1)
    for r in range(1, 4):
        total = total + dot(dh[r, 3 * part :], quarters[1, r], 1, 1)
    go_out[...] = total
    back_chain.run()
    total = gval[...]
    for k, c in enumerate(gains):
        c.wait()
        total = total + gbox[k]
    gain_out[...] = total
    for c in sends + zsends + ring.sends + fetch.sends:
        c.wait_send()


def post_kernel(n, counts, k_hbm, own_hbm, buf_hbm, got_hbm, out, dp_out, k_ref, own_ref, buf_ref, got_ref, sem):
    load(((k_hbm, k_ref), (own_hbm, own_ref), (buf_hbm, buf_ref), (got_hbm, got_ref)), sem)
    share = Share(counts, lax.axis_index("dp"))
    patch = lax.broadcasted_iota(jnp.int32, (dp_out.shape[2], KEEP), 0)
    for i in range(n):
        lanes = slice(i * KEEP, (i + 1) * KEEP)
        if i < SLOTS:
            flag = jnp.where(i < share.own, 1.0, 0.0)
            res, d_in = (own_ref[a, :, lanes].astype(F32) * flag for a in range(2))
        else:
            slot = clamp(share.spare_at + i - SLOTS, SPARE - 1)
            flag = jnp.where(i - SLOTS < share.extra, 1.0, 0.0)
            here = span(slot * KEEP, KEEP)
            res, d_in = (
                (
                    buf_ref[a, :, here].astype(F32)
                    + got_ref[0, a, :, here].astype(F32)
                    + got_ref[1, a, :, here].astype(F32)
                )
                * flag
                for a in range(2)
            )
        pick = (patch == k_ref[i : i + 1, :]).astype(F32).astype(BF16)
        out[:, lanes] = res.astype(BF16)
        dp_out[i] = dot(d_in.astype(BF16), pick, 1, 1).astype(BF16)


def sharded(patches, keep_index, counts, gain, w_qkv, w_out, cotangent):
    n, patch_count, width = patches.shape
    total_rows = n * KEEP
    rows = SLOTS * KEEP
    feats = w_qkv.shape[0]
    heads = w_out.shape[0]
    heads3 = 3 * heads
    quarter = feats // 4
    half = (heads3 + heads) // 2
    gain_row = gain[None]
    spare = SPARE * KEEP
    small = 2 * SLOTS + 16
    blk = (2, width, rows)

    def v(shape, dtype=BF16):
        return pltpu.VMEM(shape, dtype)

    scratch = [
        v((width, rows)), v((width, rows)), v((feats, rows)), v((feats, rows)), v((feats, rows)),
        v((3, heads, feats)), v((feats, heads)),
        v((2, 2, width, spare)), v((2, 2, width, spare)), v((2, 2, width, spare)),
        v((8, small, KEEP), F32), v((4, small, KEEP), F32),
        v((8, 2 * SLOTS, KEEP), F32), v((4, 2 * SLOTS, KEEP), F32),
        v((heads3, rows)), v((heads, rows)),
        v((heads3 + heads, KEEP)),
        v((6, half, KEEP)), v((6, heads, KEEP)),
        v((feats, rows)), v((feats, rows)), v((2, 4) + blk), v((2, 3) + blk),
        v((2,) + blk, F32), v((2, width, rows)), v((2, width, rows)),
        v((4, heads3 + heads, rows)), v((2, 4, quarter, rows)), v((3, feats, heads)), v((heads, feats)),
        v((3, 8, KEEP), F32), v((8, KEEP), F32),
        DMA((8,)), DMA((8,)), DMA((8,)), DMA((8,)),
        DMA((2,)), DMA((2, 4)), DMA((2, 2)), DMA((2, 8)), DMA((2, 16)),
        DMA((2, CHUNKS)), DMA((2, CHUNKS)), DMA((2, CHUNKS)), DMA((2, CHUNKS)),
        DMA((6,)), DMA((6,)), DMA((6,)), DMA((6,)),
        DMA((2, 4, 2)), DMA((2, 4, 2)), DMA((2, 3)), DMA((2, 3)), DMA((2,)), DMA((2,)),
        DMA((4, 2, 3)), DMA((4, 2, 4)), DMA((4,)), DMA((4,)), DMA((2, 4)), DMA((2, 4)),
        DMA((2, 8)), DMA((2, 8)), DMA((2,)), DMA((3,)), DMA((3,)),
    ]
    shape = jax.ShapeDtypeStruct
    first, spare_own, sel = pl.pallas_call(
        prep_kernel,
        out_shape=[
            shape((2, width, rows), BF16), shape((2, width, spare), BF16),
            shape((SLOTS * SPARE, KEEP), F32),
        ],
        in_specs=[SM] + [ANY] * 3,
        out_specs=[VM] * 3,
        scratch_shapes=[
            v((n, width, patch_count)), v((n, KEEP), jnp.int32), v((width, total_rows)), DMA((3,))
        ],
        compiler_params=pltpu.CompilerParams(vmem_limit_bytes=58 * 1024 * 1024),
    )(counts, jnp.transpose(patches, (0, 2, 1)), keep_index, cotangent.T)
    out_own, out_buf, out_got, gq, go, gg = pl.pallas_call(
        main_kernel,
        out_shape=[
            shape((2, width, rows), BF16), shape((2, width, spare), BF16),
            shape((2, 2, width, spare), BF16),
            shape((3, quarter, heads), F32), shape((heads, quarter), F32),
            shape((8, KEEP), F32),
        ],
        in_specs=[VM] * 4 + [ANY] * 2,
        out_specs=[VM] * 6,
        scratch_shapes=scratch,
        compiler_params=pltpu.CompilerParams(
            vmem_limit_bytes=58 * 1024 * 1024, collective_id=1, has_side_effects=True
        ),
    )(
        first, spare_own, sel, gain_row, jnp.transpose(w_qkv, (1, 0, 2)), w_out,
    )
    outputs, d_patches = pl.pallas_call(
        partial(post_kernel, n),
        out_shape=[shape((width, total_rows), BF16), shape((n, width, patch_count), BF16)],
        in_specs=[SM] + [ANY] * 4,
        out_specs=[VM] * 2,
        scratch_shapes=[
            v((n, KEEP), jnp.int32), v((2, width, rows)), v((2, width, spare)), v((2, 2, width, spare)),
            DMA((4,)),
        ],
        compiler_params=pltpu.CompilerParams(vmem_limit_bytes=58 * 1024 * 1024),
    )(counts, keep_index, out_own, out_buf, out_got)
    part = width // 4
    grad_gain = lax.dynamic_slice(gg[0], (lax.axis_index("dp") * part,), (part,))
    return (
        outputs.T, jnp.transpose(d_patches, (0, 2, 1)), jnp.transpose(gq, (1, 0, 2)), go, grad_gain
    )


def solution(mesh):
    placed = (
        P("dp", None, ("mcol", "mrow")),
        P("dp", None),
        P(),
        P(("mcol", "mrow")),
        P("mcol", None, "mrow"),
        P("mrow", "mcol"),
        P("dp", ("mcol", "mrow")),
    )
    return jax.shard_map(
        sharded,
        mesh=mesh,
        in_specs=placed,
        out_specs=(
            P("dp", ("mcol", "mrow")),
            P("dp", None, ("mcol", "mrow")),
            P(("mcol", "dp"), None, "mrow"),
            P("mrow", ("mcol", "dp")),
            P(("mcol", "mrow", "dp")),
        ),
        check_vma=False,
    )
```

```python
from functools import partial

import jax
import jax.numpy as jnp
from jax import lax
from jax.experimental import pallas as pl
from jax.experimental.pallas import tpu as pltpu
from jax.sharding import PartitionSpec as P

D = 6144
HD = 128
KEEP = 128
SLOTS = 4
SPARE = 6
CHUNKS = 3
EPSILON = 1e-06

F32 = jnp.float32
BF16 = jnp.bfloat16
MESH = pl.DeviceIdType.MESH
VM = pl.BlockSpec(memory_space=pltpu.VMEM)
SM = pl.BlockSpec(memory_space=pltpu.SMEM)
ANY = pl.BlockSpec(memory_space=pl.ANY)
DMA = pltpu.SemaphoreType.DMA


def dot(a, b, ca, cb):
    return lax.dot_general(a, b, (((ca,), (cb,)), ((), ())), preferred_element_type=F32)


def remote(src, dst, send, recv, where):
    return pltpu.make_async_remote_copy(
        src_ref=src, dst_ref=dst, send_sem=send, recv_sem=recv, device_id=where, device_id_type=MESH
    )


def clamp(value, top):
    return jnp.minimum(jnp.maximum(value, 0), top)


def greet(peers):
    barrier = pltpu.get_barrier_semaphore()
    for peer in peers:
        pl.semaphore_signal(barrier, inc=1, device_id=peer, device_id_type=MESH)
    pl.semaphore_wait(barrier, len(peers))


def span(start, size, step=None):
    return pl.ds(pl.multiple_of(start, step or size), size)


def load(pairs, sem):
    copies = [pltpu.make_async_copy(src, dst, sem.at[i]) for i, (src, dst) in enumerate(pairs)]
    for c in copies:
        c.start()
    for c in copies:
        c.wait()


class Place:
    def __init__(self):
        self.me = lax.axis_index("mrow")
        self.core = lax.rem(self.me, 2)
        self.y = lax.rem(lax.div(self.me, 2), 4)
        self.zh = lax.div(self.me, 8)
        self.x = lax.axis_index("mcol")
        self.dp = lax.axis_index("dp")
        self.sib = self.at(self.zh, 0, 1 - self.core)
        self.anti = self.at(1 - self.zh, 0, self.core)
        self.ys = [self.at(self.zh, d, self.core) for d in range(4)]
        self.xs = [lax.rem(self.x + d, 4) for d in range(4)]
        self.dps = [lax.rem(self.dp + d, 4) for d in range(4)]

    def at(self, zh, dy, core):
        return zh * 8 + lax.rem(self.y + dy, 4) * 2 + core

    def peers(self):
        rows = [self.sib, self.anti] + self.ys[1:]
        return (
            [{"mrow": r} for r in rows]
            + [{"mcol": c} for c in self.xs[1:]]
            + [{"dp": c} for c in self.dps[1:]]
        )


class Share:
    def __init__(self, counts, dp):
        c = [counts[g] for g in range(4)]
        keep = [jnp.minimum(v, SLOTS) for v in c]
        zero = jnp.int32(0)
        self.own = self.extra = self.spare_at = self.free = self.free_at = zero
        spare_at = free_at = zero
        for g in range(4):
            here = dp == g
            spare, free = c[g] - keep[g], SLOTS - keep[g]
            self.own = jnp.where(here, keep[g], self.own)
            self.extra = jnp.where(here, spare, self.extra)
            self.free = jnp.where(here, free, self.free)
            self.spare_at = jnp.where(here, spare_at, self.spare_at)
            self.free_at = jnp.where(here, free_at, self.free_at)
            spare_at, free_at = spare_at + spare, free_at + free

    def holds(self, slot, image):
        k = image - SLOTS
        return jnp.where((self.spare_at + k == slot) & (k < self.extra), 1.0, 0.0)

    def keeps(self, position):
        return jnp.where(position < self.own, 1.0, 0.0)

    def works(self, position, slot):
        k = position - self.own
        return jnp.where((k >= 0) & (self.free_at + k == slot), 1.0, 0.0)


class SmallSum:
    def __init__(self, place, val, box, send, recv, x_rows):
        self.place, self.val, self.box = place, val, box
        self.send, self.recv, self.x_rows = send, recv, x_rows
        self.live = []
        self.n = 0

    def push(self, peers, rows=None):
        self.live = []
        for where in peers:
            k = self.n
            self.n += 1
            stage = self.val.at[self.stage]
            box = self.box.at[k]
            if rows is not None:
                stage, box = stage.at[:rows], box.at[:rows]
            c = remote(stage, box, self.send.at[k], self.recv.at[k], where)
            c.start()
            self.live.append((k, c))

    def start(self, value):
        self.stage = 0
        self.val[0] = value
        self.push([{"mrow": self.place.sib}])

    def step(self):
        total = self.val[self.stage]
        rows = self.x_rows if self.stage == 3 else total.shape[0]
        total = total[:rows]
        for k, c in self.live:
            c.wait()
            total = total + self.box[k, :rows]
        self.stage += 1
        if self.stage < 4:
            self.val[self.stage] = total
        if self.stage == 1:
            self.push([{"mrow": r} for r in self.place.ys[1:]])
        elif self.stage == 2:
            self.push([{"mrow": self.place.anti}])
        elif self.stage == 3:
            self.push([{"mcol": c} for c in self.place.xs[1:]], self.x_rows)
        return total


class Chain:
    def __init__(self, place, own, got, fwd, send, recv):
        self.dp, self.own, self.got, self.fwd, self.send, self.recv = place.dp, own, got, fwd, send, recv
        self.near = [{"dp": place.dps[1]}, {"dp": place.dps[3]}]
        self.width = own.shape[1] // CHUNKS

    def lanes(self, ch):
        return pl.ds(ch * self.width, self.width)

    def copy(self, way, ch, first):
        src = self.own if first else self.fwd.at[way]
        return remote(
            src.at[:, self.lanes(ch)], self.got.at[way, :, self.lanes(ch)],
            self.send.at[way, ch], self.recv.at[way, ch], self.near[way],
        )

    def forward(self, way, ch):
        self.copy(way, ch, False).wait_recv()
        here = self.lanes(ch)
        self.fwd[way, :, here] = (
            self.got[way, :, here].astype(F32) + self.own[:, here].astype(F32)
        ).astype(BF16)
        self.copy(way, ch, False).start()

    def start(self):
        for dp, way in ((0, 0), (3, 1)):
            @pl.when(self.dp == dp)
            def _():
                for ch in range(CHUNKS):
                    self.copy(way, ch, True).start()
                self.got[way] = jnp.zeros(self.got.shape[1:], BF16)

    def run(self):
        for dp, way in ((1, 0), (2, 1)):
            @pl.when(self.dp == dp)
            def _():
                for w, ch in ((way, 0), (way, 1), (1 - way, 0), (way, 2), (1 - way, 1), (1 - way, 2)):
                    self.forward(w, ch)
        for dp, way in ((0, 1), (3, 0)):
            @pl.when(self.dp == dp)
            def _():
                for ch in range(CHUNKS):
                    self.copy(way, ch, False).wait_recv()
        for way, last in ((0, 3), (1, 0)):
            @pl.when(self.dp != last)
            def _():
                for ch in range(CHUNKS):
                    self.copy(way, ch, False).wait_send()

    def slot(self, s):
        here = slice(s * KEEP, (s + 1) * KEEP)
        return (
            self.own[:, here].astype(F32)
            + self.got[0, :, here].astype(F32)
            + self.got[1, :, here].astype(F32)
        )


def attend(q, k, v, do):
    def norm(t):
        c = t - jnp.mean(t, axis=0, keepdims=True)
        i = lax.rsqrt(jnp.mean(c * c, axis=0, keepdims=True) + EPSILON)
        return c * i, i

    def norm_back(d, y, i):
        return i * (
            d - jnp.mean(d, axis=0, keepdims=True) - y * jnp.mean(d * y, axis=0, keepdims=True)
        )

    def mm(a, b, ca, cb):
        return lax.dot_general(
            a, b, (((ca,), (cb,)), ((), ())), preferred_element_type=F32, precision=lax.Precision.HIGHEST
        )

    scale = HD ** (-0.5)
    qn, iq = norm(q)
    kn, ik = norm(k)
    w = jnp.exp(mm(kn, qn, 0, 0) * scale)
    w = w / jnp.sum(w, axis=0, keepdims=True)
    out = mm(v, w, 1, 0)
    dw = mm(v, do, 0, 0)
    ds = w * (dw - jnp.sum(w * dw, axis=0, keepdims=True)) * scale
    dv = mm(do, w, 1, 1)
    dq = norm_back(mm(kn, ds, 1, 0), qn, iq)
    dk = norm_back(mm(qn, ds, 1, 1), kn, ik)
    return out, dq, dk, dv


def gather_rows(
    place, locs, alls, small, zsend, ysend, fsend, csend, recv, choose_second, meanwhile
):
    width = locs[0].shape[0]
    me, sib, core = place.me, {"mrow": place.sib}, place.core
    right, left = {"mrow": place.ys[1]}, {"mrow": place.ys[3]}
    sends = []
    ncore = [0]

    def there(a, slot):
        return alls[a].at[span(slot * width, width)]

    def push(a, src, slot, sem, where):
        c = remote(src, there(a, slot), sem, recv.at[a, slot], where)
        c.start()
        sends.append(c)

    def got(a, slot):
        remote(locs[a], there(a, slot), zsend.at[0], recv.at[a, slot], sib).wait_recv()

    def to_sib(slot):
        for a in range(2):
            push(a, there(a, slot), slot, csend.at[a, ncore[0]], sib)
        ncore[0] += 1

    for a in range(2):
        if a == 1:
            choose_second()
        push(a, locs[a], me, zsend.at[a], {"mrow": place.anti})
        push(a, locs[a], me, ysend.at[a, 0], right)
        push(a, locs[a], me, ysend.at[a, 1], left)
        push(a, locs[a], me, csend.at[a, 0], sib)
        alls[a][span(me * width, width)] = locs[a][...]
    ncore[0] = 1
    small.step()
    meanwhile()
    anti = place.anti
    for a in range(2):
        got(a, anti)
        push(a, there(a, anti), anti, ysend.at[a, 2], right)
        push(a, there(a, anti), anti, ysend.at[a, 3], left)
    to_sib(anti)
    small.step()
    for half, zh in enumerate((place.zh, 1 - place.zh)):
        before, after = place.at(zh, 3, core), place.at(zh, 1, core)
        got(0, before)
        push(0, there(0, before), before, fsend.at[0, half], right)
        got(1, after)
        push(1, there(1, after), after, fsend.at[1, half], left)
        got(1, before)
        to_sib(before)
        got(0, after)
        to_sib(after)
        if half == 0:
            small.step()
    for zh in (place.zh, 1 - place.zh):
        far = place.at(zh, 2, core)
        got(0, far)
        got(1, far)
        to_sib(far)
    total = small.step()
    for zh in range(2):
        for dy in range(4):
            for a in range(2):
                got(a, place.at(zh, dy, 1 - core))
    for c in sends:
        c.wait_send()
    return total


class RingX:
    def __init__(self, place, dh, send, recv):
        self.x, self.xs, self.dh, self.send, self.recv = place.x, place.xs, dh, send, recv
        self.right, self.left = {"mcol": place.xs[1]}, {"mcol": place.xs[3]}
        self.half = dh.shape[1] // 2
        self.width = dh.shape[2] // 4
        self.sends = []

    def copy(self, slot, p, block, k, where):
        view = self.dh.at[slot, pl.ds(p * self.half, self.half), span(block * self.width, self.width)]
        return remote(view, view, self.send.at[slot, p, k], self.recv.at[slot, p, block], where)

    def push(self, slot, p, block, k, where):
        c = self.copy(slot, p, block, k, where)
        c.start()
        self.sends.append(c)

    def got(self, slot, p, block):
        self.copy(slot, p, block, 0, self.right).wait_recv()

    def start(self, slot):
        for p in range(2):
            self.push(slot, p, self.x, 0, self.right)
            self.push(slot, p, self.x, 1, self.left)

    def forward(self, slot):
        self.got(slot, 0, self.xs[3])
        self.push(slot, 0, self.xs[3], 2, self.right)
        self.got(slot, 1, self.xs[1])
        self.push(slot, 1, self.xs[1], 2, self.left)

    def finish(self, slot):
        self.got(slot, 1, self.xs[3])
        self.got(slot, 0, self.xs[1])
        self.got(slot, 0, self.xs[2])
        self.got(slot, 1, self.xs[2])


class Quarters:
    def __init__(self, place, arrays, out, zsend, zrecv, send, recv):
        self.place, self.arrays, self.out = place, arrays, out
        self.zsend, self.zrecv, self.send, self.recv = zsend, zrecv, send, recv
        self.share = out.shape[2] // 8
        self.sends = []
        self.n = [0, 0]
        self.right, self.left = {"mrow": place.ys[1]}, {"mrow": place.ys[3]}
        self.sib = {"mrow": place.sib}

    def index(self, dy, core):
        return lax.rem(self.place.y + dy, 4) * 2 + core

    def view(self, a, index):
        return self.out.at[a, 1:4, span(index * self.share, self.share)]

    def zcopy(self, a, r):
        dp, mine = self.place.dps[r], self.index(0, self.place.core)
        src = self.arrays[a].at[span(dp * self.out.shape[2] + mine * self.share, self.share)]
        dst = self.out.at[a, r, span(mine * self.share, self.share)]
        return remote(src, dst, self.zsend.at[a, r], self.zrecv.at[a, r], {"dp": dp})

    def push(self, a, index, where):
        k = self.n[a]
        self.n[a] += 1
        c = remote(self.view(a, index), self.view(a, index), self.send.at[a, k], self.recv.at[a, index], where)
        c.start()
        self.sends.append(c)

    def got(self, a, index):
        remote(
            self.view(a, index), self.view(a, index), self.send.at[a, 0], self.recv.at[a, index], self.sib
        ).wait_recv()

    def start(self):
        for a in range(2):
            for r in (1, 3, 2):
                self.zcopy(a, r).start()

    def spread(self):
        mine = self.index(0, self.place.core)
        for a in range(2):
            for r in (1, 3, 2):
                self.zcopy(a, r).wait()
            for where in (self.right, self.left, self.sib):
                self.push(a, mine, where)

    def forward(self):
        before, after = self.index(3, self.place.core), self.index(1, self.place.core)
        self.got(0, before)
        self.push(0, before, self.right)
        self.got(1, after)
        self.push(1, after, self.left)
        self.got(1, before)
        self.got(0, after)
        for a in range(2):
            self.push(a, before, self.sib)
            self.push(a, after, self.sib)

    def far(self):
        far = self.index(2, self.place.core)
        for a in range(2):
            self.got(a, far)
            self.push(a, far, self.sib)

    def finish(self):
        for a in range(2):
            for dy in range(4):
                self.got(a, self.index(dy, 1 - self.place.core))


def middle(place, q_ref, m_ref, own, work, bq, bm, sq, sm, rq, rm, between):
    x, xs = place.x, place.xs
    right, left = {"mcol": xs[1]}, {"mcol": xs[3]}
    width = work.shape[1]
    qrows = q_ref.shape[0]
    half = work.shape[0] // 2
    mrows = m_ref.shape[0]
    qminus = qrows - half
    def lanes(block):
        return span(block * width, width)

    sends = []

    def push_plus(src, slot, where):
        c = remote(src, bq.at[slot], sq.at[slot], rq.at[slot], where)
        c.start()
        sends.append(c)

    def push_minus(srcq, srcm, slot, where):
        c = remote(srcq, bq.at[slot, :qminus], sq.at[slot], rq.at[slot], where)
        d = remote(srcm, bm.at[slot], sm.at[slot], rm.at[slot], where)
        c.start()
        d.start()
        sends.extend((c, d))

    def got_plus(slot):
        remote(bq.at[slot], bq.at[slot], sq.at[slot], rq.at[slot], right).wait_recv()

    def got_minus(slot):
        remote(bq.at[slot, :qminus], bq.at[slot, :qminus], sq.at[slot], rq.at[slot], right).wait_recv()
        remote(bm.at[slot], bm.at[slot], sm.at[slot], rm.at[slot], right).wait_recv()

    plus, minus = pl.ds(0, half), pl.ds(half, qminus)
    push_plus(q_ref.at[plus, lanes(xs[2])], 0, right)
    push_minus(q_ref.at[minus, lanes(xs[2])], m_ref.at[:, lanes(xs[2])], 1, left)
    push_plus(q_ref.at[plus, lanes(xs[3])], 2, left)
    push_minus(q_ref.at[minus, lanes(xs[1])], m_ref.at[:, lanes(xs[1])], 3, right)
    got_plus(0)
    work[:half] = (bq[0].astype(F32) + q_ref[plus, lanes(xs[1])].astype(F32)).astype(BF16)
    push_plus(work.at[:half], 4, right)
    got_minus(1)
    work[half:qrows] = (
        bq[1, :qminus].astype(F32) + q_ref[minus, lanes(xs[3])].astype(F32)
    ).astype(BF16)
    work[qrows:] = (bm[1].astype(F32) + m_ref[:, lanes(xs[3])].astype(F32)).astype(BF16)
    push_minus(work.at[half:qrows], work.at[qrows:], 5, left)
    got_plus(2)
    got_minus(3)
    got_plus(4)
    got_minus(5)
    between()
    heads = mrows // HD

    def total(r0):
        cols = lanes(x)
        if r0 < half:
            parts = q_ref[r0 : r0 + HD, cols], bq[2, r0 : r0 + HD], bq[4, r0 : r0 + HD]
        elif r0 < qrows:
            b = slice(r0 - half, r0 - half + HD)
            parts = q_ref[r0 : r0 + HD, cols], bq[3, b], bq[5, b]
        else:
            b = slice(r0 - qrows, r0 - qrows + HD)
            parts = m_ref[b, cols], bm[3, b], bm[5, b]
        return parts[0].astype(F32) + parts[1].astype(F32) + parts[2].astype(F32)

    for h in range(heads):
        q, k, v, do = (total((part * heads + h) * HD) for part in range(4))
        out, dq, dk, dv = attend(q, k, v, do)
        for part, value in enumerate((dq, dk, dv, out)):
            r0 = (part * heads + h) * HD
            own[r0 : r0 + HD, lanes(x)] = value.astype(BF16)
    for c in sends:
        c.wait_send()


def main_kernel(
    counts, p_hbm, k_hbm, c_hbm, g_hbm, w_hbm, wo_hbm,
    out_own, out_buf, out_got, gq_out, go_out, gain_out,
    x_loc, u_loc, x_all, u_all, normed, wt, wot,
    p_ref, k_ref, c_ref, g_ref, sp_own, sp_got, sp_fwd, rt_fwd,
    box1, val1, box2, val2,
    q_part, m_part, work, bq, bm,
    a_part, n_part, cbox, ybuf, ysum, ztot, zbox,
    dh, quarters, w_ref, wo_ref, gbox, gval,
    s1s, s1r, s2s, s2r, zs1, ys1, fs1, cs1, r1,
    sps, spr, rts, rtr,
    sq, sm, rq, rm,
    cs2, cr2, ys2, yr2, zs2, zr2, dxs, dxr, dzs, dzr, qzs, qzr, qys, qyr, wsem, ggs, ggr,
):
    pairs = (
        (p_hbm, p_ref), (k_hbm, k_ref), (c_hbm, c_ref), (g_hbm, g_ref), (w_hbm, w_ref), (wo_hbm, wo_ref)
    )
    loads = [pltpu.make_async_copy(src, dst, wsem.at[i]) for i, (src, dst) in enumerate(pairs)]
    for c in loads:
        c.start()
    place = Place()
    peers = place.peers()
    barrier = pltpu.get_barrier_semaphore()
    for peer in peers:
        pl.semaphore_signal(barrier, inc=1, device_id=peer, device_id_type=MESH)
    width = x_loc.shape[0]
    core, zh = place.core, place.zh
    share = Share(counts, place.dp)
    patch = lax.broadcasted_iota(jnp.int32, (p_ref.shape[2], KEEP), 0)
    for c in loads[:4]:
        c.wait()

    def lanes_of(i):
        return slice(i * KEEP, (i + 1) * KEEP)

    def kept(i):
        pick = (patch == k_ref[i : i + 1, :]).astype(F32).astype(BF16)
        return dot(p_ref[i], pick, 1, 0)

    late = [(kept(i), c_ref[:, lanes_of(i)].astype(F32)) for i in range(SLOTS, 2 * SLOTS)]
    for s in range(SPARE):
        flags = [share.holds(s, i) for i in range(SLOTS, 2 * SLOTS)]
        for a in range(2):
            total = late[0][a] * flags[0]
            for image, flag in zip(late[1:], flags[1:]):
                total = total + image[a] * flag
            sp_own[a, :, lanes_of(s)] = total.astype(BF16)
    pl.semaphore_wait(barrier, len(peers))
    chains = [
        Chain(place, sp_own.at[a], sp_got.at[a], sp_fwd.at[a], sps.at[a], spr.at[a]) for a in range(2)
    ]
    for chain in chains:
        chain.start()
    first = [kept(j) for j in range(SLOTS)], [c_ref[:, lanes_of(j)].astype(F32) for j in range(SLOTS)]
    keeps = [share.keeps(j) for j in range(SLOTS)]
    works = [[share.works(j, s) for s in range(SPARE)] for j in range(SLOTS)]

    def choose(a, loc):
        chains[a].run()
        spare = [chains[a].slot(s) for s in range(SPARE)]
        values = []
        for j in range(SLOTS):
            v = first[a][j] * keeps[j]
            for s in range(SPARE):
                v = v + spare[s] * works[j][s]
            loc[:, lanes_of(j)] = v.astype(BF16)
            values.append(v)
        return values

    values = choose(0, x_loc)
    sums = [jnp.sum(v, axis=0, keepdims=True) for v in values]
    squares = [jnp.sum(v * v, axis=0, keepdims=True) for v in values]
    me_row = lax.broadcasted_iota(jnp.int32, (16, KEEP), 0) == place.me
    gval[...] = jnp.zeros(gval.shape, F32)
    gval[:1, :width] = g_ref[...]
    gain_row = gval[:1]
    own_gain = jnp.where(me_row, gain_row, 0.0)

    small = SmallSum(place, val1, box1, s1s, s1r, 2 * SLOTS)
    small.start(jnp.concatenate(sums + squares + [own_gain], axis=0))

    def turn_weights():
        for c in loads[4:]:
            c.wait()
        for p in range(3):
            wt[p] = jnp.transpose(w_ref[p])
        wot[...] = jnp.transpose(wo_ref[...])

    stats = gather_rows(
        place, (x_loc, u_loc), (x_all, u_all), small, zs1, ys1, fs1, cs1, r1,
        lambda: choose(1, u_loc), turn_weights,
    )
    gain_cols = jnp.transpose(
        jnp.concatenate([val1[3, 2 * SLOTS :], jnp.zeros((KEEP - 16, KEEP), F32)], axis=0)
    )
    mean = stats[:SLOTS] * (1.0 / D)
    inv = lax.rsqrt(stats[SLOTS:] * (1.0 / D) - mean * mean + EPSILON)
    for b in range(16):
        rb = slice(b * width, (b + 1) * width)
        col = gain_cols[:width, b : b + 1]
        for j in range(SLOTS):
            here = slice(j * KEEP, (j + 1) * KEEP)
            centred = (x_all[rb, here].astype(F32) - mean[j : j + 1]) * inv[j : j + 1]
            normed[rb, here] = (centred * col).astype(BF16)

    fetch = Quarters(place, (normed, u_all), quarters, qzs, qzr, qys, qyr)
    fetch.start()
    part = w_ref.shape[2]
    for p in range(3):
        q_part[p * part : (p + 1) * part] = dot(wt[p], normed[...], 1, 0).astype(BF16)
    m_part[...] = dot(wo_ref[...], u_all[...], 1, 0).astype(BF16)

    mine = dh.at[0]
    middle(place, q_part, m_part, mine, work, bq, bm, sq, sm, rq, rm, fetch.spread)

    ring = RingX(place, dh, dxs, dxr)
    ring.start(0)
    here = span(place.x * KEEP, KEEP)
    zsends = [
        remote(dh.at[0, :, here], dh.at[r, :, here], dzs.at[r], dzr.at[r], {"dp": place.dps[r]})
        for r in range(1, 4)
    ]
    for r in (1, 3, 2):
        zsends[r - 1].start()
    fetch.forward()
    ring.forward(0)
    ring.finish(0)
    d_all, h_all = dh.at[0, : 3 * part], dh.at[0, 3 * part :]

    hat = [jnp.zeros((8, KEEP), F32) for _ in range(SLOTS)]
    cross = [jnp.zeros((8, KEEP), F32) for _ in range(SLOTS)]
    feats = normed.shape[0]
    block = 2 * width
    for b in range(feats // block):
        rb = slice(b * block, (b + 1) * block)
        a_part[rb] = dot(wot[rb], h_all[...], 1, 0).astype(BF16)
        dn = dot(w_ref[0, rb], d_all[:part], 1, 0)
        for p in (1, 2):
            dn = dn + dot(w_ref[p, rb], d_all[p * part : (p + 1) * part], 1, 0)
        n_part[rb] = dn.astype(BF16)
        for i in range(2):
            col = gain_cols[:width, 2 * b + i : 2 * b + i + 1]
            ri = slice(i * width, (i + 1) * width)
            ra = slice((2 * b + i) * width, (2 * b + i + 1) * width)
            for j in range(SLOTS):
                here = slice(j * KEEP, (j + 1) * KEEP)
                d_hat = dn[ri, here] * col
                centred = (x_all[ra, here].astype(F32) - mean[j : j + 1]) * inv[j : j + 1]
                hat[j] = hat[j] + jnp.sum(d_hat.reshape(-1, 8, KEEP), axis=0)
                cross[j] = cross[j] + jnp.sum((d_hat * centred).reshape(-1, 8, KEEP), axis=0)
    back_part = jnp.concatenate(
        [jnp.sum(t, axis=0, keepdims=True) for t in hat + cross], axis=0
    )
    small = SmallSum(place, val2, box2, s2s, s2r, 2 * SLOTS)
    small.start(back_part)

    arrays = (a_part, n_part)
    sib, anti = {"mrow": place.sib}, {"mrow": place.anti}
    right, left = {"mrow": place.ys[1]}, {"mrow": place.ys[3]}
    sends = []

    def target(a, z, d, c):
        return arrays[a].at[span(place.at(z, d, c) * width, width)]

    def core_copy(a, d, z):
        return remote(
            target(a, z, d, 1 - core), cbox.at[a, d, z], cs2.at[a, d, z], cr2.at[a, d, z], sib
        )

    for d in (2, 1, 3, 0):
        for a in range(2):
            for z in range(2):
                c = core_copy(a, d, z)
                c.start()
                sends.append(c)

    def add_in(dst, srcs):
        for z in range(2):
            @pl.loop(0, width // 16)
            def _(i):
                r = span(i * 16, 16)
                total = dst[z, r].astype(F32)
                for s in srcs:
                    total = total + s[z][r].astype(F32)
                dst[z, r] = total.astype(BF16)

    def core_sum(a, d):
        for z in range(2):
            core_copy(a, d, z).wait_recv()
        add_in(cbox.at[a, d], [[target(a, z, d, core) for z in range(2)]])

    def ypush(a, src, slot, where):
        c = remote(src, ybuf.at[a, slot], ys2.at[a, slot], yr2.at[a, slot], where)
        c.start()
        sends.append(c)

    def ygot(a, slot):
        remote(ybuf.at[a, slot], ybuf.at[a, slot], ys2.at[a, slot], yr2.at[a, slot], right).wait_recv()

    ahead, behind = (right, left), (left, right)
    nxt, prv = (1, 3), (3, 1)
    for a in range(2):
        core_sum(a, 2)
        ypush(a, cbox.at[a, 2], 0, ahead[a])
    small.step()
    for a in range(2):
        core_sum(a, prv[a])
        ypush(a, cbox.at[a, prv[a]], 1, behind[a])
    for a in range(2):
        core_sum(a, nxt[a])
    small.step()

    fetch.far()
    for a in range(2):
        ygot(a, 0)
        add_in(cbox.at[a, nxt[a]], [[ybuf.at[a, 0, z] for z in range(2)]])
        ypush(a, cbox.at[a, nxt[a]], 2, ahead[a])
    for a in range(2):
        core_sum(a, 0)
    small.step()
    for r in (1, 3, 2):
        zsends[r - 1].wait_recv()
        ring.start(r)
    zcopies = []
    for a in range(2):
        ygot(a, 1)
        ygot(a, 2)

        @pl.loop(0, width // 16)
        def _(i):
            r = span(i * 16, 16)
            for z in range(2):
                ysum[a, z, r] = (
                    cbox[a, 0, z, r].astype(F32)
                    + ybuf[a, 1, z, r].astype(F32)
                    + ybuf[a, 2, z, r].astype(F32)
                )
            ztot[a, r] = ysum[a, 1 - zh, r].astype(BF16)

        c = remote(ztot.at[a], zbox.at[a], zs2.at[a], zr2.at[a], anti)
        c.start()
        zcopies.append(c)
    back = small.step()
    for r in (1, 3, 2):
        ring.forward(r)

    mean_hat = back[:SLOTS] * (1.0 / D)
    mean_cross = back[SLOTS:] * (1.0 / D)
    gain_col = jnp.transpose(jnp.broadcast_to(gain_row, (KEEP, KEEP)))[:width, :1]
    acc = jnp.zeros((width, KEEP), F32)
    backs = [
        Chain(place, out_buf.at[a], out_got.at[a], rt_fwd.at[a], rts.at[a], rtr.at[a]) for a in range(2)
    ]
    for a in range(2):
        zcopies[a].wait()
        results = []
        for j in range(SLOTS):
            here = lanes_of(j)
            total = ysum[a, zh, :, here] + zbox[a, :, here].astype(F32)
            xv = x_loc[:, here].astype(F32)
            if a == 0:
                result = xv + total
            else:
                centred = (xv - mean[j : j + 1]) * inv[j : j + 1]
                acc = acc + total * centred
                result = u_loc[:, here].astype(F32) + inv[j : j + 1] * (
                    total * gain_col - mean_hat[j : j + 1] - centred * mean_cross[j : j + 1]
                )
            out_own[a, :, here] = result.astype(BF16)
            results.append(result)
        for s in range(SPARE):
            total = results[0] * works[0][s]
            for j in range(1, SLOTS):
                total = total + results[j] * works[j][s]
            out_buf[a, :, lanes_of(s)] = total.astype(BF16)
        backs[a].start()
    gain_row = jnp.sum(
        jnp.transpose(jnp.concatenate([acc, jnp.zeros((KEEP - width, KEEP), F32)], axis=0)),
        axis=0, keepdims=True,
    )
    gval[...] = jnp.broadcast_to(gain_row, gval.shape)
    gains = []
    for k in range(3):
        c = remote(gval, gbox.at[k], ggs.at[k], ggr.at[k], {"dp": place.dps[k + 1]})
        c.start()
        gains.append(c)
    backs[0].run()
    fetch.finish()
    quarter = quarters.shape[2]
    for a, arr in enumerate((normed, u_all)):
        quarters[a, 0] = arr[span(place.dp * quarter, quarter)]
    for r in (1, 3, 2):
        ring.finish(r)
    for p in range(3):
        total = dot(quarters[0, 0], dh[0, p * part : (p + 1) * part], 1, 1)
        for r in range(1, 4):
            total = total + dot(quarters[0, r], dh[r, p * part : (p + 1) * part], 1, 1)
        gq_out[p] = total
    total = dot(dh[0, 3 * part :], quarters[1, 0], 1, 1)
    for r in range(1, 4):
        total = total + dot(dh[r, 3 * part :], quarters[1, r], 1, 1)
    go_out[...] = total
    backs[1].run()
    total = gval[...]
    for k, c in enumerate(gains):
        c.wait()
        total = total + gbox[k]
    gain_out[...] = total
    for c in sends + zsends + ring.sends + fetch.sends:
        c.wait_send()


def post_kernel(
    n, counts, k_hbm, own_hbm, buf_hbm, got_hbm, gg_hbm, gq_hbm, go_hbm,
    out, dp_out, gain_out, gq_out, go_out, k_ref, own_ref, buf_ref, got_ref, gg_ref, sem, osem,
):
    through = [
        pltpu.make_async_copy(src, dst, osem.at[i])
        for i, (src, dst) in enumerate(((gq_hbm, gq_out), (go_hbm, go_out)))
    ]
    for c in through:
        c.start()
    load(
        ((k_hbm, k_ref), (own_hbm, own_ref), (buf_hbm, buf_ref), (got_hbm, got_ref), (gg_hbm, gg_ref)), sem
    )
    dp = lax.axis_index("dp")
    share = Share(counts, dp)
    patch = lax.broadcasted_iota(jnp.int32, (dp_out.shape[2], KEEP), 0)
    for i in range(n):
        lanes = slice(i * KEEP, (i + 1) * KEEP)
        if i < SLOTS:
            res, d_in = (own_ref[a, :, lanes].astype(F32) * share.keeps(i) for a in range(2))
        else:
            slot = clamp(share.spare_at + i - SLOTS, SPARE - 1)
            flag = jnp.where(i - SLOTS < share.extra, 1.0, 0.0)
            here = span(slot * KEEP, KEEP)
            res, d_in = (
                (
                    buf_ref[a, :, here].astype(F32)
                    + got_ref[a, 0, :, here].astype(F32)
                    + got_ref[a, 1, :, here].astype(F32)
                )
                * flag
                for a in range(2)
            )
        pick = (patch == k_ref[i : i + 1, :]).astype(F32).astype(BF16)
        out[:, lanes] = res.astype(BF16)
        dp_out[i] = dot(d_in.astype(BF16), pick, 1, 1).astype(BF16)
    part = gain_out.shape[1]
    for g in range(4):
        @pl.when(dp == g)
        def _():
            gain_out[...] = gg_ref[:1, g * part : (g + 1) * part]
    for c in through:
        c.wait()


def sharded(patches, keep_index, counts, gain, w_qkv, w_out, cotangent):
    n, patch_count, width = patches.shape
    total_rows = n * KEEP
    rows = SLOTS * KEEP
    feats = w_qkv.shape[0]
    heads = w_out.shape[0]
    heads3 = 3 * heads
    quarter = feats // 4
    half = (heads3 + heads) // 2
    gain_row = gain[None]
    spare = SPARE * KEEP
    small = 2 * SLOTS + 16
    blk = (2, width, rows)

    def v(shape, dtype=BF16):
        return pltpu.VMEM(shape, dtype)

    scratch = [
        v((width, rows)), v((width, rows)), v((feats, rows)), v((feats, rows)), v((feats, rows)),
        v((3, heads, feats)), v((feats, heads)),
        v((n, width, patch_count)), v((n, KEEP), jnp.int32), v((width, total_rows)), v((1, width), F32),
        v((2, width, spare)), v((2, 2, width, spare)), v((2, 2, width, spare)), v((2, 2, width, spare)),
        v((8, small, KEEP), F32), v((4, small, KEEP), F32),
        v((8, 2 * SLOTS, KEEP), F32), v((4, 2 * SLOTS, KEEP), F32),
        v((heads3, rows)), v((heads, rows)),
        v((heads3 + heads, KEEP)),
        v((6, half, KEEP)), v((6, heads, KEEP)),
        v((feats, rows)), v((feats, rows)), v((2, 4) + blk), v((2, 3) + blk),
        v((2,) + blk, F32), v((2, width, rows)), v((2, width, rows)),
        v((4, heads3 + heads, rows)), v((2, 4, quarter, rows)), v((3, feats, heads)), v((heads, feats)),
        v((3, 8, KEEP), F32), v((8, KEEP), F32),
        DMA((8,)), DMA((8,)), DMA((8,)), DMA((8,)),
        DMA((2,)), DMA((2, 4)), DMA((2, 2)), DMA((2, 8)), DMA((2, 16)),
        DMA((2, 2, CHUNKS)), DMA((2, 2, CHUNKS)), DMA((2, 2, CHUNKS)), DMA((2, 2, CHUNKS)),
        DMA((6,)), DMA((6,)), DMA((6,)), DMA((6,)),
        DMA((2, 4, 2)), DMA((2, 4, 2)), DMA((2, 3)), DMA((2, 3)), DMA((2,)), DMA((2,)),
        DMA((4, 2, 3)), DMA((4, 2, 4)), DMA((4,)), DMA((4,)), DMA((2, 4)), DMA((2, 4)),
        DMA((2, 8)), DMA((2, 8)), DMA((6,)), DMA((3,)), DMA((3,)),
    ]
    shape = jax.ShapeDtypeStruct
    out_own, out_buf, out_got, gq, go, gg = pl.pallas_call(
        main_kernel,
        out_shape=[
            shape((2, width, rows), BF16), shape((2, width, spare), BF16),
            shape((2, 2, width, spare), BF16),
            shape((3, quarter, heads), F32), shape((heads, quarter), F32),
            shape((8, KEEP), F32),
        ],
        in_specs=[SM] + [ANY] * 6,
        out_specs=[VM] * 6,
        scratch_shapes=scratch,
        compiler_params=pltpu.CompilerParams(
            vmem_limit_bytes=58 * 1024 * 1024, collective_id=1, has_side_effects=True
        ),
    )(
        counts, jnp.transpose(patches, (0, 2, 1)), keep_index, cotangent.T, gain_row,
        jnp.transpose(w_qkv, (1, 0, 2)), w_out,
    )
    part = width // 4
    outputs, d_patches, grad_gain, gq, go = pl.pallas_call(
        partial(post_kernel, n),
        out_shape=[
            shape((width, total_rows), BF16), shape((n, width, patch_count), BF16), shape((1, part), F32),
            shape(gq.shape, F32), shape(go.shape, F32),
        ],
        in_specs=[SM] + [ANY] * 7,
        out_specs=[VM] * 3 + [ANY] * 2,
        scratch_shapes=[
            v((n, KEEP), jnp.int32), v((2, width, rows)), v((2, width, spare)), v((2, 2, width, spare)),
            v((8, KEEP), F32), DMA((5,)), DMA((2,)),
        ],
        compiler_params=pltpu.CompilerParams(vmem_limit_bytes=58 * 1024 * 1024),
    )(counts, keep_index, out_own, out_buf, out_got, gg, gq, go)
    return (
        outputs.T, jnp.transpose(d_patches, (0, 2, 1)), jnp.transpose(gq, (1, 0, 2)), go,
        grad_gain.reshape(part),
    )


def solution(mesh):
    placed = (
        P("dp", None, ("mcol", "mrow")),
        P("dp", None),
        P(),
        P(("mcol", "mrow")),
        P("mcol", None, "mrow"),
        P("mrow", "mcol"),
        P("dp", ("mcol", "mrow")),
    )
    return jax.shard_map(
        sharded,
        mesh=mesh,
        in_specs=placed,
        out_specs=(
            P("dp", ("mcol", "mrow")),
            P("dp", None, ("mcol", "mrow")),
            P(("mcol", "dp"), None, "mrow"),
            P("mrow", ("mcol", "dp")),
            P(("mcol", "mrow", "dp")),
        ),
        check_vma=False,
    )
```

```python
import heapq
from functools import partial

import jax
import jax.numpy as jnp
from jax import lax
from jax.experimental import pallas as pl
from jax.experimental.pallas import tpu as pltpu
from jax.sharding import PartitionSpec as P

D = 6144
HD = 128
KEEP = 128
SLOTS = 4
SPARE = 6
CHUNKS = 3
EPSILON = 1e-06

F32 = jnp.float32
BF16 = jnp.bfloat16
MESH = pl.DeviceIdType.MESH
VM = pl.BlockSpec(memory_space=pltpu.VMEM)
SM = pl.BlockSpec(memory_space=pltpu.SMEM)
ANY = pl.BlockSpec(memory_space=pl.ANY)
DMA = pltpu.SemaphoreType.DMA


def dot(a, b, ca, cb):
    return lax.dot_general(a, b, (((ca,), (cb,)), ((), ())), preferred_element_type=F32)


def remote(src, dst, send, recv, where):
    return pltpu.make_async_remote_copy(
        src_ref=src, dst_ref=dst, send_sem=send, recv_sem=recv, device_id=where, device_id_type=MESH
    )


def clamp(value, top):
    return jnp.minimum(jnp.maximum(value, 0), top)


def greet(peers):
    barrier = pltpu.get_barrier_semaphore()
    for peer in peers:
        pl.semaphore_signal(barrier, inc=1, device_id=peer, device_id_type=MESH)
    pl.semaphore_wait(barrier, len(peers))


def span(start, size, step=None):
    return pl.ds(pl.multiple_of(start, step or size), size)


class Event:
    done = False


class Plan:
    def __init__(self):
        self.now, self.count, self.queue, self.parked = 0.0, 0, [], []

    def add(self, flow, delay=0.0):
        self.count += 1
        heapq.heappush(self.queue, (self.now + delay, self.count, flow))

    def run(self):
        while self.queue:
            at, _, flow = heapq.heappop(self.queue)
            self.now = max(self.now, at)
            want = next(flow, None)
            if isinstance(want, tuple):
                self.parked.append((want, flow))
            elif want is not None:
                self.add(flow, want)
            waiting, self.parked = self.parked, []
            for events, other in waiting:
                if all(e.done for e in events):
                    self.add(other)
                else:
                    self.parked.append((events, other))
        assert not self.parked


def load(pairs, sem):
    copies = [pltpu.make_async_copy(src, dst, sem.at[i]) for i, (src, dst) in enumerate(pairs)]
    for c in copies:
        c.start()
    for c in copies:
        c.wait()


class Place:
    def __init__(self):
        self.me = lax.axis_index("mrow")
        self.core = lax.rem(self.me, 2)
        self.y = lax.rem(lax.div(self.me, 2), 4)
        self.zh = lax.div(self.me, 8)
        self.x = lax.axis_index("mcol")
        self.dp = lax.axis_index("dp")
        self.sib = self.at(self.zh, 0, 1 - self.core)
        self.anti = self.at(1 - self.zh, 0, self.core)
        self.ys = [self.at(self.zh, d, self.core) for d in range(4)]
        self.xs = [lax.rem(self.x + d, 4) for d in range(4)]
        self.dps = [lax.rem(self.dp + d, 4) for d in range(4)]

    def at(self, zh, dy, core):
        return zh * 8 + lax.rem(self.y + dy, 4) * 2 + core

    def peers(self):
        rows = [self.sib, self.anti] + self.ys[1:]
        return (
            [{"mrow": r} for r in rows]
            + [{"mcol": c} for c in self.xs[1:]]
            + [{"dp": c} for c in self.dps[1:]]
        )


class Share:
    def __init__(self, counts, dp):
        c = [counts[g] for g in range(4)]
        keep = [jnp.minimum(v, SLOTS) for v in c]
        zero = jnp.int32(0)
        self.own = self.extra = self.spare_at = self.free = self.free_at = zero
        spare_at = free_at = zero
        for g in range(4):
            here = dp == g
            spare, free = c[g] - keep[g], SLOTS - keep[g]
            self.own = jnp.where(here, keep[g], self.own)
            self.extra = jnp.where(here, spare, self.extra)
            self.free = jnp.where(here, free, self.free)
            self.spare_at = jnp.where(here, spare_at, self.spare_at)
            self.free_at = jnp.where(here, free_at, self.free_at)
            spare_at, free_at = spare_at + spare, free_at + free

    def holds(self, slot, image):
        k = image - SLOTS
        return jnp.where((self.spare_at + k == slot) & (k < self.extra), 1.0, 0.0)

    def keeps(self, position):
        return jnp.where(position < self.own, 1.0, 0.0)

    def works(self, position, slot):
        k = position - self.own
        return jnp.where((k >= 0) & (self.free_at + k == slot), 1.0, 0.0)


class SmallSum:
    def __init__(self, place, val, box, send, recv, x_rows):
        self.place, self.val, self.box = place, val, box
        self.send, self.recv, self.x_rows = send, recv, x_rows
        self.live = []
        self.n = 0

    def push(self, peers, rows=None):
        self.live = []
        for where in peers:
            k = self.n
            self.n += 1
            stage = self.val.at[self.stage]
            box = self.box.at[k]
            if rows is not None:
                stage, box = stage.at[:rows], box.at[:rows]
            c = remote(stage, box, self.send.at[k], self.recv.at[k], where)
            c.start()
            self.live.append((k, c))

    def start(self, value):
        self.stage = 0
        self.val[0] = value
        self.push([{"mrow": self.place.sib}])

    def step(self):
        total = self.val[self.stage]
        rows = self.x_rows if self.stage == 3 else total.shape[0]
        total = total[:rows]
        for k, c in self.live:
            c.wait()
            total = total + self.box[k, :rows]
        self.stage += 1
        if self.stage < 4:
            self.val[self.stage] = total
        if self.stage == 1:
            self.push([{"mrow": r} for r in self.place.ys[1:]])
        elif self.stage == 2:
            self.push([{"mrow": self.place.anti}])
        elif self.stage == 3:
            self.push([{"mcol": c} for c in self.place.xs[1:]], self.x_rows)
        return total


class Chain:
    def __init__(self, place, own, got, fwd, send, recv):
        self.dp, self.own, self.got, self.fwd, self.send, self.recv = place.dp, own, got, fwd, send, recv
        self.near = [{"dp": place.dps[1]}, {"dp": place.dps[3]}]
        self.width = own.shape[1] // CHUNKS

    def lanes(self, ch):
        return pl.ds(ch * self.width, self.width)

    def copy(self, way, ch, first):
        src = self.own if first else self.fwd.at[way]
        return remote(
            src.at[:, self.lanes(ch)], self.got.at[way, :, self.lanes(ch)],
            self.send.at[way, ch], self.recv.at[way, ch], self.near[way],
        )

    def forward(self, way, ch):
        self.copy(way, ch, False).wait_recv()
        here = self.lanes(ch)
        self.fwd[way, :, here] = (
            self.got[way, :, here].astype(F32) + self.own[:, here].astype(F32)
        ).astype(BF16)
        self.copy(way, ch, False).start()

    def start(self):
        for dp, way in ((0, 0), (3, 1)):
            @pl.when(self.dp == dp)
            def _():
                for ch in range(CHUNKS):
                    self.copy(way, ch, True).start()
                self.got[way] = jnp.zeros(self.got.shape[1:], BF16)

    def flow(self):
        for way, ch, after in (
            (0, 0, 3.5), (0, 1, 1.0), (1, 0, 2.5), (0, 2, 0.0), (1, 1, 1.0), (1, 2, 1.0)
        ):
            yield after
            for dp, w in ((1, way), (2, 1 - way)):
                @pl.when(self.dp == dp)
                def _():
                    self.forward(w, ch)
        yield 3.5
        for dp, way in ((0, 1), (3, 0)):
            @pl.when(self.dp == dp)
            def _():
                for ch in range(CHUNKS):
                    self.copy(way, ch, False).wait_recv()

    def drain(self):
        for way, last in ((0, 3), (1, 0)):
            @pl.when(self.dp != last)
            def _():
                for ch in range(CHUNKS):
                    self.copy(way, ch, False).wait_send()

    def slot(self, s):
        here = slice(s * KEEP, (s + 1) * KEEP)
        return (
            self.own[:, here].astype(F32)
            + self.got[0, :, here].astype(F32)
            + self.got[1, :, here].astype(F32)
        )


def attend(q, k, v, do):
    def norm(t):
        c = t - jnp.mean(t, axis=0, keepdims=True)
        i = lax.rsqrt(jnp.mean(c * c, axis=0, keepdims=True) + EPSILON)
        return c * i, i

    def norm_back(d, y, i):
        return i * (
            d - jnp.mean(d, axis=0, keepdims=True) - y * jnp.mean(d * y, axis=0, keepdims=True)
        )

    def mm(a, b, ca, cb):
        return lax.dot_general(
            a, b, (((ca,), (cb,)), ((), ())), preferred_element_type=F32, precision=lax.Precision.HIGHEST
        )

    scale = HD ** (-0.5)
    qn, iq = norm(q)
    kn, ik = norm(k)
    w = jnp.exp(mm(kn, qn, 0, 0) * scale)
    w = w / jnp.sum(w, axis=0, keepdims=True)
    out = mm(v, w, 1, 0)
    dw = mm(v, do, 0, 0)
    ds = w * (dw - jnp.sum(w * dw, axis=0, keepdims=True)) * scale
    dv = mm(do, w, 1, 1)
    dq = norm_back(mm(kn, ds, 1, 0), qn, iq)
    dk = norm_back(mm(qn, ds, 1, 1), kn, ik)
    return out, dq, dk, dv


def gather_rows(place, loc, out, send, recv, sends):
    width, rows = loc.shape
    half = rows // 2
    me, sib, core = place.me, {"mrow": place.sib}, place.core
    right, left = {"mrow": place.ys[1]}, {"mrow": place.ys[3]}
    count = [0]

    def view(slot, part=None):
        block = out.at[span(slot * width, width)]
        return block if part is None else block.at[:, pl.ds(part * half, half)]

    def push(slot, where, part=None, src=None):
        k = count[0]
        count[0] += 1
        c = remote(
            view(slot, part) if src is None else src, view(slot, part),
            send.at[k], recv.at[slot, part or 0], where,
        )
        c.start()
        sends.append(c)

    def got(slot, part=None):
        remote(view(slot, part), view(slot, part), send.at[0], recv.at[slot, part or 0], sib).wait_recv()

    push(me, {"mrow": place.anti}, src=loc)
    push(me, right, src=loc)
    push(me, left, src=loc)
    push(me, sib, src=loc)
    out[span(me * width, width)] = loc[...]

    def ring(zh):
        before, after = place.at(zh, 3, core), place.at(zh, 1, core)
        got(before)
        push(before, right, 0)
        got(after)
        push(after, left, 1)
        push(before, sib)
        push(after, sib)

    def far(zh):
        slot = place.at(zh, 2, core)
        got(slot, 0)
        got(slot, 1)
        push(slot, sib)

    yield 4.0
    ring(place.zh)
    yield 3.5
    got(place.anti)
    push(place.anti, right)
    push(place.anti, left)
    push(place.anti, sib)
    yield 0.5
    far(place.zh)
    yield 4.0
    ring(1 - place.zh)
    yield 4.0
    far(1 - place.zh)
    yield 2.0
    for zh in range(2):
        for dy in range(4):
            got(place.at(zh, dy, 1 - core))


class ReduceX:
    def __init__(self, place, src, buf, fwd, send, recv):
        self.place, self.src, self.buf, self.fwd, self.send, self.recv = place, src, buf, fwd, send, recv
        self.half, self.width = buf.shape[1], buf.shape[2]

    def view(self, p, block):
        return self.src.at[pl.ds(p * self.half, self.half), span(block * self.width, self.width)]

    def push(self, src, slot, where, sends):
        c = remote(src, self.buf.at[slot], self.send.at[slot], self.recv.at[slot], where)
        c.start()
        sends.append(c)

    def got(self, slot):
        b = self.buf.at[slot]
        remote(b, b, self.send.at[slot], self.recv.at[slot], {"mcol": self.place.xs[1]}).wait_recv()

    def flow(self, sends):
        xs = self.place.xs
        right, left = {"mcol": xs[1]}, {"mcol": xs[3]}
        self.push(self.view(0, xs[2]), 0, right, sends)
        self.push(self.view(1, xs[2]), 1, left, sends)
        self.push(self.view(0, xs[3]), 2, left, sends)
        self.push(self.view(1, xs[1]), 3, right, sends)
        yield 4.0
        for p, (at, where) in enumerate(((xs[1], right), (xs[3], left))):
            self.got(p)
            self.fwd[p] = (self.buf[p].astype(F32) + self.view(p, at)[...].astype(F32)).astype(BF16)
            self.push(self.fwd.at[p], 4 + p, where, sends)
        yield 4.0
        for slot in range(2, 6):
            self.got(slot)

    def total(self, r0):
        p, r = divmod(r0, self.half)
        here = slice(r, r + HD)
        return (
            self.src[r0 : r0 + HD, span(self.place.x * self.width, self.width)].astype(F32)
            + self.buf[2 + p, here].astype(F32)
            + self.buf[4 + p, here].astype(F32)
        )


class RingX:
    def __init__(self, place, dh, slot, start, rows, send, recv):
        self.x, self.xs, self.view = place.x, place.xs, dh.at[slot, pl.ds(start, rows)]
        self.send, self.recv = send, recv
        self.right, self.left = {"mcol": place.xs[1]}, {"mcol": place.xs[3]}
        self.half, self.width = rows // 2, dh.shape[2] // 4

    def copy(self, p, block, k, where):
        view = self.view.at[pl.ds(p * self.half, self.half), span(block * self.width, self.width)]
        return remote(view, view, self.send.at[p, k], self.recv.at[p, block], where)

    def push(self, p, block, k, where, sends):
        c = self.copy(p, block, k, where)
        c.start()
        sends.append(c)

    def got(self, p, block):
        self.copy(p, block, 0, self.right).wait_recv()

    def flow(self, sends, pace):
        xs = self.xs
        for p in range(2):
            self.push(p, self.x, 0, self.right, sends)
            self.push(p, self.x, 1, self.left, sends)
        yield pace
        self.got(0, xs[3])
        self.push(0, xs[3], 2, self.right, sends)
        self.got(1, xs[1])
        self.push(1, xs[1], 2, self.left, sends)
        yield pace
        self.got(1, xs[3])
        self.got(0, xs[1])
        self.got(0, xs[2])
        self.got(1, xs[2])


class Quarter:
    def __init__(self, place, array, out, zsend, zrecv, send, recv, sends):
        self.place, self.array, self.out = place, array, out
        self.zsend, self.zrecv, self.send, self.recv, self.sends = zsend, zrecv, send, recv, sends
        self.share = out.shape[1] // 8
        self.n = 0

    def index(self, dy, core):
        return lax.rem(self.place.y + dy, 4) * 2 + core

    def view(self, index, part=None):
        rows = span(index * self.share, self.share)
        half = self.out.shape[2] // 2
        return self.out.at[1:4, rows] if part is None else self.out.at[1:4, rows, pl.ds(part * half, half)]

    def zcopy(self, r):
        dp, mine = self.place.dps[r], self.index(0, self.place.core)
        src = self.array.at[span(dp * self.out.shape[1] + mine * self.share, self.share)]
        dst = self.out.at[r, span(mine * self.share, self.share)]
        return remote(src, dst, self.zsend.at[r], self.zrecv.at[r], {"dp": dp})

    def copy(self, index, where, part, k):
        view = self.view(index, part)
        return remote(view, view, self.send.at[k], self.recv.at[index, part or 0], where)

    def push(self, index, where, part=None):
        c = self.copy(index, where, part, self.n)
        self.n += 1
        c.start()
        self.sends.append(c)

    def got(self, index, part=None):
        self.copy(index, {"mrow": self.place.sib}, part, 0).wait_recv()

    def flow(self):
        place, core = self.place, self.place.core
        right, left, sib = {"mrow": place.ys[1]}, {"mrow": place.ys[3]}, {"mrow": place.sib}
        for r in (1, 3, 2):
            self.zcopy(r).start()
        yield 9.0
        mine, before, after, far = (self.index(d, core) for d in (0, 3, 1, 2))
        for r in (1, 3, 2):
            self.zcopy(r).wait()
        for where in (right, left, sib):
            self.push(mine, where)
        yield 7.0
        self.got(before)
        self.push(before, right, 0)
        self.got(after)
        self.push(after, left, 1)
        self.push(before, sib)
        self.push(after, sib)
        yield 6.0
        self.got(far, 0)
        self.got(far, 1)
        self.push(far, sib)
        yield 6.0
        for dy in range(4):
            self.got(self.index(dy, 1 - core))


class ReduceRows:
    def __init__(self, place, array, cbox, ybuf, ysum, ztot, zbox, csem, ysem, zsem, sends):
        self.place, self.array, self.cbox, self.ybuf = place, array, cbox, ybuf
        self.ysum, self.ztot, self.zbox = ysum, ztot, zbox
        self.csem, self.ysem, self.zsem, self.sends = csem, ysem, zsem, sends
        self.width, self.rows = ztot.shape

    def target(self, z, d, c):
        return self.array.at[span(self.place.at(z, d, c) * self.width, self.width)]

    def core_copy(self, d, z):
        return remote(
            self.target(z, d, 1 - self.place.core), self.cbox.at[d, z],
            self.csem[0].at[d, z], self.csem[1].at[d, z], {"mrow": self.place.sib},
        )

    def add(self, d, srcs, lanes=slice(None)):
        for z in range(2):
            @pl.loop(0, self.width // 16)
            def _(i):
                r = span(i * 16, 16)
                total = self.cbox[d, z, r, lanes].astype(F32)
                for s in srcs:
                    total = total + s[z][r, lanes].astype(F32)
                self.cbox[d, z, r, lanes] = total.astype(BF16)

    def core_sum(self, d):
        for z in range(2):
            self.core_copy(d, z).wait_recv()
        self.add(d, [[self.target(z, d, self.place.core) for z in range(2)]])

    def ypush(self, d, slot, lanes, k, where):
        c = remote(
            self.cbox.at[d, :, :, lanes], self.ybuf.at[slot, :, :, lanes],
            self.ysem[0].at[k], self.ysem[1].at[k], where,
        )
        c.start()
        self.sends.append(c)

    def ygot(self, slot, lanes, k):
        b = self.ybuf.at[slot, :, :, lanes]
        remote(b, b, self.ysem[0].at[k], self.ysem[1].at[k], {"mrow": self.place.sib}).wait_recv()

    def flow(self):
        place = self.place
        right, left = {"mrow": place.ys[1]}, {"mrow": place.ys[3]}
        lo, hi = pl.ds(0, self.rows // 2), pl.ds(self.rows // 2, self.rows // 2)
        for d in (2, 1, 3, 0):
            for z in range(2):
                c = self.core_copy(d, z)
                c.start()
                self.sends.append(c)
        yield 2.5
        self.core_sum(2)
        self.ypush(2, 0, lo, 0, right)
        self.ypush(2, 1, hi, 1, left)
        self.core_sum(1)
        self.ypush(1, 2, hi, 3, right)
        self.core_sum(3)
        self.ypush(3, 3, lo, 4, left)
        self.core_sum(0)
        yield 3.0
        self.ygot(0, lo, 0)
        self.add(1, [[self.ybuf.at[0, z] for z in range(2)]], lo)
        self.ypush(1, 2, lo, 2, right)
        self.ygot(1, hi, 1)
        self.add(3, [[self.ybuf.at[1, z] for z in range(2)]], hi)
        self.ypush(3, 3, hi, 5, left)
        yield 4.0
        for slot, lanes, k in ((2, hi, 3), (3, lo, 4), (2, lo, 2), (3, hi, 5)):
            self.ygot(slot, lanes, k)

        @pl.loop(0, self.width // 16)
        def _(i):
            r = span(i * 16, 16)
            for z in range(2):
                self.ysum[z, r] = (
                    self.cbox[0, z, r].astype(F32)
                    + self.ybuf[2, z, r].astype(F32)
                    + self.ybuf[3, z, r].astype(F32)
                )
            self.ztot[r] = self.ysum[1 - place.zh, r].astype(BF16)

        c = remote(self.ztot, self.zbox, self.zsem[0], self.zsem[1], {"mrow": place.anti})
        c.start()
        self.sends.append(c)
        yield 8.0
        c.wait_recv()

    def result(self, lanes):
        return self.ysum[self.place.zh, :, lanes] + self.zbox[:, lanes].astype(F32)


def main_kernel(
    counts, p_hbm, k_hbm, c_hbm, g_hbm, w_hbm, wo_hbm,
    out_own, out_buf, out_got, gq_out, go_out, gain_out,
    x_loc, u_loc, x_all, u_all, normed, wt, wot,
    p_ref, k_ref, c_ref, g_ref, sp_own, sp_got, sp_fwd, rt_fwd,
    box1, val1, box2, val2,
    q_part, m_part, bq, bm, fq, fm,
    a_part, n_part, cbox, ybuf, ysum, ztot, zbox,
    dh, quarters, w_ref, wo_ref, gbox, gval,
    s1s, s1r, s2s, s2r, g1s, g1r,
    sps, spr, rts, rtr,
    sq, sm, rq, rm,
    cs2, cr2, ys2, yr2, zs2, zr2, dxs, dxr, dzs, dzr, qzs, qzr, qys, qyr, wsem, ggs, ggr,
):
    pairs = (
        (p_hbm, p_ref), (k_hbm, k_ref), (c_hbm, c_ref), (g_hbm, g_ref), (w_hbm, w_ref), (wo_hbm, wo_ref)
    )
    loads = [pltpu.make_async_copy(src, dst, wsem.at[i]) for i, (src, dst) in enumerate(pairs)]
    for c in loads:
        c.start()
    place = Place()
    peers = place.peers()
    barrier = pltpu.get_barrier_semaphore()
    for peer in peers:
        pl.semaphore_signal(barrier, inc=1, device_id=peer, device_id_type=MESH)
    width = x_loc.shape[0]
    core, zh = place.core, place.zh
    share = Share(counts, place.dp)
    patch = lax.broadcasted_iota(jnp.int32, (p_ref.shape[2], KEEP), 0)
    for c in loads[:4]:
        c.wait()

    def lanes_of(i):
        return slice(i * KEEP, (i + 1) * KEEP)

    def kept(i):
        pick = (patch == k_ref[i : i + 1, :]).astype(F32).astype(BF16)
        return dot(p_ref[i], pick, 1, 0)

    late = [(kept(i), c_ref[:, lanes_of(i)].astype(F32)) for i in range(SLOTS, 2 * SLOTS)]
    for s in range(SPARE):
        flags = [share.holds(s, i) for i in range(SLOTS, 2 * SLOTS)]
        for a in range(2):
            total = late[0][a] * flags[0]
            for image, flag in zip(late[1:], flags[1:]):
                total = total + image[a] * flag
            sp_own[a, :, lanes_of(s)] = total.astype(BF16)
    pl.semaphore_wait(barrier, len(peers))
    chains = [
        Chain(place, sp_own.at[a], sp_got.at[a], sp_fwd.at[a], sps.at[a], spr.at[a]) for a in range(2)
    ]
    plan = Plan()
    sends = []
    stats_in, q_in, u_in, m_in, heads_in, grads_in, back_in = (Event() for _ in range(7))
    far_in = [Event() for _ in range(5)]
    part = w_ref.shape[2]
    gval[...] = jnp.zeros(gval.shape, F32)
    gval[:1, :width] = g_ref[...]
    gain_row = gval[:1]
    gain_col = jnp.transpose(jnp.broadcast_to(gain_row, (KEEP, KEEP)))[:width, :1]
    keeps = [share.keeps(j) for j in range(SLOTS)]
    works = [[share.works(j, s) for s in range(SPARE)] for j in range(SLOTS)]
    known = {}

    def choose(a, loc, firsts):
        spare = [chains[a].slot(s) for s in range(SPARE)]
        values = []
        for j in range(SLOTS):
            v = firsts[j] * keeps[j]
            for s in range(SPARE):
                v = v + spare[s] * works[j][s]
            loc[:, lanes_of(j)] = v.astype(BF16)
            values.append(v)
        return values

    def small_flow(small, name, event):
        for pace in (2.5, 3.0, 4.5, 3.0):
            yield pace
            known[name] = small.step()
        event.done = True

    def weights_flow():
        for c in loads[4:]:
            c.wait()
        for p in range(3):
            wt[p] = jnp.transpose(w_ref[p])
        wot[...] = jnp.transpose(wo_ref[...])
        yield 0.0

    def rows_flow():
        chains[0].start()
        firsts = [kept(j) for j in range(SLOTS)]
        yield from chains[0].flow()
        values = choose(0, x_loc, firsts)
        me_row = lax.broadcasted_iota(jnp.int32, (16, KEEP), 0) == place.me
        small = SmallSum(place, val1, box1, s1s, s1r, 2 * SLOTS)
        small.start(
            jnp.concatenate(
                [jnp.sum(v, axis=0, keepdims=True) for v in values]
                + [jnp.sum(v * v, axis=0, keepdims=True) for v in values]
                + [jnp.where(me_row, gain_row, 0.0)],
                axis=0,
            )
        )
        plan.add(small_flow(small, "stats", stats_in), 2.5)
        gather = gather_rows(place, x_loc, x_all, g1s.at[0], g1r.at[0], sends)
        pace = next(gather)
        plan.add(weights_flow())
        yield pace
        yield from gather
        yield (stats_in,)
        known["gain_cols"] = gain_cols = jnp.transpose(
            jnp.concatenate([val1[3, 2 * SLOTS :], jnp.zeros((KEEP - 16, KEEP), F32)], axis=0)
        )
        stats = known["stats"]
        known["mean"] = mean = stats[:SLOTS] * (1.0 / D)
        known["inv"] = inv = lax.rsqrt(stats[SLOTS:] * (1.0 / D) - mean * mean + EPSILON)
        for b in range(16):
            rb = slice(b * width, (b + 1) * width)
            col = gain_cols[:width, b : b + 1]
            for j in range(SLOTS):
                here = lanes_of(j)
                centred = (x_all[rb, here].astype(F32) - mean[j : j + 1]) * inv[j : j + 1]
                normed[rb, here] = (centred * col).astype(BF16)
        for p in range(3):
            q_part[p * part : (p + 1) * part] = dot(wt[p], normed[...], 1, 0).astype(BF16)
        yield from q_sum.flow(sends)
        q_in.done = True

    def cotangent_flow():
        chains[1].start()
        firsts = [c_ref[:, lanes_of(j)].astype(F32) for j in range(SLOTS)]
        yield from chains[1].flow()
        choose(1, u_loc, firsts)
        yield from gather_rows(place, u_loc, u_all, g1s.at[1], g1r.at[1], sends)
        u_in.done = True
        m_part[...] = dot(wo_ref[...], u_all[...], 1, 0).astype(BF16)
        yield from m_sum.flow(sends)
        m_in.done = True

    def quarter_flow(a, array):
        yield (u_in, q_in)
        yield from Quarter(
            place, array, quarters.at[a], qzs.at[a], qzr.at[a], qys.at[a], qyr.at[a], sends
        ).flow()
        far_in[3 + a].done = True

    q_sum = ReduceX(place, q_part, bq, fq, sq, rq)
    m_sum = ReduceX(place, m_part, bm, fm, sm, rm)

    def ring_flow(n, slot, start, rows, event, pace):
        yield from RingX(place, dh, slot, start, rows, dxs.at[n], dxr.at[n]).flow(sends, pace)
        event.done = True

    def far_flow(n, r, copy, pace):
        yield pace
        copy.wait_recv()
        yield from ring_flow(1 + r, r, 0, dh.shape[1], far_in[n], 8.0)

    def attend_flow():
        yield (q_in, m_in)
        here = span(place.x * KEEP, KEEP)
        for h in range(part // HD):
            q, k, v, do = [q_sum.total((p * (part // HD) + h) * HD) for p in range(3)] + [m_sum.total(h * HD)]
            out, dq, dk, dv = attend(q, k, v, do)
            for p, value in enumerate((dq, dk, dv, out)):
                r0 = p * part + h * HD
                dh[0, r0 : r0 + HD, here] = value.astype(BF16)
        plan.add(ring_flow(0, 0, 3 * part, part, heads_in, 3.0))
        plan.add(ring_flow(1, 0, 0, 3 * part, grads_in, 4.5))
        copies = [
            remote(dh.at[0, :, here], dh.at[r, :, here], dzs.at[r], dzr.at[r], {"dp": place.dps[r]})
            for r in range(1, 4)
        ]
        yield 0.0
        for n, r in enumerate((1, 3, 2)):
            copies[r - 1].start()
            sends.append(copies[r - 1])
            plan.add(far_flow(n, r, copies[r - 1], (14.0, 16.0, 18.0)[n]))

    feats = normed.shape[0]
    block = 2 * width
    sums = [
        ReduceRows(
            place, array, cbox.at[a], ybuf.at[a], ysum.at[a], ztot.at[a], zbox.at[a],
            (cs2.at[a], cr2.at[a]), (ys2.at[a], yr2.at[a]), (zs2.at[a], zr2.at[a]), sends,
        )
        for a, array in enumerate((a_part, n_part))
    ]
    backs = [
        Chain(place, out_buf.at[a], out_got.at[a], rt_fwd.at[a], rts.at[a], rtr.at[a]) for a in range(2)
    ]

    def give_back(a, results):
        for s in range(SPARE):
            total = results[0] * works[0][s]
            for j in range(1, SLOTS):
                total = total + results[j] * works[j][s]
            out_buf[a, :, lanes_of(s)] = total.astype(BF16)
        backs[a].start()

    def forward_flow():
        yield (heads_in,)
        for b in range(feats // block):
            rb = slice(b * block, (b + 1) * block)
            a_part[rb] = dot(wot[rb], dh[0, 3 * part :], 1, 0).astype(BF16)
        yield from sums[0].flow()
        results = []
        for j in range(SLOTS):
            result = x_loc[:, lanes_of(j)].astype(F32) + sums[0].result(lanes_of(j))
            out_own[0, :, lanes_of(j)] = result.astype(BF16)
            results.append(result)
        give_back(0, results)
        yield from backs[0].flow()

    def backward_flow():
        yield (grads_in,)
        mean, inv, gain_cols = known["mean"], known["inv"], known["gain_cols"]
        hat = [jnp.zeros((8, KEEP), F32) for _ in range(SLOTS)]
        cross = [jnp.zeros((8, KEEP), F32) for _ in range(SLOTS)]
        for b in range(feats // block):
            rb = slice(b * block, (b + 1) * block)
            dn = dot(w_ref[0, rb], dh[0, :part], 1, 0)
            for p in (1, 2):
                dn = dn + dot(w_ref[p, rb], dh[0, p * part : (p + 1) * part], 1, 0)
            n_part[rb] = dn.astype(BF16)
            for i in range(2):
                col = gain_cols[:width, 2 * b + i : 2 * b + i + 1]
                ri = slice(i * width, (i + 1) * width)
                ra = slice((2 * b + i) * width, (2 * b + i + 1) * width)
                for j in range(SLOTS):
                    here = lanes_of(j)
                    d_hat = dn[ri, here] * col
                    centred = (x_all[ra, here].astype(F32) - mean[j : j + 1]) * inv[j : j + 1]
                    hat[j] = hat[j] + jnp.sum(d_hat.reshape(-1, 8, KEEP), axis=0)
                    cross[j] = cross[j] + jnp.sum((d_hat * centred).reshape(-1, 8, KEEP), axis=0)
        small = SmallSum(place, val2, box2, s2s, s2r, 2 * SLOTS)
        small.start(jnp.concatenate([jnp.sum(t, axis=0, keepdims=True) for t in hat + cross], axis=0))
        plan.add(small_flow(small, "back", back_in), 2.5)
        yield from sums[1].flow()
        yield (back_in,)
        back = known["back"]
        mean_hat = back[:SLOTS] * (1.0 / D)
        mean_cross = back[SLOTS:] * (1.0 / D)
        acc = jnp.zeros((width, KEEP), F32)
        results = []
        for j in range(SLOTS):
            here = lanes_of(j)
            total = sums[1].result(here)
            centred = (x_loc[:, here].astype(F32) - mean[j : j + 1]) * inv[j : j + 1]
            acc = acc + total * centred
            result = u_loc[:, here].astype(F32) + inv[j : j + 1] * (
                total * gain_col - mean_hat[j : j + 1] - centred * mean_cross[j : j + 1]
            )
            out_own[1, :, here] = result.astype(BF16)
            results.append(result)
        give_back(1, results)
        row = jnp.sum(
            jnp.transpose(jnp.concatenate([acc, jnp.zeros((KEEP - width, KEEP), F32)], axis=0)),
            axis=0, keepdims=True,
        )
        gval[...] = jnp.broadcast_to(row, gval.shape)
        gains = []
        for k in range(3):
            c = remote(gval, gbox.at[k], ggs.at[k], ggr.at[k], {"dp": place.dps[k + 1]})
            c.start()
            gains.append(c)
        yield from backs[1].flow()
        total = gval[...]
        for k, c in enumerate(gains):
            c.wait()
            total = total + gbox[k]
        gain_out[...] = total

    def weight_gradient_flow():
        yield tuple(far_in) + (heads_in, grads_in)
        quarter = quarters.shape[2]
        for a, arr in enumerate((normed, u_all)):
            quarters[a, 0] = arr[span(place.dp * quarter, quarter)]
        for p in range(3):
            total = dot(quarters[0, 0], dh[0, p * part : (p + 1) * part], 1, 1)
            for r in range(1, 4):
                total = total + dot(quarters[0, r], dh[r, p * part : (p + 1) * part], 1, 1)
            gq_out[p] = total
        total = dot(dh[0, 3 * part :], quarters[1, 0], 1, 1)
        for r in range(1, 4):
            total = total + dot(dh[r, 3 * part :], quarters[1, r], 1, 1)
        go_out[...] = total

    plan.add(rows_flow())
    plan.add(cotangent_flow(), 3.0)
    for a, array in enumerate((normed, u_all)):
        plan.add(quarter_flow(a, array))
    plan.add(attend_flow())
    plan.add(forward_flow())
    plan.add(backward_flow())
    plan.add(weight_gradient_flow())
    plan.run()
    for c in sends:
        c.wait_send()
    for chain in chains + backs:
        chain.drain()


def post_kernel(
    n, counts, k_hbm, own_hbm, buf_hbm, got_hbm, gg_hbm, gq_hbm, go_hbm,
    out, dp_out, gain_out, gq_out, go_out, k_ref, own_ref, buf_ref, got_ref, gg_ref, sem, osem,
):
    through = [
        pltpu.make_async_copy(src, dst, osem.at[i])
        for i, (src, dst) in enumerate(((gq_hbm, gq_out), (go_hbm, go_out)))
    ]
    for c in through:
        c.start()
    load(
        ((k_hbm, k_ref), (own_hbm, own_ref), (buf_hbm, buf_ref), (got_hbm, got_ref), (gg_hbm, gg_ref)), sem
    )
    dp = lax.axis_index("dp")
    share = Share(counts, dp)
    patch = lax.broadcasted_iota(jnp.int32, (dp_out.shape[2], KEEP), 0)
    for i in range(n):
        lanes = slice(i * KEEP, (i + 1) * KEEP)
        if i < SLOTS:
            res, d_in = (own_ref[a, :, lanes].astype(F32) * share.keeps(i) for a in range(2))
        else:
            slot = clamp(share.spare_at + i - SLOTS, SPARE - 1)
            flag = jnp.where(i - SLOTS < share.extra, 1.0, 0.0)
            here = span(slot * KEEP, KEEP)
            res, d_in = (
                (
                    buf_ref[a, :, here].astype(F32)
                    + got_ref[a, 0, :, here].astype(F32)
                    + got_ref[a, 1, :, here].astype(F32)
                )
                * flag
                for a in range(2)
            )
        pick = (patch == k_ref[i : i + 1, :]).astype(F32).astype(BF16)
        out[:, lanes] = res.astype(BF16)
        dp_out[i] = dot(d_in.astype(BF16), pick, 1, 1).astype(BF16)
    part = gain_out.shape[1]
    for g in range(4):
        @pl.when(dp == g)
        def _():
            gain_out[...] = gg_ref[:1, g * part : (g + 1) * part]
    for c in through:
        c.wait()


def sharded(patches, keep_index, counts, gain, w_qkv, w_out, cotangent):
    n, patch_count, width = patches.shape
    total_rows = n * KEEP
    rows = SLOTS * KEEP
    feats = w_qkv.shape[0]
    heads = w_out.shape[0]
    heads3 = 3 * heads
    quarter = feats // 4
    gain_row = gain[None]
    spare = SPARE * KEEP
    small = 2 * SLOTS + 16
    blk = (2, width, rows)

    def v(shape, dtype=BF16):
        return pltpu.VMEM(shape, dtype)

    scratch = [
        v((width, rows)), v((width, rows)), v((feats, rows)), v((feats, rows)), v((feats, rows)),
        v((3, heads, feats)), v((feats, heads)),
        v((n, width, patch_count)), v((n, KEEP), jnp.int32), v((width, total_rows)), v((1, width), F32),
        v((2, width, spare)), v((2, 2, width, spare)), v((2, 2, width, spare)), v((2, 2, width, spare)),
        v((8, small, KEEP), F32), v((4, small, KEEP), F32),
        v((8, 2 * SLOTS, KEEP), F32), v((4, 2 * SLOTS, KEEP), F32),
        v((heads3, rows)), v((heads, rows)),
        v((6, heads3 // 2, KEEP)), v((6, heads // 2, KEEP)), v((2, heads3 // 2, KEEP)), v((2, heads // 2, KEEP)),
        v((feats, rows)), v((feats, rows)), v((2, 4) + blk), v((2, 4) + blk),
        v((2,) + blk, F32), v((2, width, rows)), v((2, width, rows)),
        v((4, heads3 + heads, rows)), v((2, 4, quarter, rows)), v((3, feats, heads)), v((heads, feats)),
        v((3, 8, KEEP), F32), v((8, KEEP), F32),
        DMA((8,)), DMA((8,)), DMA((8,)), DMA((8,)),
        DMA((2, 20)), DMA((2, 16, 2)),
        DMA((2, 2, CHUNKS)), DMA((2, 2, CHUNKS)), DMA((2, 2, CHUNKS)), DMA((2, 2, CHUNKS)),
        DMA((6,)), DMA((6,)), DMA((6,)), DMA((6,)),
        DMA((2, 4, 2)), DMA((2, 4, 2)), DMA((2, 6)), DMA((2, 6)), DMA((2,)), DMA((2,)),
        DMA((5, 2, 3)), DMA((5, 2, 4)), DMA((4,)), DMA((4,)), DMA((2, 4)), DMA((2, 4)),
        DMA((2, 8)), DMA((2, 8, 2)), DMA((6,)), DMA((3,)), DMA((3,)),
    ]
    shape = jax.ShapeDtypeStruct
    out_own, out_buf, out_got, gq, go, gg = pl.pallas_call(
        main_kernel,
        out_shape=[
            shape((2, width, rows), BF16), shape((2, width, spare), BF16),
            shape((2, 2, width, spare), BF16),
            shape((3, quarter, heads), F32), shape((heads, quarter), F32),
            shape((8, KEEP), F32),
        ],
        in_specs=[SM] + [ANY] * 6,
        out_specs=[VM] * 6,
        scratch_shapes=scratch,
        compiler_params=pltpu.CompilerParams(
            vmem_limit_bytes=58 * 1024 * 1024, collective_id=1, has_side_effects=True
        ),
    )(
        counts, jnp.transpose(patches, (0, 2, 1)), keep_index, cotangent.T, gain_row,
        jnp.transpose(w_qkv, (1, 0, 2)), w_out,
    )
    part = width // 4
    outputs, d_patches, grad_gain, gq, go = pl.pallas_call(
        partial(post_kernel, n),
        out_shape=[
            shape((width, total_rows), BF16), shape((n, width, patch_count), BF16), shape((1, part), F32),
            shape(gq.shape, F32), shape(go.shape, F32),
        ],
        in_specs=[SM] + [ANY] * 7,
        out_specs=[VM] * 5,
        scratch_shapes=[
            v((n, KEEP), jnp.int32), v((2, width, rows)), v((2, width, spare)), v((2, 2, width, spare)),
            v((8, KEEP), F32), DMA((5,)), DMA((2,)),
        ],
        compiler_params=pltpu.CompilerParams(vmem_limit_bytes=58 * 1024 * 1024),
    )(counts, keep_index, out_own, out_buf, out_got, gg, gq, go)
    return (
        outputs.T, jnp.transpose(d_patches, (0, 2, 1)), jnp.transpose(gq, (1, 0, 2)), go,
        grad_gain.reshape(part),
    )


def solution(mesh):
    placed = (
        P("dp", None, ("mcol", "mrow")),
        P("dp", None),
        P(),
        P(("mcol", "mrow")),
        P("mcol", None, "mrow"),
        P("mrow", "mcol"),
        P("dp", ("mcol", "mrow")),
    )
    return jax.shard_map(
        sharded,
        mesh=mesh,
        in_specs=placed,
        out_specs=(
            P("dp", ("mcol", "mrow")),
            P("dp", None, ("mcol", "mrow")),
            P(("mcol", "dp"), None, "mrow"),
            P("mrow", ("mcol", "dp")),
            P(("mcol", "mrow", "dp")),
        ),
        check_vma=False,
    )
```

```python
import heapq
from functools import partial

import jax
import jax.numpy as jnp
from jax import lax
from jax.experimental import pallas as pl
from jax.experimental.pallas import tpu as pltpu
from jax.sharding import PartitionSpec as P

D = 6144
HD = 128
KEEP = 128
SLOTS = 4
SPARE = 6
CHUNKS = 2
DIRECT = (True, False)
EPSILON = 1e-06

F32 = jnp.float32
BF16 = jnp.bfloat16
MESH = pl.DeviceIdType.MESH
VM = pl.BlockSpec(memory_space=pltpu.VMEM)
SM = pl.BlockSpec(memory_space=pltpu.SMEM)
ANY = pl.BlockSpec(memory_space=pl.ANY)
DMA = pltpu.SemaphoreType.DMA


def dot(a, b, ca, cb):
    return lax.dot_general(a, b, (((ca,), (cb,)), ((), ())), preferred_element_type=F32)


def remote(src, dst, send, recv, where):
    return pltpu.make_async_remote_copy(
        src_ref=src, dst_ref=dst, send_sem=send, recv_sem=recv, device_id=where, device_id_type=MESH
    )


def clamp(value, top):
    return jnp.minimum(jnp.maximum(value, 0), top)


def greet(peers):
    barrier = pltpu.get_barrier_semaphore()
    for peer in peers:
        pl.semaphore_signal(barrier, inc=1, device_id=peer, device_id_type=MESH)
    pl.semaphore_wait(barrier, len(peers))


def span(start, size, step=None):
    return pl.ds(pl.multiple_of(start, step or size), size)


class Event:
    done = False


class Plan:
    def __init__(self):
        self.now, self.count, self.queue, self.parked = 0.0, 0, [], []

    def add(self, flow, delay=0.0):
        self.count += 1
        heapq.heappush(self.queue, (self.now + delay, self.count, flow))

    def run(self):
        while self.queue:
            at, _, flow = heapq.heappop(self.queue)
            self.now = max(self.now, at)
            want = next(flow, None)
            if isinstance(want, tuple):
                self.parked.append((want, flow))
            elif want is not None:
                self.add(flow, want)
            waiting, self.parked = self.parked, []
            for events, other in waiting:
                if all(e.done for e in events):
                    self.add(other)
                else:
                    self.parked.append((events, other))
        assert not self.parked


def load(pairs, sem):
    copies = [pltpu.make_async_copy(src, dst, sem.at[i]) for i, (src, dst) in enumerate(pairs)]
    for c in copies:
        c.start()
    for c in copies:
        c.wait()


class Place:
    def __init__(self):
        self.me = lax.axis_index("mrow")
        self.core = lax.rem(self.me, 2)
        self.y = lax.rem(lax.div(self.me, 2), 4)
        self.zh = lax.div(self.me, 8)
        self.x = lax.axis_index("mcol")
        self.dp = lax.axis_index("dp")
        self.sib = self.at(self.zh, 0, 1 - self.core)
        self.anti = self.at(1 - self.zh, 0, self.core)
        self.ys = [self.at(self.zh, d, self.core) for d in range(4)]
        self.xs = [lax.rem(self.x + d, 4) for d in range(4)]
        self.dps = [lax.rem(self.dp + d, 4) for d in range(4)]

    def at(self, zh, dy, core):
        return zh * 8 + lax.rem(self.y + dy, 4) * 2 + core

    def peers(self):
        rows = [self.sib, self.anti] + self.ys[1:]
        return (
            [{"mrow": r} for r in rows]
            + [{"mcol": c} for c in self.xs[1:]]
            + [{"dp": c} for c in self.dps[1:]]
        )


class Share:
    def __init__(self, counts, dp):
        c = [counts[g] for g in range(4)]
        keep = [jnp.minimum(v, SLOTS) for v in c]
        zero = jnp.int32(0)
        self.own = self.extra = self.spare_at = self.free = self.free_at = zero
        spare_at = free_at = zero
        for g in range(4):
            here = dp == g
            spare, free = c[g] - keep[g], SLOTS - keep[g]
            self.own = jnp.where(here, keep[g], self.own)
            self.extra = jnp.where(here, spare, self.extra)
            self.free = jnp.where(here, free, self.free)
            self.spare_at = jnp.where(here, spare_at, self.spare_at)
            self.free_at = jnp.where(here, free_at, self.free_at)
            spare_at, free_at = spare_at + spare, free_at + free

    def holds(self, slot, image):
        k = image - SLOTS
        return jnp.where((self.spare_at + k == slot) & (k < self.extra), 1.0, 0.0)

    def keeps(self, position):
        return jnp.where(position < self.own, 1.0, 0.0)

    def works(self, position, slot):
        k = position - self.own
        return jnp.where((k >= 0) & (self.free_at + k == slot), 1.0, 0.0)


class SmallSum:
    def __init__(self, place, val, box, send, recv, x_rows):
        self.place, self.val, self.box = place, val, box
        self.send, self.recv, self.x_rows = send, recv, x_rows
        self.live = []
        self.n = 0

    def push(self, peers, rows=None):
        self.live = []
        for where in peers:
            k = self.n
            self.n += 1
            stage = self.val.at[self.stage]
            box = self.box.at[k]
            if rows is not None:
                stage, box = stage.at[:rows], box.at[:rows]
            c = remote(stage, box, self.send.at[k], self.recv.at[k], where)
            c.start()
            self.live.append((k, c))

    def start(self, value):
        self.stage = 0
        self.val[0] = value
        self.push([{"mrow": self.place.sib}])

    def step(self):
        total = self.val[self.stage]
        rows = self.x_rows if self.stage == 3 else total.shape[0]
        total = total[:rows]
        for k, c in self.live:
            c.wait()
            total = total + self.box[k, :rows]
        self.stage += 1
        if self.stage < 4:
            self.val[self.stage] = total
        if self.stage == 1:
            self.push([{"mrow": r} for r in self.place.ys[1:]])
        elif self.stage == 2:
            self.push([{"mrow": self.place.anti}])
        elif self.stage == 3:
            self.push([{"mcol": c} for c in self.place.xs[1:]], self.x_rows)
        return total


class Chain:
    def __init__(self, place, own, got, fwd, send, recv):
        self.dp, self.own, self.got, self.fwd, self.send, self.recv = place.dp, own, got, fwd, send, recv
        self.near = [{"dp": place.dps[1]}, {"dp": place.dps[3]}]
        self.width = own.shape[1] // CHUNKS

    def lanes(self, ch):
        return pl.ds(ch * self.width, self.width)

    def copy(self, way, ch, first):
        src = self.own if first else self.fwd.at[way]
        return remote(
            src.at[:, self.lanes(ch)], self.got.at[way, :, self.lanes(ch)],
            self.send.at[way, ch], self.recv.at[way, ch], self.near[way],
        )

    def forward(self, way, ch):
        self.copy(way, ch, False).wait_recv()
        here = self.lanes(ch)
        self.fwd[way, :, here] = (
            self.got[way, :, here].astype(F32) + self.own[:, here].astype(F32)
        ).astype(BF16)
        self.copy(way, ch, False).start()

    def start(self):
        for dp, way in ((0, 0), (3, 1)):
            @pl.when(self.dp == dp)
            def _():
                for ch in range(CHUNKS):
                    self.copy(way, ch, True).start()
                self.got[way] = jnp.zeros(self.got.shape[1:], BF16)

    def flow(self):
        for way, ch, after in (
            (0, 0, 3.5), (0, 1, 1.0), (1, 0, 2.5), (1, 1, 1.5)
        ):
            yield after
            for dp, w in ((1, way), (2, 1 - way)):
                @pl.when(self.dp == dp)
                def _():
                    self.forward(w, ch)
        yield 3.5
        for dp, way in ((0, 1), (3, 0)):
            @pl.when(self.dp == dp)
            def _():
                for ch in range(CHUNKS):
                    self.copy(way, ch, False).wait_recv()

    def drain(self):
        for way, last in ((0, 3), (1, 0)):
            @pl.when(self.dp != last)
            def _():
                for ch in range(CHUNKS):
                    self.copy(way, ch, False).wait_send()

    def slot(self, s):
        here = slice(s * KEEP, (s + 1) * KEEP)
        return (
            self.own[:, here].astype(F32)
            + self.got[0, :, here].astype(F32)
            + self.got[1, :, here].astype(F32)
        )


def attend(q, k, v, do):
    def norm(t):
        c = t - jnp.mean(t, axis=0, keepdims=True)
        i = lax.rsqrt(jnp.mean(c * c, axis=0, keepdims=True) + EPSILON)
        return c * i, i

    def norm_back(d, y, i):
        return i * (
            d - jnp.mean(d, axis=0, keepdims=True) - y * jnp.mean(d * y, axis=0, keepdims=True)
        )

    def mm(a, b, ca, cb):
        return lax.dot_general(
            a, b, (((ca,), (cb,)), ((), ())), preferred_element_type=F32, precision=lax.Precision.HIGHEST
        )

    scale = HD ** (-0.5)
    qn, iq = norm(q)
    kn, ik = norm(k)
    w = jnp.exp(mm(kn, qn, 0, 0) * scale)
    w = w / jnp.sum(w, axis=0, keepdims=True)
    out = mm(v, w, 1, 0)
    dw = mm(v, do, 0, 0)
    ds = w * (dw - jnp.sum(w * dw, axis=0, keepdims=True)) * scale
    dv = mm(do, w, 1, 1)
    dq = norm_back(mm(kn, ds, 1, 0), qn, iq)
    dk = norm_back(mm(qn, ds, 1, 1), kn, ik)
    return out, dq, dk, dv


def gather_rows(place, loc, out, send, recv, sends, direct):
    width, rows = loc.shape
    half = rows // 2
    me, sib, core = place.me, {"mrow": place.sib}, place.core
    right, left, across = ({"mrow": place.ys[d]} for d in (1, 3, 2))
    count = [0]

    def view(slot, part=None):
        block = out.at[span(slot * width, width)]
        return block if part is None else block.at[:, pl.ds(part * half, half)]

    def push(slot, where, part=None, src=None):
        k = count[0]
        count[0] += 1
        c = remote(
            view(slot, part) if src is None else src, view(slot, part),
            send.at[k], recv.at[slot, part or 0], where,
        )
        c.start()
        sends.append(c)

    def got(slot, part=None):
        remote(view(slot, part), view(slot, part), send.at[0], recv.at[slot, part or 0], sib).wait_recv()

    push(me, {"mrow": place.anti}, src=loc)
    push(me, right, src=loc)
    push(me, left, src=loc)
    if direct:
        push(me, across, src=loc)
    push(me, sib, src=loc)
    out[span(me * width, width)] = loc[...]

    def ring(zh):
        before, after = place.at(zh, 3, core), place.at(zh, 1, core)
        got(before)
        if not direct:
            push(before, right, 0)
        got(after)
        if not direct:
            push(after, left, 1)
        push(before, sib)
        push(after, sib)

    def far(zh):
        slot = place.at(zh, 2, core)
        if direct:
            got(slot)
        else:
            got(slot, 0)
            got(slot, 1)
        push(slot, sib)

    yield 4.0
    ring(place.zh)
    yield 3.5
    got(place.anti)
    push(place.anti, right)
    push(place.anti, left)
    if direct:
        push(place.anti, across)
    push(place.anti, sib)
    yield 0.5
    far(place.zh)
    yield 4.0
    ring(1 - place.zh)
    yield 1.5 if direct else 4.0
    far(1 - place.zh)
    yield 2.0
    for zh in range(2):
        for dy in range(4):
            got(place.at(zh, dy, 1 - core))


class ReduceX:
    def __init__(self, place, src, buf, fwd, send, recv):
        self.place, self.src, self.buf, self.fwd, self.send, self.recv = place, src, buf, fwd, send, recv
        self.half, self.width = buf.shape[1], buf.shape[2]

    def view(self, p, block):
        return self.src.at[pl.ds(p * self.half, self.half), span(block * self.width, self.width)]

    def push(self, src, slot, where, sends):
        c = remote(src, self.buf.at[slot], self.send.at[slot], self.recv.at[slot], where)
        c.start()
        sends.append(c)

    def got(self, slot):
        b = self.buf.at[slot]
        remote(b, b, self.send.at[slot], self.recv.at[slot], {"mcol": self.place.xs[1]}).wait_recv()

    def flow(self, sends):
        xs = self.place.xs
        right, left = {"mcol": xs[1]}, {"mcol": xs[3]}
        self.push(self.view(0, xs[2]), 0, right, sends)
        self.push(self.view(1, xs[2]), 1, left, sends)
        self.push(self.view(0, xs[3]), 2, left, sends)
        self.push(self.view(1, xs[1]), 3, right, sends)
        yield 4.0
        for p, (at, where) in enumerate(((xs[1], right), (xs[3], left))):
            self.got(p)
            self.fwd[p] = (self.buf[p].astype(F32) + self.view(p, at)[...].astype(F32)).astype(BF16)
            self.push(self.fwd.at[p], 4 + p, where, sends)
        yield 4.0
        for slot in range(2, 6):
            self.got(slot)

    def total(self, r0):
        p, r = divmod(r0, self.half)
        here = slice(r, r + HD)
        return (
            self.src[r0 : r0 + HD, span(self.place.x * self.width, self.width)].astype(F32)
            + self.buf[2 + p, here].astype(F32)
            + self.buf[4 + p, here].astype(F32)
        )


class RingX:
    def __init__(self, place, dh, slot, start, rows, send, recv):
        self.x, self.xs, self.view = place.x, place.xs, dh.at[slot, pl.ds(start, rows)]
        self.send, self.recv = send, recv
        self.right, self.left = {"mcol": place.xs[1]}, {"mcol": place.xs[3]}
        self.half, self.width = rows // 2, dh.shape[2] // 4

    def copy(self, p, block, k, where):
        view = self.view.at[pl.ds(p * self.half, self.half), span(block * self.width, self.width)]
        return remote(view, view, self.send.at[p, k], self.recv.at[p, block], where)

    def push(self, p, block, k, where, sends):
        c = self.copy(p, block, k, where)
        c.start()
        sends.append(c)

    def got(self, p, block):
        self.copy(p, block, 0, self.right).wait_recv()

    def flow(self, sends, pace):
        xs = self.xs
        for p in range(2):
            self.push(p, self.x, 0, self.right, sends)
            self.push(p, self.x, 1, self.left, sends)
        yield pace
        self.got(0, xs[3])
        self.push(0, xs[3], 2, self.right, sends)
        self.got(1, xs[1])
        self.push(1, xs[1], 2, self.left, sends)
        yield pace
        self.got(1, xs[3])
        self.got(0, xs[1])
        self.got(0, xs[2])
        self.got(1, xs[2])


class Quarter:
    def __init__(self, place, array, out, zsend, zrecv, send, recv, sends):
        self.place, self.array, self.out = place, array, out
        self.zsend, self.zrecv, self.send, self.recv, self.sends = zsend, zrecv, send, recv, sends
        self.share = out.shape[1] // 8
        self.n = 0

    def index(self, dy, core):
        return lax.rem(self.place.y + dy, 4) * 2 + core

    def view(self, index, part=None):
        rows = span(index * self.share, self.share)
        half = self.out.shape[2] // 2
        return self.out.at[1:4, rows] if part is None else self.out.at[1:4, rows, pl.ds(part * half, half)]

    def zcopy(self, r):
        dp, mine = self.place.dps[r], self.index(0, self.place.core)
        src = self.array.at[span(dp * self.out.shape[1] + mine * self.share, self.share)]
        dst = self.out.at[r, span(mine * self.share, self.share)]
        return remote(src, dst, self.zsend.at[r], self.zrecv.at[r], {"dp": dp})

    def copy(self, index, where, part, k):
        view = self.view(index, part)
        return remote(view, view, self.send.at[k], self.recv.at[index, part or 0], where)

    def push(self, index, where, part=None):
        c = self.copy(index, where, part, self.n)
        self.n += 1
        c.start()
        self.sends.append(c)

    def got(self, index, part=None):
        self.copy(index, {"mrow": self.place.sib}, part, 0).wait_recv()

    def flow(self):
        place, core = self.place, self.place.core
        right, left, sib = {"mrow": place.ys[1]}, {"mrow": place.ys[3]}, {"mrow": place.sib}
        for r in (1, 3, 2):
            self.zcopy(r).start()
        yield 9.0
        mine, before, after, far = (self.index(d, core) for d in (0, 3, 1, 2))
        for r in (1, 3, 2):
            self.zcopy(r).wait()
        for where in (right, left, sib):
            self.push(mine, where)
        yield 7.0
        self.got(before)
        self.push(before, right, 0)
        self.got(after)
        self.push(after, left, 1)
        self.push(before, sib)
        self.push(after, sib)
        yield 6.0
        self.got(far, 0)
        self.got(far, 1)
        self.push(far, sib)
        yield 6.0
        for dy in range(4):
            self.got(self.index(dy, 1 - core))


class ReduceRows:
    def __init__(self, place, array, cbox, ybuf, ysum, ztot, zbox, csem, ysem, zsem, sends):
        self.place, self.array, self.cbox, self.ybuf = place, array, cbox, ybuf
        self.ysum, self.ztot, self.zbox = ysum, ztot, zbox
        self.csem, self.ysem, self.zsem, self.sends = csem, ysem, zsem, sends
        self.width, self.rows = ztot.shape

    def target(self, z, d, c):
        return self.array.at[span(self.place.at(z, d, c) * self.width, self.width)]

    def core_copy(self, d, z):
        return remote(
            self.target(z, d, 1 - self.place.core), self.cbox.at[d, z],
            self.csem[0].at[d, z], self.csem[1].at[d, z], {"mrow": self.place.sib},
        )

    def add(self, d, srcs, lanes=slice(None)):
        for z in range(2):
            @pl.loop(0, self.width // 16)
            def _(i):
                r = span(i * 16, 16)
                total = self.cbox[d, z, r, lanes].astype(F32)
                for s in srcs:
                    total = total + s[z][r, lanes].astype(F32)
                self.cbox[d, z, r, lanes] = total.astype(BF16)

    def core_sum(self, d):
        for z in range(2):
            self.core_copy(d, z).wait_recv()
        self.add(d, [[self.target(z, d, self.place.core) for z in range(2)]])

    def ypush(self, d, slot, lanes, k, where):
        c = remote(
            self.cbox.at[d, :, :, lanes], self.ybuf.at[slot, :, :, lanes],
            self.ysem[0].at[k], self.ysem[1].at[k], where,
        )
        c.start()
        self.sends.append(c)

    def ygot(self, slot, lanes, k):
        b = self.ybuf.at[slot, :, :, lanes]
        remote(b, b, self.ysem[0].at[k], self.ysem[1].at[k], {"mrow": self.place.sib}).wait_recv()

    def flow(self):
        place = self.place
        right, left = {"mrow": place.ys[1]}, {"mrow": place.ys[3]}
        lo, hi = pl.ds(0, self.rows // 2), pl.ds(self.rows // 2, self.rows // 2)
        for d in (2, 1, 3, 0):
            for z in range(2):
                c = self.core_copy(d, z)
                c.start()
                self.sends.append(c)
        yield 2.5
        self.core_sum(2)
        self.ypush(2, 0, lo, 0, right)
        self.ypush(2, 1, hi, 1, left)
        self.core_sum(1)
        self.ypush(1, 2, hi, 3, right)
        self.core_sum(3)
        self.ypush(3, 3, lo, 4, left)
        self.core_sum(0)
        yield 3.0
        self.ygot(0, lo, 0)
        self.add(1, [[self.ybuf.at[0, z] for z in range(2)]], lo)
        self.ypush(1, 2, lo, 2, right)
        self.ygot(1, hi, 1)
        self.add(3, [[self.ybuf.at[1, z] for z in range(2)]], hi)
        self.ypush(3, 3, hi, 5, left)
        yield 4.0
        for slot, lanes, k in ((2, hi, 3), (3, lo, 4), (2, lo, 2), (3, hi, 5)):
            self.ygot(slot, lanes, k)

        @pl.loop(0, self.width // 16)
        def _(i):
            r = span(i * 16, 16)
            for z in range(2):
                self.ysum[z, r] = (
                    self.cbox[0, z, r].astype(F32)
                    + self.ybuf[2, z, r].astype(F32)
                    + self.ybuf[3, z, r].astype(F32)
                )
            self.ztot[r] = self.ysum[1 - place.zh, r].astype(BF16)

        c = remote(self.ztot, self.zbox, self.zsem[0], self.zsem[1], {"mrow": place.anti})
        c.start()
        self.sends.append(c)
        yield 8.0
        c.wait_recv()

    def result(self, lanes):
        return self.ysum[self.place.zh, :, lanes] + self.zbox[:, lanes].astype(F32)


def main_kernel(
    counts, p_hbm, k_hbm, c_hbm, g_hbm, w_hbm, wo_hbm,
    out_own, out_buf, out_got, gq_out, go_out, gain_out,
    x_loc, u_loc, x_all, u_all, normed, wt, wot,
    p_ref, k_ref, c_ref, g_ref, sp_own, sp_got, sp_fwd, rt_fwd,
    box1, val1, box2, val2,
    q_part, m_part, bq, bm, fq, fm,
    a_part, n_part, cbox, ybuf, ysum, ztot, zbox,
    dh, quarters, w_ref, wo_ref, gbox, gval,
    s1s, s1r, s2s, s2r, g1s, g1r,
    sps, spr, rts, rtr,
    sq, sm, rq, rm,
    cs2, cr2, ys2, yr2, zs2, zr2, dxs, dxr, dzs, dzr, qzs, qzr, qys, qyr, wsem, ggs, ggr,
):
    pairs = (
        (p_hbm, p_ref), (k_hbm, k_ref), (c_hbm, c_ref), (g_hbm, g_ref), (w_hbm, w_ref), (wo_hbm, wo_ref)
    )
    loads = [pltpu.make_async_copy(src, dst, wsem.at[i]) for i, (src, dst) in enumerate(pairs)]
    for c in loads:
        c.start()
    place = Place()
    peers = place.peers()
    barrier = pltpu.get_barrier_semaphore()
    for peer in peers:
        pl.semaphore_signal(barrier, inc=1, device_id=peer, device_id_type=MESH)
    width = x_loc.shape[0]
    core, zh = place.core, place.zh
    share = Share(counts, place.dp)
    patch = lax.broadcasted_iota(jnp.int32, (p_ref.shape[2], KEEP), 0)
    for c in loads[:4]:
        c.wait()

    def lanes_of(i):
        return slice(i * KEEP, (i + 1) * KEEP)

    def kept(i):
        pick = (patch == k_ref[i : i + 1, :]).astype(F32).astype(BF16)
        return dot(p_ref[i], pick, 1, 0)

    late = [(kept(i), c_ref[:, lanes_of(i)].astype(F32)) for i in range(SLOTS, 2 * SLOTS)]
    for s in range(SPARE):
        flags = [share.holds(s, i) for i in range(SLOTS, 2 * SLOTS)]
        for a in range(2):
            total = late[0][a] * flags[0]
            for image, flag in zip(late[1:], flags[1:]):
                total = total + image[a] * flag
            sp_own[a, :, lanes_of(s)] = total.astype(BF16)
    pl.semaphore_wait(barrier, len(peers))
    chains = [
        Chain(place, sp_own.at[a], sp_got.at[a], sp_fwd.at[a], sps.at[a], spr.at[a]) for a in range(2)
    ]
    plan = Plan()
    sends = []
    stats_in, q_in, u_in, m_in, heads_in, grads_in, back_in = (Event() for _ in range(7))
    normed_in = Event()
    far_in = [Event() for _ in range(5)]
    part = w_ref.shape[2]
    gval[...] = jnp.zeros(gval.shape, F32)
    gval[:1, :width] = g_ref[...]
    gain_row = gval[:1]
    gain_col = jnp.transpose(jnp.broadcast_to(gain_row, (KEEP, KEEP)))[:width, :1]
    keeps = [share.keeps(j) for j in range(SLOTS)]
    works = [[share.works(j, s) for s in range(SPARE)] for j in range(SLOTS)]
    known = {}

    def choose(a, loc, firsts):
        spare = [chains[a].slot(s) for s in range(SPARE)]
        values = []
        for j in range(SLOTS):
            v = firsts[j] * keeps[j]
            for s in range(SPARE):
                v = v + spare[s] * works[j][s]
            loc[:, lanes_of(j)] = v.astype(BF16)
            values.append(v)
        return values

    def small_flow(small, name, event):
        for pace in (2.5, 3.0, 4.5, 3.0):
            yield pace
            known[name] = small.step()
        event.done = True

    def weights_flow():
        for c in loads[4:]:
            c.wait()
        for p in range(3):
            wt[p] = jnp.transpose(w_ref[p])
        wot[...] = jnp.transpose(wo_ref[...])
        yield 0.0

    def rows_flow():
        chains[0].start()
        firsts = [kept(j) for j in range(SLOTS)]
        yield from chains[0].flow()
        values = choose(0, x_loc, firsts)
        me_row = lax.broadcasted_iota(jnp.int32, (16, KEEP), 0) == place.me
        small = SmallSum(place, val1, box1, s1s, s1r, 2 * SLOTS)
        small.start(
            jnp.concatenate(
                [jnp.sum(v, axis=0, keepdims=True) for v in values]
                + [jnp.sum(v * v, axis=0, keepdims=True) for v in values]
                + [jnp.where(me_row, gain_row, 0.0)],
                axis=0,
            )
        )
        plan.add(small_flow(small, "stats", stats_in), 2.5)
        gather = gather_rows(place, x_loc, x_all, g1s.at[0], g1r.at[0], sends, DIRECT[0])
        pace = next(gather)
        plan.add(weights_flow())
        yield pace
        yield from gather
        yield (stats_in,)
        known["gain_cols"] = gain_cols = jnp.transpose(
            jnp.concatenate([val1[3, 2 * SLOTS :], jnp.zeros((KEEP - 16, KEEP), F32)], axis=0)
        )
        stats = known["stats"]
        known["mean"] = mean = stats[:SLOTS] * (1.0 / D)
        known["inv"] = inv = lax.rsqrt(stats[SLOTS:] * (1.0 / D) - mean * mean + EPSILON)
        for b in range(16):
            rb = slice(b * width, (b + 1) * width)
            col = gain_cols[:width, b : b + 1]
            for j in range(SLOTS):
                here = lanes_of(j)
                centred = (x_all[rb, here].astype(F32) - mean[j : j + 1]) * inv[j : j + 1]
                normed[rb, here] = (centred * col).astype(BF16)
        normed_in.done = True
        for p in range(3):
            q_part[p * part : (p + 1) * part] = dot(wt[p], normed[...], 1, 0).astype(BF16)
        yield from q_sum.flow(sends)
        q_in.done = True

    def cotangent_flow():
        chains[1].start()
        firsts = [c_ref[:, lanes_of(j)].astype(F32) for j in range(SLOTS)]
        yield from chains[1].flow()
        choose(1, u_loc, firsts)
        yield from gather_rows(place, u_loc, u_all, g1s.at[1], g1r.at[1], sends, DIRECT[1])
        u_in.done = True
        m_part[...] = dot(wo_ref[...], u_all[...], 1, 0).astype(BF16)
        yield from m_sum.flow(sends)
        m_in.done = True

    def quarter_flow(a, array):
        yield ((normed_in, u_in)[a],)
        yield from Quarter(
            place, array, quarters.at[a], qzs.at[a], qzr.at[a], qys.at[a], qyr.at[a], sends
        ).flow()
        far_in[3 + a].done = True

    q_sum = ReduceX(place, q_part, bq, fq, sq, rq)
    m_sum = ReduceX(place, m_part, bm, fm, sm, rm)

    def ring_flow(n, slot, start, rows, event, pace):
        yield from RingX(place, dh, slot, start, rows, dxs.at[n], dxr.at[n]).flow(sends, pace)
        event.done = True

    def far_flow(n, r, copy, pace):
        yield pace
        copy.wait_recv()
        yield from ring_flow(1 + r, r, 0, dh.shape[1], far_in[n], 8.0)

    def attend_flow():
        yield (q_in, m_in)
        here = span(place.x * KEEP, KEEP)
        for h in range(part // HD):
            q, k, v, do = [q_sum.total((p * (part // HD) + h) * HD) for p in range(3)] + [m_sum.total(h * HD)]
            out, dq, dk, dv = attend(q, k, v, do)
            for p, value in enumerate((dq, dk, dv, out)):
                r0 = p * part + h * HD
                dh[0, r0 : r0 + HD, here] = value.astype(BF16)
        plan.add(ring_flow(0, 0, 3 * part, part, heads_in, 3.0))
        plan.add(ring_flow(1, 0, 0, 3 * part, grads_in, 4.5))
        copies = [
            remote(dh.at[0, :, here], dh.at[r, :, here], dzs.at[r], dzr.at[r], {"dp": place.dps[r]})
            for r in range(1, 4)
        ]
        yield 0.0
        for n, r in enumerate((1, 3, 2)):
            copies[r - 1].start()
            sends.append(copies[r - 1])
            plan.add(far_flow(n, r, copies[r - 1], (14.0, 16.0, 18.0)[n]))

    feats = normed.shape[0]
    block = 2 * width
    sums = [
        ReduceRows(
            place, array, cbox.at[a], ybuf.at[a], ysum.at[a], ztot.at[a], zbox.at[a],
            (cs2.at[a], cr2.at[a]), (ys2.at[a], yr2.at[a]), (zs2.at[a], zr2.at[a]), sends,
        )
        for a, array in enumerate((a_part, n_part))
    ]
    backs = [
        Chain(place, out_buf.at[a], out_got.at[a], rt_fwd.at[a], rts.at[a], rtr.at[a]) for a in range(2)
    ]

    def give_back(a, results):
        for s in range(SPARE):
            total = results[0] * works[0][s]
            for j in range(1, SLOTS):
                total = total + results[j] * works[j][s]
            out_buf[a, :, lanes_of(s)] = total.astype(BF16)
        backs[a].start()

    def forward_flow():
        yield (heads_in,)
        for b in range(feats // block):
            rb = slice(b * block, (b + 1) * block)
            a_part[rb] = dot(wot[rb], dh[0, 3 * part :], 1, 0).astype(BF16)
        yield from sums[0].flow()
        results = []
        for j in range(SLOTS):
            result = x_loc[:, lanes_of(j)].astype(F32) + sums[0].result(lanes_of(j))
            out_own[0, :, lanes_of(j)] = result.astype(BF16)
            results.append(result)
        give_back(0, results)
        yield from backs[0].flow()

    def backward_flow():
        yield (grads_in,)
        mean, inv, gain_cols = known["mean"], known["inv"], known["gain_cols"]
        hat = [jnp.zeros((8, KEEP), F32) for _ in range(SLOTS)]
        cross = [jnp.zeros((8, KEEP), F32) for _ in range(SLOTS)]
        for b in range(feats // block):
            rb = slice(b * block, (b + 1) * block)
            dn = dot(w_ref[0, rb], dh[0, :part], 1, 0)
            for p in (1, 2):
                dn = dn + dot(w_ref[p, rb], dh[0, p * part : (p + 1) * part], 1, 0)
            n_part[rb] = dn.astype(BF16)
            for i in range(2):
                col = gain_cols[:width, 2 * b + i : 2 * b + i + 1]
                ri = slice(i * width, (i + 1) * width)
                ra = slice((2 * b + i) * width, (2 * b + i + 1) * width)
                for j in range(SLOTS):
                    here = lanes_of(j)
                    d_hat = dn[ri, here] * col
                    centred = (x_all[ra, here].astype(F32) - mean[j : j + 1]) * inv[j : j + 1]
                    hat[j] = hat[j] + jnp.sum(d_hat.reshape(-1, 8, KEEP), axis=0)
                    cross[j] = cross[j] + jnp.sum((d_hat * centred).reshape(-1, 8, KEEP), axis=0)
        small = SmallSum(place, val2, box2, s2s, s2r, 2 * SLOTS)
        small.start(jnp.concatenate([jnp.sum(t, axis=0, keepdims=True) for t in hat + cross], axis=0))
        plan.add(small_flow(small, "back", back_in), 2.5)
        yield from sums[1].flow()
        yield (back_in,)
        back = known["back"]
        mean_hat = back[:SLOTS] * (1.0 / D)
        mean_cross = back[SLOTS:] * (1.0 / D)
        acc = jnp.zeros((width, KEEP), F32)
        results = []
        for j in range(SLOTS):
            here = lanes_of(j)
            total = sums[1].result(here)
            centred = (x_loc[:, here].astype(F32) - mean[j : j + 1]) * inv[j : j + 1]
            acc = acc + total * centred
            result = u_loc[:, here].astype(F32) + inv[j : j + 1] * (
                total * gain_col - mean_hat[j : j + 1] - centred * mean_cross[j : j + 1]
            )
            out_own[1, :, here] = result.astype(BF16)
            results.append(result)
        give_back(1, results)
        row = jnp.sum(
            jnp.transpose(jnp.concatenate([acc, jnp.zeros((KEEP - width, KEEP), F32)], axis=0)),
            axis=0, keepdims=True,
        )
        gval[...] = jnp.broadcast_to(row, gval.shape)
        gains = []
        for k in range(3):
            c = remote(gval, gbox.at[k], ggs.at[k], ggr.at[k], {"dp": place.dps[k + 1]})
            c.start()
            gains.append(c)
        yield from backs[1].flow()
        total = gval[...]
        for k, c in enumerate(gains):
            c.wait()
            total = total + gbox[k]
        gain_out[...] = total

    def weight_gradient_flow():
        yield tuple(far_in) + (heads_in, grads_in)
        quarter = quarters.shape[2]
        for a, arr in enumerate((normed, u_all)):
            quarters[a, 0] = arr[span(place.dp * quarter, quarter)]
        for p in range(3):
            total = dot(quarters[0, 0], dh[0, p * part : (p + 1) * part], 1, 1)
            for r in range(1, 4):
                total = total + dot(quarters[0, r], dh[r, p * part : (p + 1) * part], 1, 1)
            gq_out[p] = total
        total = dot(dh[0, 3 * part :], quarters[1, 0], 1, 1)
        for r in range(1, 4):
            total = total + dot(dh[r, 3 * part :], quarters[1, r], 1, 1)
        go_out[...] = total

    plan.add(rows_flow())
    plan.add(cotangent_flow(), 3.0)
    for a, array in enumerate((normed, u_all)):
        plan.add(quarter_flow(a, array))
    plan.add(attend_flow())
    plan.add(forward_flow())
    plan.add(backward_flow())
    plan.add(weight_gradient_flow())
    plan.run()
    for c in sends:
        c.wait_send()
    for chain in chains + backs:
        chain.drain()


def post_kernel(
    n, counts, k_hbm, own_hbm, buf_hbm, got_hbm, gg_hbm, gq_hbm, go_hbm,
    out, dp_out, gain_out, gq_out, go_out, k_ref, own_ref, buf_ref, got_ref, gg_ref, sem, osem,
):
    through = [
        pltpu.make_async_copy(src, dst, osem.at[i])
        for i, (src, dst) in enumerate(((gq_hbm, gq_out), (go_hbm, go_out)))
    ]
    for c in through:
        c.start()
    load(
        ((k_hbm, k_ref), (own_hbm, own_ref), (buf_hbm, buf_ref), (got_hbm, got_ref), (gg_hbm, gg_ref)), sem
    )
    dp = lax.axis_index("dp")
    share = Share(counts, dp)
    patch = lax.broadcasted_iota(jnp.int32, (dp_out.shape[2], KEEP), 0)
    for i in range(n):
        lanes = slice(i * KEEP, (i + 1) * KEEP)
        if i < SLOTS:
            res, d_in = (own_ref[a, :, lanes].astype(F32) * share.keeps(i) for a in range(2))
        else:
            slot = clamp(share.spare_at + i - SLOTS, SPARE - 1)
            flag = jnp.where(i - SLOTS < share.extra, 1.0, 0.0)
            here = span(slot * KEEP, KEEP)
            res, d_in = (
                (
                    buf_ref[a, :, here].astype(F32)
                    + got_ref[a, 0, :, here].astype(F32)
                    + got_ref[a, 1, :, here].astype(F32)
                )
                * flag
                for a in range(2)
            )
        pick = (patch == k_ref[i : i + 1, :]).astype(F32).astype(BF16)
        out[:, lanes] = res.astype(BF16)
        dp_out[i] = dot(d_in.astype(BF16), pick, 1, 1).astype(BF16)
    part = gain_out.shape[1]
    for g in range(4):
        @pl.when(dp == g)
        def _():
            gain_out[...] = gg_ref[:1, g * part : (g + 1) * part]
    for c in through:
        c.wait()


def sharded(patches, keep_index, counts, gain, w_qkv, w_out, cotangent):
    n, patch_count, width = patches.shape
    total_rows = n * KEEP
    rows = SLOTS * KEEP
    feats = w_qkv.shape[0]
    heads = w_out.shape[0]
    heads3 = 3 * heads
    quarter = feats // 4
    gain_row = gain[None]
    spare = SPARE * KEEP
    small = 2 * SLOTS + 16
    blk = (2, width, rows)

    def v(shape, dtype=BF16):
        return pltpu.VMEM(shape, dtype)

    scratch = [
        v((width, rows)), v((width, rows)), v((feats, rows)), v((feats, rows)), v((feats, rows)),
        v((3, heads, feats)), v((feats, heads)),
        v((n, width, patch_count)), v((n, KEEP), jnp.int32), v((width, total_rows)), v((1, width), F32),
        v((2, width, spare)), v((2, 2, width, spare)), v((2, 2, width, spare)), v((2, 2, width, spare)),
        v((8, small, KEEP), F32), v((4, small, KEEP), F32),
        v((8, 2 * SLOTS, KEEP), F32), v((4, 2 * SLOTS, KEEP), F32),
        v((heads3, rows)), v((heads, rows)),
        v((6, heads3 // 2, KEEP)), v((6, heads // 2, KEEP)), v((2, heads3 // 2, KEEP)), v((2, heads // 2, KEEP)),
        v((feats, rows)), v((feats, rows)), v((2, 4) + blk), v((2, 4) + blk),
        v((2,) + blk, F32), v((2, width, rows)), v((2, width, rows)),
        v((4, heads3 + heads, rows)), v((2, 4, quarter, rows)), v((3, feats, heads)), v((heads, feats)),
        v((3, 8, KEEP), F32), v((8, KEEP), F32),
        DMA((8,)), DMA((8,)), DMA((8,)), DMA((8,)),
        DMA((2, 20)), DMA((2, 16, 2)),
        DMA((2, 2, CHUNKS)), DMA((2, 2, CHUNKS)), DMA((2, 2, CHUNKS)), DMA((2, 2, CHUNKS)),
        DMA((6,)), DMA((6,)), DMA((6,)), DMA((6,)),
        DMA((2, 4, 2)), DMA((2, 4, 2)), DMA((2, 6)), DMA((2, 6)), DMA((2,)), DMA((2,)),
        DMA((5, 2, 3)), DMA((5, 2, 4)), DMA((4,)), DMA((4,)), DMA((2, 4)), DMA((2, 4)),
        DMA((2, 8)), DMA((2, 8, 2)), DMA((6,)), DMA((3,)), DMA((3,)),
    ]
    shape = jax.ShapeDtypeStruct
    out_own, out_buf, out_got, gq, go, gg = pl.pallas_call(
        main_kernel,
        out_shape=[
            shape((2, width, rows), BF16), shape((2, width, spare), BF16),
            shape((2, 2, width, spare), BF16),
            shape((3, quarter, heads), F32), shape((heads, quarter), F32),
            shape((8, KEEP), F32),
        ],
        in_specs=[SM] + [ANY] * 6,
        out_specs=[VM] * 6,
        scratch_shapes=scratch,
        compiler_params=pltpu.CompilerParams(
            vmem_limit_bytes=58 * 1024 * 1024, collective_id=1, has_side_effects=True
        ),
    )(
        counts, jnp.transpose(patches, (0, 2, 1)), keep_index, cotangent.T, gain_row,
        jnp.transpose(w_qkv, (1, 0, 2)), w_out,
    )
    part = width // 4
    outputs, d_patches, grad_gain, gq, go = pl.pallas_call(
        partial(post_kernel, n),
        out_shape=[
            shape((width, total_rows), BF16), shape((n, width, patch_count), BF16), shape((1, part), F32),
            shape(gq.shape, F32), shape(go.shape, F32),
        ],
        in_specs=[SM] + [ANY] * 7,
        out_specs=[VM] * 5,
        scratch_shapes=[
            v((n, KEEP), jnp.int32), v((2, width, rows)), v((2, width, spare)), v((2, 2, width, spare)),
            v((8, KEEP), F32), DMA((5,)), DMA((2,)),
        ],
        compiler_params=pltpu.CompilerParams(vmem_limit_bytes=58 * 1024 * 1024),
    )(counts, keep_index, out_own, out_buf, out_got, gg, gq, go)
    return (
        outputs.T, jnp.transpose(d_patches, (0, 2, 1)), jnp.transpose(gq, (1, 0, 2)), go,
        grad_gain.reshape(part),
    )


def solution(mesh):
    placed = (
        P("dp", None, ("mcol", "mrow")),
        P("dp", None),
        P(),
        P(("mcol", "mrow")),
        P("mcol", None, "mrow"),
        P("mrow", "mcol"),
        P("dp", ("mcol", "mrow")),
    )
    return jax.shard_map(
        sharded,
        mesh=mesh,
        in_specs=placed,
        out_specs=(
            P("dp", ("mcol", "mrow")),
            P("dp", None, ("mcol", "mrow")),
            P(("mcol", "dp"), None, "mrow"),
            P("mrow", ("mcol", "dp")),
            P(("mcol", "mrow", "dp")),
        ),
        check_vma=False,
    )
```

```python
import heapq
from functools import partial

import jax
import jax.numpy as jnp
from jax import lax
from jax.experimental import pallas as pl
from jax.experimental.pallas import tpu as pltpu
from jax.sharding import PartitionSpec as P

D = 6144
HD = 128
KEEP = 128
SLOTS = 4
SPARE = 6
CHUNKS = 2
DIRECT = (True, True)
EPSILON = 1e-06

F32 = jnp.float32
BF16 = jnp.bfloat16
MESH = pl.DeviceIdType.MESH
VM = pl.BlockSpec(memory_space=pltpu.VMEM)
SM = pl.BlockSpec(memory_space=pltpu.SMEM)
ANY = pl.BlockSpec(memory_space=pl.ANY)
DMA = pltpu.SemaphoreType.DMA


def dot(a, b, ca, cb):
    return lax.dot_general(a, b, (((ca,), (cb,)), ((), ())), preferred_element_type=F32)


def remote(src, dst, send, recv, where):
    return pltpu.make_async_remote_copy(
        src_ref=src, dst_ref=dst, send_sem=send, recv_sem=recv, device_id=where, device_id_type=MESH
    )


def clamp(value, top):
    return jnp.minimum(jnp.maximum(value, 0), top)


def greet(peers):
    barrier = pltpu.get_barrier_semaphore()
    for peer in peers:
        pl.semaphore_signal(barrier, inc=1, device_id=peer, device_id_type=MESH)
    pl.semaphore_wait(barrier, len(peers))


def span(start, size, step=None):
    return pl.ds(pl.multiple_of(start, step or size), size)


class Event:
    done = False


class Plan:
    def __init__(self):
        self.now, self.count, self.queue, self.parked = 0.0, 0, [], []

    def add(self, flow, delay=0.0):
        self.count += 1
        heapq.heappush(self.queue, (self.now + delay, self.count, flow))

    def run(self):
        while self.queue:
            at, _, flow = heapq.heappop(self.queue)
            self.now = max(self.now, at)
            want = next(flow, None)
            if isinstance(want, tuple):
                self.parked.append((want, flow))
            elif want is not None:
                self.add(flow, want)
            waiting, self.parked = self.parked, []
            for events, other in waiting:
                if all(e.done for e in events):
                    self.add(other)
                else:
                    self.parked.append((events, other))
        assert not self.parked


def load(pairs, sem):
    copies = [pltpu.make_async_copy(src, dst, sem.at[i]) for i, (src, dst) in enumerate(pairs)]
    for c in copies:
        c.start()
    for c in copies:
        c.wait()


class Place:
    def __init__(self):
        self.me = lax.axis_index("mrow")
        self.core = lax.rem(self.me, 2)
        self.y = lax.rem(lax.div(self.me, 2), 4)
        self.zh = lax.div(self.me, 8)
        self.x = lax.axis_index("mcol")
        self.dp = lax.axis_index("dp")
        self.sib = self.at(self.zh, 0, 1 - self.core)
        self.anti = self.at(1 - self.zh, 0, self.core)
        self.ys = [self.at(self.zh, d, self.core) for d in range(4)]
        self.xs = [lax.rem(self.x + d, 4) for d in range(4)]
        self.dps = [lax.rem(self.dp + d, 4) for d in range(4)]

    def at(self, zh, dy, core):
        return zh * 8 + lax.rem(self.y + dy, 4) * 2 + core

    def peers(self):
        rows = [self.sib, self.anti] + self.ys[1:]
        return (
            [{"mrow": r} for r in rows]
            + [{"mcol": c} for c in self.xs[1:]]
            + [{"dp": c} for c in self.dps[1:]]
        )


class Share:
    def __init__(self, counts, dp):
        c = [counts[g] for g in range(4)]
        keep = [jnp.minimum(v, SLOTS) for v in c]
        zero = jnp.int32(0)
        self.own = self.extra = self.spare_at = self.free = self.free_at = zero
        spare_at = free_at = zero
        for g in range(4):
            here = dp == g
            spare, free = c[g] - keep[g], SLOTS - keep[g]
            self.own = jnp.where(here, keep[g], self.own)
            self.extra = jnp.where(here, spare, self.extra)
            self.free = jnp.where(here, free, self.free)
            self.spare_at = jnp.where(here, spare_at, self.spare_at)
            self.free_at = jnp.where(here, free_at, self.free_at)
            spare_at, free_at = spare_at + spare, free_at + free

    def holds(self, slot, image):
        k = image - SLOTS
        return jnp.where((self.spare_at + k == slot) & (k < self.extra), 1.0, 0.0)

    def keeps(self, position):
        return jnp.where(position < self.own, 1.0, 0.0)

    def works(self, position, slot):
        k = position - self.own
        return jnp.where((k >= 0) & (self.free_at + k == slot), 1.0, 0.0)


class SmallSum:
    def __init__(self, place, val, box, send, recv, x_rows):
        self.place, self.val, self.box = place, val, box
        self.send, self.recv, self.x_rows = send, recv, x_rows
        self.live = []
        self.n = 0

    def push(self, peers, rows=None):
        self.live = []
        for where in peers:
            k = self.n
            self.n += 1
            stage = self.val.at[self.stage]
            box = self.box.at[k]
            if rows is not None:
                stage, box = stage.at[:rows], box.at[:rows]
            c = remote(stage, box, self.send.at[k], self.recv.at[k], where)
            c.start()
            self.live.append((k, c))

    def start(self, value):
        self.stage = 0
        self.val[0] = value
        self.push([{"mrow": self.place.sib}])

    def step(self):
        total = self.val[self.stage]
        rows = self.x_rows if self.stage == 3 else total.shape[0]
        total = total[:rows]
        for k, c in self.live:
            c.wait()
            total = total + self.box[k, :rows]
        self.stage += 1
        if self.stage < 4:
            self.val[self.stage] = total
        if self.stage == 1:
            self.push([{"mrow": r} for r in self.place.ys[1:]])
        elif self.stage == 2:
            self.push([{"mrow": self.place.anti}])
        elif self.stage == 3:
            self.push([{"mcol": c} for c in self.place.xs[1:]], self.x_rows)
        return total


class Chain:
    def __init__(self, place, own, got, fwd, send, recv):
        self.dp, self.own, self.got, self.fwd, self.send, self.recv = place.dp, own, got, fwd, send, recv
        self.near = [{"dp": place.dps[1]}, {"dp": place.dps[3]}]
        self.width = own.shape[1] // CHUNKS

    def lanes(self, ch):
        return pl.ds(ch * self.width, self.width)

    def copy(self, way, ch, first):
        src = self.own if first else self.fwd.at[way]
        return remote(
            src.at[:, self.lanes(ch)], self.got.at[way, :, self.lanes(ch)],
            self.send.at[way, ch], self.recv.at[way, ch], self.near[way],
        )

    def forward(self, way, ch):
        self.copy(way, ch, False).wait_recv()
        here = self.lanes(ch)
        self.fwd[way, :, here] = self.got[way, :, here] + self.own[:, here]
        self.copy(way, ch, False).start()

    def start(self):
        for dp, way in ((0, 0), (3, 1)):
            @pl.when(self.dp == dp)
            def _():
                for ch in range(CHUNKS):
                    self.copy(way, ch, True).start()
                self.got[way] = jnp.zeros(self.got.shape[1:], BF16)

    def flow(self):
        for way, ch, after in (
            (0, 0, 3.5), (0, 1, 1.0), (1, 0, 2.5), (1, 1, 1.5)
        ):
            yield after
            for dp, w in ((1, way), (2, 1 - way)):
                @pl.when(self.dp == dp)
                def _():
                    self.forward(w, ch)
        yield 3.5
        for dp, way in ((0, 1), (3, 0)):
            @pl.when(self.dp == dp)
            def _():
                for ch in range(CHUNKS):
                    self.copy(way, ch, False).wait_recv()

    def drain(self):
        for way, last in ((0, 3), (1, 0)):
            @pl.when(self.dp != last)
            def _():
                for ch in range(CHUNKS):
                    self.copy(way, ch, False).wait_send()

    def slot(self, s):
        here = slice(s * KEEP, (s + 1) * KEEP)
        return (
            self.own[:, here].astype(F32)
            + self.got[0, :, here].astype(F32)
            + self.got[1, :, here].astype(F32)
        )


def attend(q, k, v, do):
    def norm(t):
        c = t - jnp.mean(t, axis=0, keepdims=True)
        i = lax.rsqrt(jnp.mean(c * c, axis=0, keepdims=True) + EPSILON)
        return c * i, i

    def norm_back(d, y, i):
        return i * (
            d - jnp.mean(d, axis=0, keepdims=True) - y * jnp.mean(d * y, axis=0, keepdims=True)
        )

    def mm(a, b, ca, cb):
        return lax.dot_general(
            a, b, (((ca,), (cb,)), ((), ())), preferred_element_type=F32, precision=lax.Precision.HIGHEST
        )

    scale = HD ** (-0.5)
    qn, iq = norm(q)
    kn, ik = norm(k)
    w = jnp.exp(mm(kn, qn, 0, 0) * scale)
    w = w / jnp.sum(w, axis=0, keepdims=True)
    out = mm(v, w, 1, 0)
    dw = mm(v, do, 0, 0)
    ds = w * (dw - jnp.sum(w * dw, axis=0, keepdims=True)) * scale
    dv = mm(do, w, 1, 1)
    dq = norm_back(mm(kn, ds, 1, 0), qn, iq)
    dk = norm_back(mm(qn, ds, 1, 1), kn, ik)
    return out, dq, dk, dv


def gather_rows(place, loc, out, send, recv, sends, direct):
    width, rows = loc.shape
    half = rows // 2
    me, sib, core = place.me, {"mrow": place.sib}, place.core
    right, left, across = ({"mrow": place.ys[d]} for d in (1, 3, 2))
    count = [0]

    def view(slot, part=None):
        block = out.at[span(slot * width, width)]
        return block if part is None else block.at[:, pl.ds(part * half, half)]

    def push(slot, where, part=None, src=None):
        k = count[0]
        count[0] += 1
        c = remote(
            view(slot, part) if src is None else src, view(slot, part),
            send.at[k], recv.at[slot, part or 0], where,
        )
        c.start()
        sends.append(c)

    def got(slot, part=None):
        remote(view(slot, part), view(slot, part), send.at[0], recv.at[slot, part or 0], sib).wait_recv()

    push(me, {"mrow": place.anti}, src=loc)
    push(me, right, src=loc)
    push(me, left, src=loc)
    if direct:
        push(me, across, src=loc)
    push(me, sib, src=loc)
    out[span(me * width, width)] = loc[...]

    def ring(zh):
        before, after = place.at(zh, 3, core), place.at(zh, 1, core)
        got(before)
        if not direct:
            push(before, right, 0)
        got(after)
        if not direct:
            push(after, left, 1)
        push(before, sib)
        push(after, sib)

    def far(zh):
        slot = place.at(zh, 2, core)
        if direct:
            got(slot)
        else:
            got(slot, 0)
            got(slot, 1)
        push(slot, sib)

    yield 4.0
    ring(place.zh)
    yield 3.5
    got(place.anti)
    push(place.anti, right)
    push(place.anti, left)
    if direct:
        push(place.anti, across)
    push(place.anti, sib)
    yield 0.5
    far(place.zh)
    yield 4.0
    ring(1 - place.zh)
    yield 1.5 if direct else 4.0
    far(1 - place.zh)
    yield 2.0
    for zh in range(2):
        for dy in range(4):
            got(place.at(zh, dy, 1 - core))


class ReduceX:
    def __init__(self, place, src, buf, fwd, send, recv):
        self.place, self.src, self.buf, self.fwd, self.send, self.recv = place, src, buf, fwd, send, recv
        self.half, self.width = buf.shape[1], buf.shape[2]

    def view(self, p, block):
        return self.src.at[pl.ds(p * self.half, self.half), span(block * self.width, self.width)]

    def push(self, src, slot, where, sends):
        c = remote(src, self.buf.at[slot], self.send.at[slot], self.recv.at[slot], where)
        c.start()
        sends.append(c)

    def got(self, slot):
        b = self.buf.at[slot]
        remote(b, b, self.send.at[slot], self.recv.at[slot], {"mcol": self.place.xs[1]}).wait_recv()

    def flow(self, sends):
        xs = self.place.xs
        right, left = {"mcol": xs[1]}, {"mcol": xs[3]}
        self.push(self.view(0, xs[2]), 0, right, sends)
        self.push(self.view(1, xs[2]), 1, left, sends)
        self.push(self.view(0, xs[3]), 2, left, sends)
        self.push(self.view(1, xs[1]), 3, right, sends)
        yield 4.0
        for p, (at, where) in enumerate(((xs[1], right), (xs[3], left))):
            self.got(p)
            self.fwd[p] = self.buf[p] + self.view(p, at)[...]
            self.push(self.fwd.at[p], 4 + p, where, sends)
        yield 4.0
        for slot in range(2, 6):
            self.got(slot)

    def total(self, r0):
        p, r = divmod(r0, self.half)
        here = slice(r, r + HD)
        return (
            self.src[r0 : r0 + HD, span(self.place.x * self.width, self.width)].astype(F32)
            + self.buf[2 + p, here].astype(F32)
            + self.buf[4 + p, here].astype(F32)
        )


class RingX:
    def __init__(self, place, dh, slot, start, rows, send, recv):
        self.x, self.xs, self.view = place.x, place.xs, dh.at[slot, pl.ds(start, rows)]
        self.send, self.recv = send, recv
        self.right, self.left = {"mcol": place.xs[1]}, {"mcol": place.xs[3]}
        self.half, self.width = rows // 2, dh.shape[2] // 4

    def copy(self, p, block, k, where):
        view = self.view.at[pl.ds(p * self.half, self.half), span(block * self.width, self.width)]
        return remote(view, view, self.send.at[p, k], self.recv.at[p, block], where)

    def push(self, p, block, k, where, sends):
        c = self.copy(p, block, k, where)
        c.start()
        sends.append(c)

    def got(self, p, block):
        self.copy(p, block, 0, self.right).wait_recv()

    def flow(self, sends, pace):
        xs = self.xs
        for p in range(2):
            self.push(p, self.x, 0, self.right, sends)
            self.push(p, self.x, 1, self.left, sends)
        yield pace
        self.got(0, xs[3])
        self.push(0, xs[3], 2, self.right, sends)
        self.got(1, xs[1])
        self.push(1, xs[1], 2, self.left, sends)
        yield pace
        self.got(1, xs[3])
        self.got(0, xs[1])
        self.got(0, xs[2])
        self.got(1, xs[2])


class Quarter:
    def __init__(self, place, array, out, zsend, zrecv, send, recv, sends):
        self.place, self.array, self.out = place, array, out
        self.zsend, self.zrecv, self.send, self.recv, self.sends = zsend, zrecv, send, recv, sends
        self.share = out.shape[1] // 8
        self.n = 0

    def index(self, dy, core):
        return lax.rem(self.place.y + dy, 4) * 2 + core

    def view(self, index, part=None):
        rows = span(index * self.share, self.share)
        half = self.out.shape[2] // 2
        return self.out.at[1:4, rows] if part is None else self.out.at[1:4, rows, pl.ds(part * half, half)]

    def zcopy(self, r):
        dp, mine = self.place.dps[r], self.index(0, self.place.core)
        src = self.array.at[span(dp * self.out.shape[1] + mine * self.share, self.share)]
        dst = self.out.at[r, span(mine * self.share, self.share)]
        return remote(src, dst, self.zsend.at[r], self.zrecv.at[r], {"dp": dp})

    def copy(self, index, where, part, k):
        view = self.view(index, part)
        return remote(view, view, self.send.at[k], self.recv.at[index, part or 0], where)

    def push(self, index, where, part=None):
        c = self.copy(index, where, part, self.n)
        self.n += 1
        c.start()
        self.sends.append(c)

    def got(self, index, part=None):
        self.copy(index, {"mrow": self.place.sib}, part, 0).wait_recv()

    def flow(self):
        place, core = self.place, self.place.core
        right, left, sib = {"mrow": place.ys[1]}, {"mrow": place.ys[3]}, {"mrow": place.sib}
        for r in (1, 3, 2):
            self.zcopy(r).start()
        yield 9.0
        mine, before, after, far = (self.index(d, core) for d in (0, 3, 1, 2))
        for r in (1, 3, 2):
            self.zcopy(r).wait()
        for where in (right, left, sib):
            self.push(mine, where)
        yield 7.0
        self.got(before)
        self.push(before, right, 0)
        self.got(after)
        self.push(after, left, 1)
        self.push(before, sib)
        self.push(after, sib)
        yield 6.0
        self.got(far, 0)
        self.got(far, 1)
        self.push(far, sib)
        yield 6.0
        for dy in range(4):
            self.got(self.index(dy, 1 - core))


class ReduceRows:
    def __init__(self, place, array, cbox, ybuf, ysum, ztot, zbox, csem, ysem, zsem, sends):
        self.place, self.array, self.cbox, self.ybuf = place, array, cbox, ybuf
        self.ysum, self.ztot, self.zbox = ysum, ztot, zbox
        self.csem, self.ysem, self.zsem, self.sends = csem, ysem, zsem, sends
        self.width, self.rows = ztot.shape

    def target(self, z, d, c):
        return self.array.at[span(self.place.at(z, d, c) * self.width, self.width)]

    def core_copy(self, d, z):
        return remote(
            self.target(z, d, 1 - self.place.core), self.cbox.at[d, z],
            self.csem[0].at[d, z], self.csem[1].at[d, z], {"mrow": self.place.sib},
        )

    def add(self, d, srcs, lanes=slice(None)):
        for z in range(2):
            total = self.cbox[d, z, :, lanes]
            for s in srcs:
                total = total + s[z][:, lanes]
            self.cbox[d, z, :, lanes] = total

    def core_sum(self, d):
        for z in range(2):
            self.core_copy(d, z).wait_recv()
        self.add(d, [[self.target(z, d, self.place.core) for z in range(2)]])

    def ypush(self, d, slot, lanes, k, where):
        c = remote(
            self.cbox.at[d, :, :, lanes], self.ybuf.at[slot, :, :, lanes],
            self.ysem[0].at[k], self.ysem[1].at[k], where,
        )
        c.start()
        self.sends.append(c)

    def ygot(self, slot, lanes, k):
        b = self.ybuf.at[slot, :, :, lanes]
        remote(b, b, self.ysem[0].at[k], self.ysem[1].at[k], {"mrow": self.place.sib}).wait_recv()

    def flow(self):
        place = self.place
        right, left = {"mrow": place.ys[1]}, {"mrow": place.ys[3]}
        lo, hi = pl.ds(0, self.rows // 2), pl.ds(self.rows // 2, self.rows // 2)
        for d in (2, 1, 3, 0):
            for z in range(2):
                c = self.core_copy(d, z)
                c.start()
                self.sends.append(c)
        yield 2.5
        self.core_sum(2)
        self.ypush(2, 0, lo, 0, right)
        self.ypush(2, 1, hi, 1, left)
        self.core_sum(1)
        self.ypush(1, 2, hi, 3, right)
        self.core_sum(3)
        self.ypush(3, 3, lo, 4, left)
        self.core_sum(0)
        yield 3.0
        self.ygot(0, lo, 0)
        self.add(1, [[self.ybuf.at[0, z] for z in range(2)]], lo)
        self.ypush(1, 2, lo, 2, right)
        self.ygot(1, hi, 1)
        self.add(3, [[self.ybuf.at[1, z] for z in range(2)]], hi)
        self.ypush(3, 3, hi, 5, left)
        yield 4.0
        for slot, lanes, k in ((2, hi, 3), (3, lo, 4), (2, lo, 2), (3, hi, 5)):
            self.ygot(slot, lanes, k)

        for z in range(2):
            self.ysum[z] = (
                self.cbox[0, z].astype(F32) + self.ybuf[2, z].astype(F32) + self.ybuf[3, z].astype(F32)
            )
        self.ztot[...] = self.ysum[1 - place.zh].astype(BF16)

        c = remote(self.ztot, self.zbox, self.zsem[0], self.zsem[1], {"mrow": place.anti})
        c.start()
        self.sends.append(c)
        yield 8.0
        c.wait_recv()

    def result(self, lanes):
        return self.ysum[self.place.zh, :, lanes] + self.zbox[:, lanes].astype(F32)


def main_kernel(
    counts, p_hbm, k_hbm, c_hbm, g_hbm, w_hbm, wo_hbm,
    out_own, out_sum, gq_out, go_out, gain_out,
    x_loc, u_loc, x_all, u_all, normed, wt, wot,
    p_ref, k_ref, c_ref, g_ref, sp_own, sp_got, sp_fwd, out_buf, out_got, rt_fwd,
    box1, val1, box2, val2,
    q_part, m_part, bq, bm, fq, fm,
    a_part, n_part, cbox, ybuf, ysum, ztot, zbox,
    dh, quarters, w_ref, wo_ref, gbox, gval,
    s1s, s1r, s2s, s2r, g1s, g1r,
    sps, spr, rts, rtr,
    sq, sm, rq, rm,
    cs2, cr2, ys2, yr2, zs2, zr2, dxs, dxr, dzs, dzr, qzs, qzr, qys, qyr, wsem, ggs, ggr,
):
    pairs = (
        (p_hbm, p_ref), (k_hbm, k_ref), (c_hbm, c_ref), (g_hbm, g_ref), (w_hbm, w_ref), (wo_hbm, wo_ref)
    )
    loads = [pltpu.make_async_copy(src, dst, wsem.at[i]) for i, (src, dst) in enumerate(pairs)]
    for c in loads:
        c.start()
    place = Place()
    peers = place.peers()
    barrier = pltpu.get_barrier_semaphore()
    for peer in peers:
        pl.semaphore_signal(barrier, inc=1, device_id=peer, device_id_type=MESH)
    width = x_loc.shape[0]
    core, zh = place.core, place.zh
    share = Share(counts, place.dp)
    patch = lax.broadcasted_iota(jnp.int32, (p_ref.shape[2], KEEP), 0)
    for c in loads[:4]:
        c.wait()

    def lanes_of(i):
        return slice(i * KEEP, (i + 1) * KEEP)

    def kept(i):
        pick = (patch == k_ref[i : i + 1, :]).astype(F32).astype(BF16)
        return dot(p_ref[i], pick, 1, 0)

    late = [(kept(i), c_ref[:, lanes_of(i)].astype(F32)) for i in range(SLOTS, 2 * SLOTS)]
    for s in range(SPARE):
        flags = [share.holds(s, i) for i in range(SLOTS, 2 * SLOTS)]
        for a in range(2):
            total = late[0][a] * flags[0]
            for image, flag in zip(late[1:], flags[1:]):
                total = total + image[a] * flag
            sp_own[a, :, lanes_of(s)] = total.astype(BF16)
    pl.semaphore_wait(barrier, len(peers))
    chains = [
        Chain(place, sp_own.at[a], sp_got.at[a], sp_fwd.at[a], sps.at[a], spr.at[a]) for a in range(2)
    ]
    plan = Plan()
    sends = []
    stats_in, q_in, u_in, m_in, heads_in, grads_in, back_in = (Event() for _ in range(7))
    normed_in = Event()
    far_in = [Event() for _ in range(5)]
    part = w_ref.shape[2]
    gval[...] = jnp.zeros(gval.shape, F32)
    gval[:1, :width] = g_ref[...]
    gain_row = gval[:1]
    gain_col = jnp.transpose(jnp.broadcast_to(gain_row, (KEEP, KEEP)))[:width, :1]
    keeps = [share.keeps(j) for j in range(SLOTS)]
    works = [[share.works(j, s) for s in range(SPARE)] for j in range(SLOTS)]
    known = {}

    def choose(a, loc, firsts):
        spare = [chains[a].slot(s) for s in range(SPARE)]
        values = []
        for j in range(SLOTS):
            v = firsts[j] * keeps[j]
            for s in range(SPARE):
                v = v + spare[s] * works[j][s]
            loc[:, lanes_of(j)] = v.astype(BF16)
            values.append(v)
        return values

    def small_flow(small, name, event):
        for pace in (2.5, 3.0, 4.5, 3.0):
            yield pace
            known[name] = small.step()
        event.done = True

    def weights_flow():
        for c in loads[4:]:
            c.wait()
        for p in range(3):
            wt[p] = jnp.transpose(w_ref[p])
        wot[...] = jnp.transpose(wo_ref[...])
        yield 0.0

    def rows_flow():
        chains[0].start()
        firsts = [kept(j) for j in range(SLOTS)]
        yield from chains[0].flow()
        values = choose(0, x_loc, firsts)
        me_row = lax.broadcasted_iota(jnp.int32, (16, KEEP), 0) == place.me
        small = SmallSum(place, val1, box1, s1s, s1r, 2 * SLOTS)
        small.start(
            jnp.concatenate(
                [jnp.sum(v, axis=0, keepdims=True) for v in values]
                + [jnp.sum(v * v, axis=0, keepdims=True) for v in values]
                + [jnp.where(me_row, gain_row, 0.0)],
                axis=0,
            )
        )
        plan.add(small_flow(small, "stats", stats_in), 2.5)
        gather = gather_rows(place, x_loc, x_all, g1s.at[0], g1r.at[0], sends, DIRECT[0])
        pace = next(gather)
        plan.add(weights_flow())
        yield pace
        yield from gather
        yield (stats_in,)
        known["gain_cols"] = gain_cols = jnp.transpose(
            jnp.concatenate([val1[3, 2 * SLOTS :], jnp.zeros((KEEP - 16, KEEP), F32)], axis=0)
        )
        stats = known["stats"]
        known["mean"] = mean = stats[:SLOTS] * (1.0 / D)
        known["inv"] = inv = lax.rsqrt(stats[SLOTS:] * (1.0 / D) - mean * mean + EPSILON)
        for b in range(16):
            rb = slice(b * width, (b + 1) * width)
            col = gain_cols[:width, b : b + 1]
            for j in range(SLOTS):
                here = lanes_of(j)
                centred = (x_all[rb, here].astype(F32) - mean[j : j + 1]) * inv[j : j + 1]
                normed[rb, here] = (centred * col).astype(BF16)
        normed_in.done = True
        for p in range(3):
            q_part[p * part : (p + 1) * part] = dot(wt[p], normed[...], 1, 0).astype(BF16)
        yield from q_sum.flow(sends)
        q_in.done = True

    def cotangent_flow():
        chains[1].start()
        firsts = [c_ref[:, lanes_of(j)].astype(F32) for j in range(SLOTS)]
        yield from chains[1].flow()
        choose(1, u_loc, firsts)
        yield from gather_rows(place, u_loc, u_all, g1s.at[1], g1r.at[1], sends, DIRECT[1])
        u_in.done = True
        m_part[...] = dot(wo_ref[...], u_all[...], 1, 0).astype(BF16)
        yield from m_sum.flow(sends)
        m_in.done = True

    def quarter_flow(a, array):
        yield ((normed_in, u_in)[a],)
        yield from Quarter(
            place, array, quarters.at[a], qzs.at[a], qzr.at[a], qys.at[a], qyr.at[a], sends
        ).flow()
        far_in[3 + a].done = True

    q_sum = ReduceX(place, q_part, bq, fq, sq, rq)
    m_sum = ReduceX(place, m_part, bm, fm, sm, rm)

    def ring_flow(n, slot, start, rows, event, pace):
        yield from RingX(place, dh, slot, start, rows, dxs.at[n], dxr.at[n]).flow(sends, pace)
        event.done = True

    def far_flow(n, r, copy, pace):
        yield pace
        copy.wait_recv()
        yield from ring_flow(1 + r, r, 0, dh.shape[1], far_in[n], 10.0)

    def attend_flow():
        yield (q_in, m_in)
        here = span(place.x * KEEP, KEEP)
        for h in range(part // HD):
            q, k, v, do = [q_sum.total((p * (part // HD) + h) * HD) for p in range(3)] + [m_sum.total(h * HD)]
            out, dq, dk, dv = attend(q, k, v, do)
            for p, value in enumerate((dq, dk, dv, out)):
                r0 = p * part + h * HD
                dh[0, r0 : r0 + HD, here] = value.astype(BF16)
        plan.add(ring_flow(0, 0, 3 * part, part, heads_in, 3.0))
        plan.add(ring_flow(1, 0, 0, 3 * part, grads_in, 4.5))
        copies = [
            remote(dh.at[0, :, here], dh.at[r, :, here], dzs.at[r], dzr.at[r], {"dp": place.dps[r]})
            for r in range(1, 4)
        ]
        yield 0.0
        for n, r in enumerate((1, 3, 2)):
            copies[r - 1].start()
            sends.append(copies[r - 1])
            plan.add(far_flow(n, r, copies[r - 1], (14.0, 16.0, 18.0)[n]))

    feats = normed.shape[0]
    block = 2 * width
    sums = [
        ReduceRows(
            place, array, cbox.at[a], ybuf.at[a], ysum.at[a], ztot.at[a], zbox.at[a],
            (cs2.at[a], cr2.at[a]), (ys2.at[a], yr2.at[a]), (zs2.at[a], zr2.at[a]), sends,
        )
        for a, array in enumerate((a_part, n_part))
    ]
    backs = [
        Chain(place, out_buf.at[a], out_got.at[a], rt_fwd.at[a], rts.at[a], rtr.at[a]) for a in range(2)
    ]

    def give_back(a, results):
        for s in range(SPARE):
            total = results[0] * works[0][s]
            for j in range(1, SLOTS):
                total = total + results[j] * works[j][s]
            out_buf[a, :, lanes_of(s)] = total.astype(BF16)
        backs[a].start()

    def forward_flow():
        yield (heads_in,)
        for b in range(feats // block):
            rb = slice(b * block, (b + 1) * block)
            a_part[rb] = dot(wot[rb], dh[0, 3 * part :], 1, 0).astype(BF16)
        yield from sums[0].flow()
        results = []
        for j in range(SLOTS):
            result = x_loc[:, lanes_of(j)].astype(F32) + sums[0].result(lanes_of(j))
            out_own[0, :, lanes_of(j)] = result.astype(BF16)
            results.append(result)
        give_back(0, results)
        yield from backs[0].flow()
        out_sum[0] = out_buf[0] + out_got[0, 0] + out_got[0, 1]

    def backward_flow():
        yield (grads_in,)
        mean, inv, gain_cols = known["mean"], known["inv"], known["gain_cols"]
        hat = [jnp.zeros((8, KEEP), F32) for _ in range(SLOTS)]
        cross = [jnp.zeros((8, KEEP), F32) for _ in range(SLOTS)]
        for b in range(feats // block):
            rb = slice(b * block, (b + 1) * block)
            dn = dot(w_ref[0, rb], dh[0, :part], 1, 0)
            for p in (1, 2):
                dn = dn + dot(w_ref[p, rb], dh[0, p * part : (p + 1) * part], 1, 0)
            n_part[rb] = dn.astype(BF16)
            for i in range(2):
                col = gain_cols[:width, 2 * b + i : 2 * b + i + 1]
                ri = slice(i * width, (i + 1) * width)
                ra = slice((2 * b + i) * width, (2 * b + i + 1) * width)
                for j in range(SLOTS):
                    here = lanes_of(j)
                    d_hat = dn[ri, here] * col
                    centred = (x_all[ra, here].astype(F32) - mean[j : j + 1]) * inv[j : j + 1]
                    hat[j] = hat[j] + jnp.sum(d_hat.reshape(-1, 8, KEEP), axis=0)
                    cross[j] = cross[j] + jnp.sum((d_hat * centred).reshape(-1, 8, KEEP), axis=0)
        small = SmallSum(place, val2, box2, s2s, s2r, 2 * SLOTS)
        small.start(jnp.concatenate([jnp.sum(t, axis=0, keepdims=True) for t in hat + cross], axis=0))
        plan.add(small_flow(small, "back", back_in), 2.5)
        yield from sums[1].flow()
        yield (back_in,)
        back = known["back"]
        mean_hat = back[:SLOTS] * (1.0 / D)
        mean_cross = back[SLOTS:] * (1.0 / D)
        acc = jnp.zeros((width, KEEP), F32)
        results = []
        for j in range(SLOTS):
            here = lanes_of(j)
            total = sums[1].result(here)
            centred = (x_loc[:, here].astype(F32) - mean[j : j + 1]) * inv[j : j + 1]
            acc = acc + total * centred
            result = u_loc[:, here].astype(F32) + inv[j : j + 1] * (
                total * gain_col - mean_hat[j : j + 1] - centred * mean_cross[j : j + 1]
            )
            out_own[1, :, here] = result.astype(BF16)
            results.append(result)
        give_back(1, results)
        row = jnp.sum(
            jnp.transpose(jnp.concatenate([acc, jnp.zeros((KEEP - width, KEEP), F32)], axis=0)),
            axis=0, keepdims=True,
        )
        gval[...] = jnp.broadcast_to(row, gval.shape)
        gains = []
        for k in range(3):
            c = remote(gval, gbox.at[k], ggs.at[k], ggr.at[k], {"dp": place.dps[k + 1]})
            c.start()
            gains.append(c)
        yield from backs[1].flow()
        out_sum[1] = out_buf[1] + out_got[1, 0] + out_got[1, 1]
        total = gval[...]
        for k, c in enumerate(gains):
            c.wait()
            total = total + gbox[k]
        gain_out[...] = total

    def weight_gradient_flow():
        yield tuple(far_in) + (heads_in, grads_in)
        quarter = quarters.shape[2]
        for a, arr in enumerate((normed, u_all)):
            quarters[a, 0] = arr[span(place.dp * quarter, quarter)]
        for p in range(3):
            total = dot(quarters[0, 0], dh[0, p * part : (p + 1) * part], 1, 1)
            for r in range(1, 4):
                total = total + dot(quarters[0, r], dh[r, p * part : (p + 1) * part], 1, 1)
            gq_out[p] = total
        total = dot(dh[0, 3 * part :], quarters[1, 0], 1, 1)
        for r in range(1, 4):
            total = total + dot(dh[r, 3 * part :], quarters[1, r], 1, 1)
        go_out[...] = total

    plan.add(rows_flow())
    plan.add(cotangent_flow(), 3.0)
    for a, array in enumerate((normed, u_all)):
        plan.add(quarter_flow(a, array))
    plan.add(attend_flow())
    plan.add(forward_flow())
    plan.add(backward_flow())
    plan.add(weight_gradient_flow())
    plan.run()
    for c in sends:
        c.wait_send()
    for chain in chains + backs:
        chain.drain()


def post_kernel(
    n, counts, k_hbm, own_hbm, sum_hbm, gg_hbm, gq_hbm, go_hbm,
    out, dp_out, gain_out, gq_out, go_out, k_ref, own_ref, sum_ref, gg_ref, sem, osem,
):
    through = [
        pltpu.make_async_copy(src, dst, osem.at[i])
        for i, (src, dst) in enumerate(((gq_hbm, gq_out), (go_hbm, go_out)))
    ]
    for c in through:
        c.start()
    load(
        ((k_hbm, k_ref), (own_hbm, own_ref), (sum_hbm, sum_ref), (gg_hbm, gg_ref)), sem
    )
    dp = lax.axis_index("dp")
    share = Share(counts, dp)
    patch = lax.broadcasted_iota(jnp.int32, (dp_out.shape[2], KEEP), 0)
    for i in range(n):
        lanes = slice(i * KEEP, (i + 1) * KEEP)
        if i < SLOTS:
            res, d_in = (own_ref[a, :, lanes].astype(F32) * share.keeps(i) for a in range(2))
        else:
            slot = clamp(share.spare_at + i - SLOTS, SPARE - 1)
            flag = jnp.where(i - SLOTS < share.extra, 1.0, 0.0)
            here = span(slot * KEEP, KEEP)
            res, d_in = (sum_ref[a, :, here].astype(F32) * flag for a in range(2))
        pick = (patch == k_ref[i : i + 1, :]).astype(F32).astype(BF16)
        out[:, lanes] = res.astype(BF16)
        dp_out[i] = dot(d_in.astype(BF16), pick, 1, 1).astype(BF16)
    part = gain_out.shape[1]
    for g in range(4):
        @pl.when(dp == g)
        def _():
            gain_out[...] = gg_ref[:1, g * part : (g + 1) * part]
    for c in through:
        c.wait()


def sharded(patches, keep_index, counts, gain, w_qkv, w_out, cotangent):
    n, patch_count, width = patches.shape
    total_rows = n * KEEP
    rows = SLOTS * KEEP
    feats = w_qkv.shape[0]
    heads = w_out.shape[0]
    heads3 = 3 * heads
    quarter = feats // 4
    gain_row = gain[None]
    spare = SPARE * KEEP
    small = 2 * SLOTS + 16
    blk = (2, width, rows)

    def v(shape, dtype=BF16):
        return pltpu.VMEM(shape, dtype)

    scratch = [
        v((width, rows)), v((width, rows)), v((feats, rows)), v((feats, rows)), v((feats, rows)),
        v((3, heads, feats)), v((feats, heads)),
        v((n, width, patch_count)), v((n, KEEP), jnp.int32), v((width, total_rows)), v((1, width), F32),
        v((2, width, spare)), v((2, 2, width, spare)), v((2, 2, width, spare)),
        v((2, width, spare)), v((2, 2, width, spare)), v((2, 2, width, spare)),
        v((8, small, KEEP), F32), v((4, small, KEEP), F32),
        v((8, 2 * SLOTS, KEEP), F32), v((4, 2 * SLOTS, KEEP), F32),
        v((heads3, rows)), v((heads, rows)),
        v((6, heads3 // 2, KEEP)), v((6, heads // 2, KEEP)), v((2, heads3 // 2, KEEP)), v((2, heads // 2, KEEP)),
        v((feats, rows)), v((feats, rows)), v((2, 4) + blk), v((2, 4) + blk),
        v((2,) + blk, F32), v((2, width, rows)), v((2, width, rows)),
        v((4, heads3 + heads, rows)), v((2, 4, quarter, rows)), v((3, feats, heads)), v((heads, feats)),
        v((3, 8, KEEP), F32), v((8, KEEP), F32),
        DMA((8,)), DMA((8,)), DMA((8,)), DMA((8,)),
        DMA((2, 20)), DMA((2, 16, 2)),
        DMA((2, 2, CHUNKS)), DMA((2, 2, CHUNKS)), DMA((2, 2, CHUNKS)), DMA((2, 2, CHUNKS)),
        DMA((6,)), DMA((6,)), DMA((6,)), DMA((6,)),
        DMA((2, 4, 2)), DMA((2, 4, 2)), DMA((2, 6)), DMA((2, 6)), DMA((2,)), DMA((2,)),
        DMA((5, 2, 3)), DMA((5, 2, 4)), DMA((4,)), DMA((4,)), DMA((2, 4)), DMA((2, 4)),
        DMA((2, 8)), DMA((2, 8, 2)), DMA((6,)), DMA((3,)), DMA((3,)),
    ]
    shape = jax.ShapeDtypeStruct
    out_own, out_sum, gq, go, gg = pl.pallas_call(
        main_kernel,
        out_shape=[
            shape((2, width, rows), BF16), shape((2, width, spare), BF16),
            shape((3, quarter, heads), F32), shape((heads, quarter), F32),
            shape((8, KEEP), F32),
        ],
        in_specs=[SM] + [ANY] * 6,
        out_specs=[VM] * 5,
        scratch_shapes=scratch,
        compiler_params=pltpu.CompilerParams(
            vmem_limit_bytes=58 * 1024 * 1024, collective_id=1, has_side_effects=True
        ),
    )(
        counts, jnp.transpose(patches, (0, 2, 1)), keep_index, cotangent.T, gain_row,
        jnp.transpose(w_qkv, (1, 0, 2)), w_out,
    )
    part = width // 4
    outputs, d_patches, grad_gain, gq, go = pl.pallas_call(
        partial(post_kernel, n),
        out_shape=[
            shape((width, total_rows), BF16), shape((n, width, patch_count), BF16), shape((1, part), F32),
            shape(gq.shape, F32), shape(go.shape, F32),
        ],
        in_specs=[SM] + [ANY] * 6,
        out_specs=[VM] * 5,
        scratch_shapes=[
            v((n, KEEP), jnp.int32), v((2, width, rows)), v((2, width, spare)), v((8, KEEP), F32),
            DMA((4,)), DMA((2,)),
        ],
        compiler_params=pltpu.CompilerParams(vmem_limit_bytes=58 * 1024 * 1024),
    )(counts, keep_index, out_own, out_sum, gg, gq, go)
    return (
        outputs.T, jnp.transpose(d_patches, (0, 2, 1)), jnp.transpose(gq, (1, 0, 2)), go,
        grad_gain.reshape(part),
    )


def solution(mesh):
    placed = (
        P("dp", None, ("mcol", "mrow")),
        P("dp", None),
        P(),
        P(("mcol", "mrow")),
        P("mcol", None, "mrow"),
        P("mrow", "mcol"),
        P("dp", ("mcol", "mrow")),
    )
    return jax.shard_map(
        sharded,
        mesh=mesh,
        in_specs=placed,
        out_specs=(
            P("dp", ("mcol", "mrow")),
            P("dp", None, ("mcol", "mrow")),
            P(("mcol", "dp"), None, "mrow"),
            P("mrow", ("mcol", "dp")),
            P(("mcol", "mrow", "dp")),
        ),
        check_vma=False,
    )
```

```python
import heapq
from functools import partial

import jax
import jax.numpy as jnp
from jax import lax
from jax.experimental import pallas as pl
from jax.experimental.pallas import tpu as pltpu
from jax.sharding import PartitionSpec as P

D = 6144
HD = 128
KEEP = 128
SLOTS = 4
SPARE = 6
CHUNKS = 2
DIRECT = (True, True)
EPSILON = 1e-06

F32 = jnp.float32
BF16 = jnp.bfloat16
MESH = pl.DeviceIdType.MESH
VM = pl.BlockSpec(memory_space=pltpu.VMEM)
SM = pl.BlockSpec(memory_space=pltpu.SMEM)
ANY = pl.BlockSpec(memory_space=pl.ANY)
DMA = pltpu.SemaphoreType.DMA


def dot(a, b, ca, cb):
    return lax.dot_general(a, b, (((ca,), (cb,)), ((), ())), preferred_element_type=F32)


def remote(src, dst, send, recv, where):
    return pltpu.make_async_remote_copy(
        src_ref=src, dst_ref=dst, send_sem=send, recv_sem=recv, device_id=where, device_id_type=MESH
    )


def clamp(value, top):
    return jnp.minimum(jnp.maximum(value, 0), top)


def greet(peers):
    barrier = pltpu.get_barrier_semaphore()
    for peer in peers:
        pl.semaphore_signal(barrier, inc=1, device_id=peer, device_id_type=MESH)
    pl.semaphore_wait(barrier, len(peers))


def span(start, size, step=None):
    return pl.ds(pl.multiple_of(start, step or size), size)


class Event:
    done = False


class Plan:
    def __init__(self):
        self.now, self.count, self.queue, self.parked = 0.0, 0, [], []

    def add(self, flow, delay=0.0):
        self.count += 1
        heapq.heappush(self.queue, (self.now + delay, self.count, flow))

    def run(self):
        while self.queue:
            at, _, flow = heapq.heappop(self.queue)
            self.now = max(self.now, at)
            want = next(flow, None)
            if isinstance(want, tuple):
                self.parked.append((want, flow))
            elif want is not None:
                self.add(flow, want)
            waiting, self.parked = self.parked, []
            for events, other in waiting:
                if all(e.done for e in events):
                    self.add(other)
                else:
                    self.parked.append((events, other))
        assert not self.parked


def load(pairs, sem):
    copies = [pltpu.make_async_copy(src, dst, sem.at[i]) for i, (src, dst) in enumerate(pairs)]
    for c in copies:
        c.start()
    for c in copies:
        c.wait()


class Place:
    def __init__(self):
        self.me = lax.axis_index("mrow")
        self.core = lax.rem(self.me, 2)
        self.y = lax.rem(lax.div(self.me, 2), 4)
        self.zh = lax.div(self.me, 8)
        self.x = lax.axis_index("mcol")
        self.dp = lax.axis_index("dp")
        self.sib = self.at(self.zh, 0, 1 - self.core)
        self.anti = self.at(1 - self.zh, 0, self.core)
        self.ys = [self.at(self.zh, d, self.core) for d in range(4)]
        self.xs = [lax.rem(self.x + d, 4) for d in range(4)]
        self.dps = [lax.rem(self.dp + d, 4) for d in range(4)]

    def at(self, zh, dy, core):
        return zh * 8 + lax.rem(self.y + dy, 4) * 2 + core

    def peers(self):
        rows = [self.sib, self.anti] + self.ys[1:]
        return (
            [{"mrow": r} for r in rows]
            + [{"mcol": c} for c in self.xs[1:]]
            + [{"dp": c} for c in self.dps[1:]]
        )


class Share:
    def __init__(self, counts, dp):
        c = [counts[g] for g in range(4)]
        keep = [jnp.minimum(v, SLOTS) for v in c]
        zero = jnp.int32(0)
        self.own = self.extra = self.spare_at = self.free = self.free_at = zero
        spare_at = free_at = zero
        for g in range(4):
            here = dp == g
            spare, free = c[g] - keep[g], SLOTS - keep[g]
            self.own = jnp.where(here, keep[g], self.own)
            self.extra = jnp.where(here, spare, self.extra)
            self.free = jnp.where(here, free, self.free)
            self.spare_at = jnp.where(here, spare_at, self.spare_at)
            self.free_at = jnp.where(here, free_at, self.free_at)
            spare_at, free_at = spare_at + spare, free_at + free

    def holds(self, slot, image):
        k = image - SLOTS
        return jnp.where((self.spare_at + k == slot) & (k < self.extra), 1.0, 0.0)

    def keeps(self, position):
        return jnp.where(position < self.own, 1.0, 0.0)

    def works(self, position, slot):
        k = position - self.own
        return jnp.where((k >= 0) & (self.free_at + k == slot), 1.0, 0.0)


class SmallSum:
    def __init__(self, place, val, box, send, recv, x_rows):
        self.place, self.val, self.box = place, val, box
        self.send, self.recv, self.x_rows = send, recv, x_rows
        self.live = []
        self.n = 0

    def push(self, peers, rows=None):
        self.live = []
        for where in peers:
            k = self.n
            self.n += 1
            stage = self.val.at[self.stage]
            box = self.box.at[k]
            if rows is not None:
                stage, box = stage.at[:rows], box.at[:rows]
            c = remote(stage, box, self.send.at[k], self.recv.at[k], where)
            c.start()
            self.live.append((k, c))

    def start(self, value):
        self.stage = 0
        self.val[0] = value
        self.push([{"mrow": self.place.sib}])

    def step(self):
        total = self.val[self.stage]
        rows = self.x_rows if self.stage == 3 else total.shape[0]
        total = total[:rows]
        for k, c in self.live:
            c.wait()
            total = total + self.box[k, :rows]
        self.stage += 1
        if self.stage < 4:
            self.val[self.stage] = total
        if self.stage == 1:
            self.push([{"mrow": r} for r in self.place.ys[1:]])
        elif self.stage == 2:
            self.push([{"mrow": self.place.anti}])
        elif self.stage == 3:
            self.push([{"mcol": c} for c in self.place.xs[1:]], self.x_rows)
        return total


class Chain:
    def __init__(self, place, own, got, fwd, send, recv):
        self.dp, self.own, self.got, self.fwd, self.send, self.recv = place.dp, own, got, fwd, send, recv
        self.near = [{"dp": place.dps[1]}, {"dp": place.dps[3]}]
        self.width = own.shape[1] // CHUNKS

    def lanes(self, ch):
        return pl.ds(ch * self.width, self.width)

    def copy(self, way, ch, first):
        src = self.own if first else self.fwd.at[way]
        return remote(
            src.at[:, self.lanes(ch)], self.got.at[way, :, self.lanes(ch)],
            self.send.at[way, ch], self.recv.at[way, ch], self.near[way],
        )

    def forward(self, way, ch):
        self.copy(way, ch, False).wait_recv()
        here = self.lanes(ch)
        self.fwd[way, :, here] = self.got[way, :, here] + self.own[:, here]
        self.copy(way, ch, False).start()

    def start(self):
        for dp, way in ((0, 0), (3, 1)):
            @pl.when(self.dp == dp)
            def _():
                for ch in range(CHUNKS):
                    self.copy(way, ch, True).start()
                self.got[way] = jnp.zeros(self.got.shape[1:], BF16)

    def flow(self):
        for way, ch, after in (
            (0, 0, 3.5), (0, 1, 1.0), (1, 0, 2.5), (1, 1, 1.5)
        ):
            yield after
            for dp, w in ((1, way), (2, 1 - way)):
                @pl.when(self.dp == dp)
                def _():
                    self.forward(w, ch)
        yield 3.5
        for dp, way in ((0, 1), (3, 0)):
            @pl.when(self.dp == dp)
            def _():
                for ch in range(CHUNKS):
                    self.copy(way, ch, False).wait_recv()

    def drain(self):
        for way, last in ((0, 3), (1, 0)):
            @pl.when(self.dp != last)
            def _():
                for ch in range(CHUNKS):
                    self.copy(way, ch, False).wait_send()

    def slot(self, s):
        here = slice(s * KEEP, (s + 1) * KEEP)
        return (
            self.own[:, here].astype(F32)
            + self.got[0, :, here].astype(F32)
            + self.got[1, :, here].astype(F32)
        )


def attend(q, k, v, do):
    def norm(t):
        c = t - jnp.mean(t, axis=0, keepdims=True)
        i = lax.rsqrt(jnp.mean(c * c, axis=0, keepdims=True) + EPSILON)
        return c * i, i

    def norm_back(d, y, i):
        return i * (
            d - jnp.mean(d, axis=0, keepdims=True) - y * jnp.mean(d * y, axis=0, keepdims=True)
        )

    def mm(a, b, ca, cb):
        return lax.dot_general(
            a, b, (((ca,), (cb,)), ((), ())), preferred_element_type=F32, precision=lax.Precision.HIGHEST
        )

    scale = HD ** (-0.5)
    qn, iq = norm(q)
    kn, ik = norm(k)
    w = jnp.exp(mm(kn, qn, 0, 0) * scale)
    w = w / jnp.sum(w, axis=0, keepdims=True)
    out = mm(v, w, 1, 0)
    dw = mm(v, do, 0, 0)
    ds = w * (dw - jnp.sum(w * dw, axis=0, keepdims=True)) * scale
    dv = mm(do, w, 1, 1)
    dq = norm_back(mm(kn, ds, 1, 0), qn, iq)
    dk = norm_back(mm(qn, ds, 1, 1), kn, ik)
    return out, dq, dk, dv


def gather_rows(place, loc, out, send, recv, sends, direct):
    width, rows = loc.shape
    half = rows // 2
    me, sib, core = place.me, {"mrow": place.sib}, place.core
    right, left, across = ({"mrow": place.ys[d]} for d in (1, 3, 2))
    count = [0]

    def view(slot, part=None):
        block = out.at[span(slot * width, width)]
        return block if part is None else block.at[:, pl.ds(part * half, half)]

    def push(slot, where, part=None, src=None):
        k = count[0]
        count[0] += 1
        c = remote(
            view(slot, part) if src is None else src, view(slot, part),
            send.at[k], recv.at[slot, part or 0], where,
        )
        c.start()
        sends.append(c)

    def got(slot, part=None):
        remote(view(slot, part), view(slot, part), send.at[0], recv.at[slot, part or 0], sib).wait_recv()

    push(me, {"mrow": place.anti}, src=loc)
    push(me, right, src=loc)
    push(me, left, src=loc)
    if direct:
        push(me, across, src=loc)
    push(me, sib, src=loc)
    out[span(me * width, width)] = loc[...]

    def ring(zh):
        before, after = place.at(zh, 3, core), place.at(zh, 1, core)
        got(before)
        if not direct:
            push(before, right, 0)
        got(after)
        if not direct:
            push(after, left, 1)
        push(before, sib)
        push(after, sib)

    def far(zh):
        slot = place.at(zh, 2, core)
        if direct:
            got(slot)
        else:
            got(slot, 0)
            got(slot, 1)
        push(slot, sib)

    yield 4.0
    ring(place.zh)
    yield 3.5
    got(place.anti)
    push(place.anti, right)
    push(place.anti, left)
    if direct:
        push(place.anti, across)
    push(place.anti, sib)
    yield 0.5
    far(place.zh)
    yield 4.0
    ring(1 - place.zh)
    yield 1.5 if direct else 4.0
    far(1 - place.zh)
    yield 2.0
    for zh in range(2):
        for dy in range(4):
            got(place.at(zh, dy, 1 - core))


class ReduceX:
    def __init__(self, place, src, buf, fwd, send, recv):
        self.place, self.src, self.buf, self.fwd, self.send, self.recv = place, src, buf, fwd, send, recv
        self.half, self.width = buf.shape[1], buf.shape[2]

    def view(self, p, block):
        return self.src.at[pl.ds(p * self.half, self.half), span(block * self.width, self.width)]

    def push(self, src, slot, where, sends):
        c = remote(src, self.buf.at[slot], self.send.at[slot], self.recv.at[slot], where)
        c.start()
        sends.append(c)

    def got(self, slot):
        b = self.buf.at[slot]
        remote(b, b, self.send.at[slot], self.recv.at[slot], {"mcol": self.place.xs[1]}).wait_recv()

    def flow(self, sends):
        xs = self.place.xs
        right, left = {"mcol": xs[1]}, {"mcol": xs[3]}
        self.push(self.view(0, xs[2]), 0, right, sends)
        self.push(self.view(1, xs[2]), 1, left, sends)
        self.push(self.view(0, xs[3]), 2, left, sends)
        self.push(self.view(1, xs[1]), 3, right, sends)
        yield 4.0
        for p, (at, where) in enumerate(((xs[1], right), (xs[3], left))):
            self.got(p)
            self.fwd[p] = self.buf[p] + self.view(p, at)[...]
            self.push(self.fwd.at[p], 4 + p, where, sends)
        yield 4.0
        for slot in range(2, 6):
            self.got(slot)

    def total(self, r0):
        p, r = divmod(r0, self.half)
        here = slice(r, r + HD)
        return (
            self.src[r0 : r0 + HD, span(self.place.x * self.width, self.width)].astype(F32)
            + self.buf[2 + p, here].astype(F32)
            + self.buf[4 + p, here].astype(F32)
        )


class RingX:
    def __init__(self, place, dh, slot, start, rows, send, recv):
        self.x, self.xs, self.view = place.x, place.xs, dh.at[slot, pl.ds(start, rows)]
        self.send, self.recv = send, recv
        self.right, self.left = {"mcol": place.xs[1]}, {"mcol": place.xs[3]}
        self.half, self.width = rows // 2, dh.shape[2] // 4

    def copy(self, p, block, k, where):
        view = self.view.at[pl.ds(p * self.half, self.half), span(block * self.width, self.width)]
        return remote(view, view, self.send.at[p, k], self.recv.at[p, block], where)

    def push(self, p, block, k, where, sends):
        c = self.copy(p, block, k, where)
        c.start()
        sends.append(c)

    def got(self, p, block):
        self.copy(p, block, 0, self.right).wait_recv()

    def flow(self, sends, pace):
        xs = self.xs
        for p in range(2):
            self.push(p, self.x, 0, self.right, sends)
            self.push(p, self.x, 1, self.left, sends)
        yield pace
        self.got(0, xs[3])
        self.push(0, xs[3], 2, self.right, sends)
        self.got(1, xs[1])
        self.push(1, xs[1], 2, self.left, sends)
        yield pace
        self.got(1, xs[3])
        self.got(0, xs[1])
        self.got(0, xs[2])
        self.got(1, xs[2])


class Quarter:
    def __init__(self, place, array, out, zsend, zrecv, send, recv, sends):
        self.place, self.array, self.out = place, array, out
        self.zsend, self.zrecv, self.send, self.recv, self.sends = zsend, zrecv, send, recv, sends
        self.share = out.shape[1] // 8
        self.n = 0

    def index(self, dy, core):
        return lax.rem(self.place.y + dy, 4) * 2 + core

    def view(self, index, part=None):
        rows = span(index * self.share, self.share)
        half = self.out.shape[2] // 2
        return self.out.at[1:4, rows] if part is None else self.out.at[1:4, rows, pl.ds(part * half, half)]

    def zcopy(self, r):
        dp, mine = self.place.dps[r], self.index(0, self.place.core)
        src = self.array.at[span(dp * self.out.shape[1] + mine * self.share, self.share)]
        dst = self.out.at[r, span(mine * self.share, self.share)]
        return remote(src, dst, self.zsend.at[r], self.zrecv.at[r], {"dp": dp})

    def copy(self, index, where, part, k):
        view = self.view(index, part)
        return remote(view, view, self.send.at[k], self.recv.at[index, part or 0], where)

    def push(self, index, where, part=None):
        c = self.copy(index, where, part, self.n)
        self.n += 1
        c.start()
        self.sends.append(c)

    def got(self, index, part=None):
        self.copy(index, {"mrow": self.place.sib}, part, 0).wait_recv()

    def flow(self):
        place, core = self.place, self.place.core
        right, left, sib = {"mrow": place.ys[1]}, {"mrow": place.ys[3]}, {"mrow": place.sib}
        for r in (1, 3, 2):
            self.zcopy(r).start()
        yield 9.0
        mine, before, after, far = (self.index(d, core) for d in (0, 3, 1, 2))
        for r in (1, 3, 2):
            self.zcopy(r).wait()
        for where in (right, left, sib):
            self.push(mine, where)
        yield 7.0
        self.got(before)
        self.push(before, right, 0)
        self.got(after)
        self.push(after, left, 1)
        self.push(before, sib)
        self.push(after, sib)
        yield 6.0
        self.got(far, 0)
        self.got(far, 1)
        self.push(far, sib)
        yield 6.0
        for dy in range(4):
            self.got(self.index(dy, 1 - core))


class ReduceRows:
    def __init__(self, place, array, cbox, ybuf, ysum, ztot, zbox, csem, ysem, zsem, sends):
        self.place, self.array, self.cbox, self.ybuf = place, array, cbox, ybuf
        self.ysum, self.ztot, self.zbox = ysum, ztot, zbox
        self.csem, self.ysem, self.zsem, self.sends = csem, ysem, zsem, sends
        self.width, self.rows = ztot.shape

    def target(self, z, d, c):
        return self.array.at[span(self.place.at(z, d, c) * self.width, self.width)]

    def core_copy(self, d, z):
        return remote(
            self.target(z, d, 1 - self.place.core), self.cbox.at[d, z],
            self.csem[0].at[d, z], self.csem[1].at[d, z], {"mrow": self.place.sib},
        )

    def add(self, d, srcs, lanes=slice(None)):
        for z in range(2):
            total = self.cbox[d, z, :, lanes]
            for s in srcs:
                total = total + s[z][:, lanes]
            self.cbox[d, z, :, lanes] = total

    def core_sum(self, d):
        for z in range(2):
            self.core_copy(d, z).wait_recv()
        self.add(d, [[self.target(z, d, self.place.core) for z in range(2)]])

    def ypush(self, d, slot, lanes, k, where):
        c = remote(
            self.cbox.at[d, :, :, lanes], self.ybuf.at[slot, :, :, lanes],
            self.ysem[0].at[k], self.ysem[1].at[k], where,
        )
        c.start()
        self.sends.append(c)

    def ygot(self, slot, lanes, k):
        b = self.ybuf.at[slot, :, :, lanes]
        remote(b, b, self.ysem[0].at[k], self.ysem[1].at[k], {"mrow": self.place.sib}).wait_recv()

    def flow(self):
        place = self.place
        right, left = {"mrow": place.ys[1]}, {"mrow": place.ys[3]}
        lo, hi = pl.ds(0, self.rows // 2), pl.ds(self.rows // 2, self.rows // 2)
        for d in (2, 1, 3, 0):
            for z in range(2):
                c = self.core_copy(d, z)
                c.start()
                self.sends.append(c)
        yield 2.5
        self.core_sum(2)
        self.ypush(2, 0, lo, 0, right)
        self.ypush(2, 1, hi, 1, left)
        self.core_sum(1)
        self.ypush(1, 2, hi, 3, right)
        self.core_sum(3)
        self.ypush(3, 3, lo, 4, left)
        self.core_sum(0)
        yield 3.0
        self.ygot(0, lo, 0)
        self.add(1, [[self.ybuf.at[0, z] for z in range(2)]], lo)
        self.ypush(1, 2, lo, 2, right)
        self.ygot(1, hi, 1)
        self.add(3, [[self.ybuf.at[1, z] for z in range(2)]], hi)
        self.ypush(3, 3, hi, 5, left)
        yield 4.0
        for slot, lanes, k in ((2, hi, 3), (3, lo, 4), (2, lo, 2), (3, hi, 5)):
            self.ygot(slot, lanes, k)

        for z in range(2):
            self.ysum[z] = (
                self.cbox[0, z].astype(F32) + self.ybuf[2, z].astype(F32) + self.ybuf[3, z].astype(F32)
            )
        self.ztot[...] = self.ysum[1 - place.zh].astype(BF16)

        c = remote(self.ztot, self.zbox, self.zsem[0], self.zsem[1], {"mrow": place.anti})
        c.start()
        self.sends.append(c)
        yield 8.0
        c.wait_recv()

    def result(self, lanes):
        return self.ysum[self.place.zh, :, lanes] + self.zbox[:, lanes].astype(F32)


def main_kernel(
    counts, p_hbm, k_hbm, c_hbm, g_hbm, w_hbm, wo_hbm,
    out_own, out_sum, gq_out, go_out, gain_out,
    x_loc, u_loc, x_all, u_all, normed, wt, wot,
    p_ref, k_ref, c_ref, g_ref, sp_own, sp_got, sp_fwd, out_buf, out_got, rt_fwd,
    box1, val1, box2, val2,
    q_part, m_part, bq, bm, fq, fm,
    a_part, n_part, cbox, ybuf, ysum, ztot, zbox,
    dh, quarters, w_ref, wo_ref, gbox, gval,
    s1s, s1r, s2s, s2r, g1s, g1r,
    sps, spr, rts, rtr,
    sq, sm, rq, rm,
    cs2, cr2, ys2, yr2, zs2, zr2, dxs, dxr, dzs, dzr, qzs, qzr, qys, qyr, wsem, ggs, ggr,
):
    pairs = (
        (p_hbm, p_ref), (k_hbm, k_ref), (c_hbm, c_ref), (g_hbm, g_ref), (w_hbm, w_ref), (wo_hbm, wo_ref)
    )
    loads = [pltpu.make_async_copy(src, dst, wsem.at[i]) for i, (src, dst) in enumerate(pairs)]
    for c in loads:
        c.start()
    place = Place()
    peers = place.peers()
    barrier = pltpu.get_barrier_semaphore()
    for peer in peers:
        pl.semaphore_signal(barrier, inc=1, device_id=peer, device_id_type=MESH)
    width = x_loc.shape[0]
    core, zh = place.core, place.zh
    share = Share(counts, place.dp)
    patch = lax.broadcasted_iota(jnp.int32, (p_ref.shape[2], KEEP), 0)
    for c in loads[:4]:
        c.wait()

    def lanes_of(i):
        return slice(i * KEEP, (i + 1) * KEEP)

    def kept(i):
        pick = (patch == k_ref[i : i + 1, :]).astype(F32).astype(BF16)
        return dot(p_ref[i], pick, 1, 0)

    late = [(kept(i), c_ref[:, lanes_of(i)].astype(F32)) for i in range(SLOTS, 2 * SLOTS)]
    for s in range(SPARE):
        flags = [share.holds(s, i) for i in range(SLOTS, 2 * SLOTS)]
        for a in range(2):
            total = late[0][a] * flags[0]
            for image, flag in zip(late[1:], flags[1:]):
                total = total + image[a] * flag
            sp_own[a, :, lanes_of(s)] = total.astype(BF16)
    pl.semaphore_wait(barrier, len(peers))
    chains = [
        Chain(place, sp_own.at[a], sp_got.at[a], sp_fwd.at[a], sps.at[a], spr.at[a]) for a in range(2)
    ]
    plan = Plan()
    sends = []
    stats_in, q_in, u_in, m_in, heads_in, grads_in, back_in = (Event() for _ in range(7))
    normed_in = Event()
    far_in = [Event() for _ in range(5)]
    part = w_ref.shape[2]
    gval[...] = jnp.zeros(gval.shape, F32)
    gval[:1, :width] = g_ref[...]
    gain_row = gval[:1]
    gain_col = jnp.transpose(jnp.broadcast_to(gain_row, (KEEP, KEEP)))[:width, :1]
    keeps = [share.keeps(j) for j in range(SLOTS)]
    works = [[share.works(j, s) for s in range(SPARE)] for j in range(SLOTS)]
    known = {}

    def choose(a, loc, firsts):
        spare = [chains[a].slot(s) for s in range(SPARE)]
        values = []
        for j in range(SLOTS):
            v = firsts[j] * keeps[j]
            for s in range(SPARE):
                v = v + spare[s] * works[j][s]
            loc[:, lanes_of(j)] = v.astype(BF16)
            values.append(v)
        return values

    def small_flow(small, name, event):
        for pace in (2.5, 3.0, 4.5, 3.0):
            yield pace
            known[name] = small.step()
        event.done = True

    def weights_flow():
        for c in loads[4:]:
            c.wait()
        for p in range(3):
            wt[p] = jnp.transpose(w_ref[p])
        wot[...] = jnp.transpose(wo_ref[...])
        yield 0.0

    def rows_flow():
        chains[0].start()
        firsts = [kept(j) for j in range(SLOTS)]
        yield from chains[0].flow()
        values = choose(0, x_loc, firsts)
        me_row = lax.broadcasted_iota(jnp.int32, (16, KEEP), 0) == place.me
        small = SmallSum(place, val1, box1, s1s, s1r, 2 * SLOTS)
        small.start(
            jnp.concatenate(
                [jnp.sum(v, axis=0, keepdims=True) for v in values]
                + [jnp.sum(v * v, axis=0, keepdims=True) for v in values]
                + [jnp.where(me_row, gain_row, 0.0)],
                axis=0,
            )
        )
        plan.add(small_flow(small, "stats", stats_in), 2.5)
        gather = gather_rows(place, x_loc, x_all, g1s.at[0], g1r.at[0], sends, DIRECT[0])
        pace = next(gather)
        plan.add(weights_flow())
        yield pace
        yield from gather
        yield (stats_in,)
        known["gain_cols"] = gain_cols = jnp.transpose(
            jnp.concatenate([val1[3, 2 * SLOTS :], jnp.zeros((KEEP - 16, KEEP), F32)], axis=0)
        )
        stats = known["stats"]
        known["mean"] = mean = stats[:SLOTS] * (1.0 / D)
        known["inv"] = inv = lax.rsqrt(stats[SLOTS:] * (1.0 / D) - mean * mean + EPSILON)
        for b in range(16):
            rb = slice(b * width, (b + 1) * width)
            col = gain_cols[:width, b : b + 1]
            for j in range(SLOTS):
                here = lanes_of(j)
                centred = (x_all[rb, here].astype(F32) - mean[j : j + 1]) * inv[j : j + 1]
                normed[rb, here] = (centred * col).astype(BF16)
        normed_in.done = True
        for p in range(3):
            q_part[p * part : (p + 1) * part] = dot(wt[p], normed[...], 1, 0).astype(BF16)
        yield from q_sum.flow(sends)
        q_in.done = True

    def cotangent_flow():
        chains[1].start()
        firsts = [c_ref[:, lanes_of(j)].astype(F32) for j in range(SLOTS)]
        yield from chains[1].flow()
        choose(1, u_loc, firsts)
        yield from gather_rows(place, u_loc, u_all, g1s.at[1], g1r.at[1], sends, DIRECT[1])
        u_in.done = True
        m_part[...] = dot(wo_ref[...], u_all[...], 1, 0).astype(BF16)
        yield from m_sum.flow(sends)
        m_in.done = True

    def quarter_flow(a, array):
        yield ((normed_in, u_in)[a],)
        yield from Quarter(
            place, array, quarters.at[a], qzs.at[a], qzr.at[a], qys.at[a], qyr.at[a], sends
        ).flow()
        far_in[3 + a].done = True

    q_sum = ReduceX(place, q_part, bq, fq, sq, rq)
    m_sum = ReduceX(place, m_part, bm, fm, sm, rm)

    def ring_flow(n, slot, start, rows, event, pace):
        yield from RingX(place, dh, slot, start, rows, dxs.at[n], dxr.at[n]).flow(sends, pace)
        event.done = True

    def far_flow(n, r, copy, pace):
        yield pace
        copy.wait_recv()
        yield from ring_flow(1 + r, r, 0, dh.shape[1], far_in[n], 10.0)

    def attend_flow():
        yield (q_in, m_in)
        here = span(place.x * KEEP, KEEP)
        for h in range(part // HD):
            q, k, v, do = [q_sum.total((p * (part // HD) + h) * HD) for p in range(3)] + [m_sum.total(h * HD)]
            out, dq, dk, dv = attend(q, k, v, do)
            for p, value in enumerate((dq, dk, dv, out)):
                r0 = p * part + h * HD
                dh[0, r0 : r0 + HD, here] = value.astype(BF16)
        plan.add(ring_flow(0, 0, 3 * part, part, heads_in, 3.0))
        plan.add(ring_flow(1, 0, 0, 3 * part, grads_in, 4.5))
        copies = [
            remote(dh.at[0, :, here], dh.at[r, :, here], dzs.at[r], dzr.at[r], {"dp": place.dps[r]})
            for r in range(1, 4)
        ]
        yield 0.0
        for n, r in enumerate((1, 3, 2)):
            copies[r - 1].start()
            sends.append(copies[r - 1])
            plan.add(far_flow(n, r, copies[r - 1], (13.0, 15.0, 17.0)[n]))

    feats = normed.shape[0]
    block = 2 * width
    sums = [
        ReduceRows(
            place, array, cbox.at[a], ybuf.at[a], ysum.at[a], ztot.at[a], zbox.at[a],
            (cs2.at[a], cr2.at[a]), (ys2.at[a], yr2.at[a]), (zs2.at[a], zr2.at[a]), sends,
        )
        for a, array in enumerate((a_part, n_part))
    ]
    backs = [
        Chain(place, out_buf.at[a], out_got.at[a], rt_fwd.at[a], rts.at[a], rtr.at[a]) for a in range(2)
    ]

    def give_back(a, results):
        for s in range(SPARE):
            total = results[0] * works[0][s]
            for j in range(1, SLOTS):
                total = total + results[j] * works[j][s]
            out_buf[a, :, lanes_of(s)] = total.astype(BF16)
        backs[a].start()

    def forward_flow():
        yield (heads_in,)
        for b in range(feats // block):
            rb = slice(b * block, (b + 1) * block)
            a_part[rb] = dot(wot[rb], dh[0, 3 * part :], 1, 0).astype(BF16)
        yield from sums[0].flow()
        results = []
        for j in range(SLOTS):
            result = x_loc[:, lanes_of(j)].astype(F32) + sums[0].result(lanes_of(j))
            out_own[0, :, lanes_of(j)] = result.astype(BF16)
            results.append(result)
        give_back(0, results)
        yield from backs[0].flow()
        out_sum[0] = out_buf[0] + out_got[0, 0] + out_got[0, 1]

    def backward_flow():
        yield (grads_in,)
        mean, inv, gain_cols = known["mean"], known["inv"], known["gain_cols"]
        hat = [jnp.zeros((8, KEEP), F32) for _ in range(SLOTS)]
        cross = [jnp.zeros((8, KEEP), F32) for _ in range(SLOTS)]
        for b in range(feats // block):
            rb = slice(b * block, (b + 1) * block)
            dn = dot(w_ref[0, rb], dh[0, :part], 1, 0)
            for p in (1, 2):
                dn = dn + dot(w_ref[p, rb], dh[0, p * part : (p + 1) * part], 1, 0)
            n_part[rb] = dn.astype(BF16)
            for i in range(2):
                col = gain_cols[:width, 2 * b + i : 2 * b + i + 1]
                ri = slice(i * width, (i + 1) * width)
                ra = slice((2 * b + i) * width, (2 * b + i + 1) * width)
                for j in range(SLOTS):
                    here = lanes_of(j)
                    d_hat = dn[ri, here] * col
                    centred = (x_all[ra, here].astype(F32) - mean[j : j + 1]) * inv[j : j + 1]
                    hat[j] = hat[j] + jnp.sum(d_hat.reshape(-1, 8, KEEP), axis=0)
                    cross[j] = cross[j] + jnp.sum((d_hat * centred).reshape(-1, 8, KEEP), axis=0)
        small = SmallSum(place, val2, box2, s2s, s2r, 2 * SLOTS)
        small.start(jnp.concatenate([jnp.sum(t, axis=0, keepdims=True) for t in hat + cross], axis=0))
        plan.add(small_flow(small, "back", back_in), 2.5)
        yield from sums[1].flow()
        yield (back_in,)
        back = known["back"]
        mean_hat = back[:SLOTS] * (1.0 / D)
        mean_cross = back[SLOTS:] * (1.0 / D)
        acc = jnp.zeros((width, KEEP), F32)
        results = []
        for j in range(SLOTS):
            here = lanes_of(j)
            total = sums[1].result(here)
            centred = (x_loc[:, here].astype(F32) - mean[j : j + 1]) * inv[j : j + 1]
            acc = acc + total * centred
            result = u_loc[:, here].astype(F32) + inv[j : j + 1] * (
                total * gain_col - mean_hat[j : j + 1] - centred * mean_cross[j : j + 1]
            )
            out_own[1, :, here] = result.astype(BF16)
            results.append(result)
        give_back(1, results)
        row = jnp.sum(
            jnp.transpose(jnp.concatenate([acc, jnp.zeros((KEEP - width, KEEP), F32)], axis=0)),
            axis=0, keepdims=True,
        )
        gval[...] = jnp.broadcast_to(row, gval.shape)
        gains = []
        for k in range(3):
            c = remote(gval, gbox.at[k], ggs.at[k], ggr.at[k], {"dp": place.dps[k + 1]})
            c.start()
            gains.append(c)
        yield from backs[1].flow()
        out_sum[1] = out_buf[1] + out_got[1, 0] + out_got[1, 1]
        total = gval[...]
        for k, c in enumerate(gains):
            c.wait()
            total = total + gbox[k]
        gain_out[...] = total

    def weight_gradient_flow():
        yield tuple(far_in) + (heads_in, grads_in)
        quarter = quarters.shape[2]
        for a, arr in enumerate((normed, u_all)):
            quarters[a, 0] = arr[span(place.dp * quarter, quarter)]
        for p in range(3):
            total = dot(quarters[0, 0], dh[0, p * part : (p + 1) * part], 1, 1)
            for r in range(1, 4):
                total = total + dot(quarters[0, r], dh[r, p * part : (p + 1) * part], 1, 1)
            gq_out[p] = total
        total = dot(dh[0, 3 * part :], quarters[1, 0], 1, 1)
        for r in range(1, 4):
            total = total + dot(dh[r, 3 * part :], quarters[1, r], 1, 1)
        go_out[...] = total

    plan.add(rows_flow())
    plan.add(cotangent_flow(), 3.0)
    for a, array in enumerate((normed, u_all)):
        plan.add(quarter_flow(a, array))
    plan.add(attend_flow())
    plan.add(forward_flow())
    plan.add(backward_flow())
    plan.add(weight_gradient_flow())
    plan.run()
    for c in sends:
        c.wait_send()
    for chain in chains + backs:
        chain.drain()


def post_kernel(
    n, counts, k_hbm, own_hbm, sum_hbm, gg_hbm, gq_hbm, go_hbm,
    out, dp_out, gain_out, gq_out, go_out, k_ref, own_ref, sum_ref, gg_ref, sem, osem,
):
    through = [
        pltpu.make_async_copy(src, dst, osem.at[i])
        for i, (src, dst) in enumerate(((gq_hbm, gq_out), (go_hbm, go_out)))
    ]
    for c in through:
        c.start()
    load(
        ((k_hbm, k_ref), (own_hbm, own_ref), (sum_hbm, sum_ref), (gg_hbm, gg_ref)), sem
    )
    dp = lax.axis_index("dp")
    share = Share(counts, dp)
    patch = lax.broadcasted_iota(jnp.int32, (dp_out.shape[2], KEEP), 0)
    for i in range(n):
        lanes = slice(i * KEEP, (i + 1) * KEEP)
        if i < SLOTS:
            res, d_in = (own_ref[a, :, lanes].astype(F32) * share.keeps(i) for a in range(2))
        else:
            slot = clamp(share.spare_at + i - SLOTS, SPARE - 1)
            flag = jnp.where(i - SLOTS < share.extra, 1.0, 0.0)
            here = span(slot * KEEP, KEEP)
            res, d_in = (sum_ref[a, :, here].astype(F32) * flag for a in range(2))
        pick = (patch == k_ref[i : i + 1, :]).astype(F32).astype(BF16)
        out[:, lanes] = res.astype(BF16)
        dp_out[i] = dot(d_in.astype(BF16), pick, 1, 1).astype(BF16)
    part = gain_out.shape[1]
    for g in range(4):
        @pl.when(dp == g)
        def _():
            gain_out[...] = gg_ref[:1, g * part : (g + 1) * part]
    for c in through:
        c.wait()


def sharded(patches, keep_index, counts, gain, w_qkv, w_out, cotangent):
    n, patch_count, width = patches.shape
    total_rows = n * KEEP
    rows = SLOTS * KEEP
    feats = w_qkv.shape[0]
    heads = w_out.shape[0]
    heads3 = 3 * heads
    quarter = feats // 4
    gain_row = gain[None]
    spare = SPARE * KEEP
    small = 2 * SLOTS + 16
    blk = (2, width, rows)

    def v(shape, dtype=BF16):
        return pltpu.VMEM(shape, dtype)

    scratch = [
        v((width, rows)), v((width, rows)), v((feats, rows)), v((feats, rows)), v((feats, rows)),
        v((3, heads, feats)), v((feats, heads)),
        v((n, width, patch_count)), v((n, KEEP), jnp.int32), v((width, total_rows)), v((1, width), F32),
        v((2, width, spare)), v((2, 2, width, spare)), v((2, 2, width, spare)),
        v((2, width, spare)), v((2, 2, width, spare)), v((2, 2, width, spare)),
        v((8, small, KEEP), F32), v((4, small, KEEP), F32),
        v((8, 2 * SLOTS, KEEP), F32), v((4, 2 * SLOTS, KEEP), F32),
        v((heads3, rows)), v((heads, rows)),
        v((6, heads3 // 2, KEEP)), v((6, heads // 2, KEEP)), v((2, heads3 // 2, KEEP)), v((2, heads // 2, KEEP)),
        v((feats, rows)), v((feats, rows)), v((2, 4) + blk), v((2, 4) + blk),
        v((2,) + blk, F32), v((2, width, rows)), v((2, width, rows)),
        v((4, heads3 + heads, rows)), v((2, 4, quarter, rows)), v((3, feats, heads)), v((heads, feats)),
        v((3, 8, KEEP), F32), v((8, KEEP), F32),
        DMA((8,)), DMA((8,)), DMA((8,)), DMA((8,)),
        DMA((2, 20)), DMA((2, 16, 2)),
        DMA((2, 2, CHUNKS)), DMA((2, 2, CHUNKS)), DMA((2, 2, CHUNKS)), DMA((2, 2, CHUNKS)),
        DMA((6,)), DMA((6,)), DMA((6,)), DMA((6,)),
        DMA((2, 4, 2)), DMA((2, 4, 2)), DMA((2, 6)), DMA((2, 6)), DMA((2,)), DMA((2,)),
        DMA((5, 2, 3)), DMA((5, 2, 4)), DMA((4,)), DMA((4,)), DMA((2, 4)), DMA((2, 4)),
        DMA((2, 8)), DMA((2, 8, 2)), DMA((6,)), DMA((3,)), DMA((3,)),
    ]
    shape = jax.ShapeDtypeStruct
    out_own, out_sum, gq, go, gg = pl.pallas_call(
        main_kernel,
        out_shape=[
            shape((2, width, rows), BF16), shape((2, width, spare), BF16),
            shape((3, quarter, heads), F32), shape((heads, quarter), F32),
            shape((8, KEEP), F32),
        ],
        in_specs=[SM] + [ANY] * 6,
        out_specs=[VM] * 5,
        scratch_shapes=scratch,
        compiler_params=pltpu.CompilerParams(
            vmem_limit_bytes=58 * 1024 * 1024, collective_id=1, has_side_effects=True
        ),
    )(
        counts, jnp.transpose(patches, (0, 2, 1)), keep_index, cotangent.T, gain_row,
        jnp.transpose(w_qkv, (1, 0, 2)), w_out,
    )
    part = width // 4
    outputs, d_patches, grad_gain, gq, go = pl.pallas_call(
        partial(post_kernel, n),
        out_shape=[
            shape((width, total_rows), BF16), shape((n, width, patch_count), BF16), shape((1, part), F32),
            shape(gq.shape, F32), shape(go.shape, F32),
        ],
        in_specs=[SM] + [ANY] * 6,
        out_specs=[VM] * 5,
        scratch_shapes=[
            v((n, KEEP), jnp.int32), v((2, width, rows)), v((2, width, spare)), v((8, KEEP), F32),
            DMA((4,)), DMA((2,)),
        ],
        compiler_params=pltpu.CompilerParams(vmem_limit_bytes=58 * 1024 * 1024),
    )(counts, keep_index, out_own, out_sum, gg, gq, go)
    return (
        outputs.T, jnp.transpose(d_patches, (0, 2, 1)), jnp.transpose(gq, (1, 0, 2)), go,
        grad_gain.reshape(part),
    )


def solution(mesh):
    placed = (
        P("dp", None, ("mcol", "mrow")),
        P("dp", None),
        P(),
        P(("mcol", "mrow")),
        P("mcol", None, "mrow"),
        P("mrow", "mcol"),
        P("dp", ("mcol", "mrow")),
    )
    return jax.shard_map(
        sharded,
        mesh=mesh,
        in_specs=placed,
        out_specs=(
            P("dp", ("mcol", "mrow")),
            P("dp", None, ("mcol", "mrow")),
            P(("mcol", "dp"), None, "mrow"),
            P("mrow", ("mcol", "dp")),
            P(("mcol", "mrow", "dp")),
        ),
        check_vma=False,
    )
```
